512 devices in a mesh: sect: 8 (over z_hi, core), blk: 64 (over x, y, z_lo).
Axes of the slice: x: 4, y: 4, z: 16 (z_hi: 4, z_lo: 4; z = z_hi * 4 + z_lo), core: 2. Of those that a mesh axis runs over, the one named last changes fastest.
Arguments:
- gas_field: float32 [5, 128, 32, 8192], P(None, 'sect', None, 'blk'), may hold values from -6 to 6
- diffusion: float32 [128, 32, 8192], P('sect', None, 'blk'), may hold values from 0.02 to 0.16
- reaction: float32 [5, 5], replicated, may hold values from -2.5 to 2.5
- particles: float32 [16, 1048576], P(None, ('sect', 'blk')), may hold values from -6 to 6
- mixing: float32 [16, 16], replicated, may hold values from -1.5 to 1.5
- heating: float32 [16], replicated, may hold values from -3 to 3
- wall_cell: int32 [1048576], P(('sect', 'blk')), may hold values from 0 to 2047
- tile_hop: int32 [1048576, 1], P(('sect', 'blk')), may hold values from 0 to 4; in each aligned block of 2048 rows (0 to 2047, 2048 to 4095, ...) at most 1024 rows name the same one
Outputs:
- gas_next: float32 [5, 128, 32, 8192], P(None, 'sect', None, 'blk')
- arrived: float32 [16, 2621440], P(None, ('sect', 'blk'))
The draws below stay inside these ranges and needn't reach their ends.
Inputs may be any that keep to these rules, and one draw needn't show every extreme that they name: `tile_hop`: among the 2048 particles of one device, at most 1024 have the same move, and in some devices exactly 1024 do.
All inputs are finite; a program needn't handle non-finite values.
Results may differ from the reference program's by a relative error of at most 0.0001.
Values sent between devices are 32-bit elements; how exact they have to be, the bound alone decides.
No kernel may reach another device: no remote copies, remote signals or barrier semaphores. Data moves between devices by JAX's collectives and lax.ppermute only.
A program may use at most 64 MiB of HBM per device.

```python
import math
import jax
import jax.numpy as jnp
import numpy as np
from jax import lax

COMP = 5
VALS = 16
GX = 16
GR = 32
GA = 128
PD = 2048
REACH = 2
ITERS = 3
CAP = 1024
WALL = 2048
NX = 128
NA = 8192
NPART = 1048576
N_SECT = 8
N_BLK = 64


def place_ends(array, rng, least, high):
    longest = array.shape.index(max(array.shape))
    spots = []
    for shift in (0, 1):
        where = [jax.random.randint(jax.random.fold_in(rng, axis), (), 0, length) for axis, length in enumerate(array.shape)]
        where[longest] = (where[longest] + shift) % array.shape[longest]
        spots.append(tuple(where))
    return array.at[spots[0]].set(least).at[spots[1]].set(high)


def levels(key, extent, split, low, high):
    gain, own = 1.0, jax.random.fold_in(key, 6)
    for position, parts in split:
        heights = jnp.exp(jax.random.uniform(jax.random.fold_in(own, position), (parts,), jnp.float32, low / len(split), high / len(split)))
        gain = gain * jnp.repeat(heights, extent[position] // parts).reshape([-1 if axis == position else 1 for axis in range(len(extent))])
    return gain


def assign_block(key, own, number, rows, count, top, bound, slope):
    ranking = jax.random.permutation(key, count)
    heavy_load, usual = portions_of(count, rows * top, bound, slope, True), portions_of(count, rows * top, bound, slope, False)
    places = jnp.arange(count)

    def named(sizes, offset_by):
        used = int((sizes > 0).sum())
        fixed = max(1, used // 4)
        shifted = fixed + (places - fixed + offset_by * (used - fixed)) % max(1, count - fixed)
        return jnp.zeros((count,), jnp.int32).at[ranking[jnp.where(places < fixed, places, shifted)]].set(jnp.asarray(sizes, jnp.int32))

    sizes = jnp.where(number % 4 == 0, named(heavy_load, number // 4), named(usual, number - number // 4 - 1))
    mixed = jax.random.permutation(jax.random.fold_in(own, 3), count)
    donor, taker = mixed[0:count // 2 * 2:2], mixed[1:count // 2 * 2:2]
    room = jnp.minimum(sizes[donor] - 1, bound - sizes[taker]) // 2
    room = jnp.where((donor == ranking[0]) | (taker == ranking[0]) | (sizes[taker] == 0), 0, jnp.maximum(room, 0))
    shifted = jax.random.randint(jax.random.fold_in(own, 4), (count // 2,), 0, 1 << 20) % (room + 1)
    sizes = sizes.at[donor].add(-shifted).at[taker].add(shifted)
    items = jnp.searchsorted(jnp.cumsum(sizes), jnp.arange(rows * top), side="right").astype(jnp.int32)
    table = items.reshape(top, rows).T
    table = table[jax.random.permutation(jax.random.fold_in(own, 1), rows)]
    offset_by = jax.random.randint(jax.random.fold_in(own, 2), (rows, 1), 0, top)
    return jnp.take_along_axis(table, (jnp.arange(top)[None, :] + offset_by) % top, axis=1)


def portions_of(count, total, most, lean, full):
    weights = [(1 << 20) // math.isqrt(rank ** lean) + 1 for rank in range(1, count + 1)]
    largest = most if full else min(most, max(-(-total // count), total * weights[0] // sum(weights)))
    least = 1 if total - largest >= count - 1 else 0
    counts, rest = [largest] + [least] * (count - 1), total - largest - least * (count - 1)
    while rest > 0:
        free = [i for i in range(1, count) if counts[i] < largest] or [i for i in range(1, count) if counts[i] < most]
        pool, budget = sum([weights[i] for i in free]), rest
        for i in free:
            more = min(most - counts[i], max(1, budget * weights[i] // pool), rest)
            counts[i] = counts[i] + more
            rest = rest - more
    return np.array(counts)


def noise(rng, dims, deviation, bound, split=(), held_as=jnp.bfloat16):
    loudness = levels(rng, dims, split, -0.22, 0.18) if split else 1.0
    drawn = jax.random.normal(rng, dims, jnp.float32) * deviation * loudness
    return jnp.minimum(jnp.maximum(drawn, -bound), bound).astype(held_as)


def setup_inputs(seed: int = 0) -> dict:
    arg_keys = jax.random.split(jax.random.key(seed), 9)
    gas_field = noise(arg_keys[0], (COMP, NX, GR, NA), 1.0, 6.0, ((1, 8), (3, 64)), jnp.float32)
    diffusion = jnp.clip(jnp.exp(math.log(0.16) - 2.0794415 * jax.random.uniform(arg_keys[1], (NX, GR, NA), jnp.float32) ** levels(arg_keys[1], (NX, GR, NA), ((0, 8), (2, 64)), -0.2, 0.2)), 0.02, 0.16)
    reaction = noise(arg_keys[2], (COMP, COMP), COMP ** -0.5, 2.5, (), jnp.float32)
    particles = noise(arg_keys[3], (VALS, NPART), 1.0, 6.0, ((1, 512),), jnp.float32)
    mixing = noise(arg_keys[4], (VALS, VALS), VALS ** -0.5, 1.5, (), jnp.float32)
    heating = noise(arg_keys[5], (VALS,), 0.5, 3.0, (), jnp.float32)
    wall_cell = place_ends(jax.random.randint(arg_keys[6], (NPART,), 0, WALL), jax.random.fold_in(arg_keys[6], 1), 0, WALL - 1).astype(jnp.int32)
    tile_hop_keys = jax.random.split(jax.random.fold_in(arg_keys[7], 1), NPART // PD)
    tile_hop_turns = jax.random.permutation(jax.random.fold_in(arg_keys[7], 3), NPART // PD)
    tile_hop = jax.vmap(lambda own, number: assign_block(jax.random.fold_in(arg_keys[7], 2), own, number, PD, 2 * REACH + 1, 1, CAP, 2))(tile_hop_keys, tile_hop_turns).reshape((NPART, 1))
    return dict(gas_field=gas_field, diffusion=diffusion, reaction=reaction, particles=particles, mixing=mixing, heating=heating, wall_cell=wall_cell, tile_hop=tile_hop)


DIFFUSE = (1.0, 0.8, 0.6, 0.9, 0.7)


def advance(field, kappa, reaction, axial_pad, loop_pad):
    radial_pad = jnp.concatenate([field[:, :, :1], field, field[:, :, -1:]], axis=2)
    laplace = axial_pad[:, 2:] + axial_pad[:, :-2]
    laplace = laplace + radial_pad[:, :, 2:] + radial_pad[:, :, :-2]
    laplace = laplace + loop_pad[..., 2:] + loop_pad[..., :-2] - 6.0 * field
    rates = jnp.asarray(DIFFUSE, jnp.float32)[:, None, None, None]
    coupled = jnp.tensordot(reaction, field, axes=(1, 0), precision=lax.Precision.HIGHEST)
    return field + rates * kappa[None] * laplace + 0.3 * coupled


def reference(gas_field, diffusion, reaction, particles, mixing, heating, wall_cell, tile_hop):
    field = gas_field
    for sweep in range(ITERS):
        axial_pad = jnp.pad(field, ((0, 0), (1, 1), (0, 0), (0, 0)))
        loop_pad = jnp.concatenate([field[..., -1:], field, field[..., :1]], axis=3)
        field = advance(field, diffusion, reaction, axial_pad, loop_pad)
    wall_rows = field[0, :, GR - 1, :]
    earlier = jnp.concatenate([jnp.zeros((GX, NA), jnp.float32), wall_rows[:-GX]], axis=0)
    flux = 0.5 * (wall_rows + earlier)
    flux_tiles = flux.reshape(N_SECT, GX, N_BLK, GA).transpose(0, 2, 1, 3).reshape(N_SECT * N_BLK, GX * GA)
    cells = wall_cell.reshape(N_SECT * N_BLK, PD).astype(jnp.int32)
    look = jnp.take_along_axis(flux_tiles, cells, axis=1).reshape(NPART)
    heated = particles + 0.5 * jnp.dot(mixing, particles, precision=lax.Precision.HIGHEST)
    heated = heated + heating[:, None] * (look - particles[0])[None, :]
    values = heated.reshape(VALS, N_SECT, N_BLK, PD)
    moves = tile_hop[:, 0].reshape(N_SECT, N_BLK, PD)
    sect_ids = lax.broadcasted_iota(jnp.int32, moves.shape, 0)
    tile_ids = lax.broadcasted_iota(jnp.int32, moves.shape, 1)
    blocks = []
    for offset_index in range(2 * REACH + 1):
        chosen = moves == offset_index
        ranks = (jnp.cumsum(chosen.astype(jnp.int32), axis=2) - 1).astype(jnp.int32)
        slots = jnp.where(chosen, ranks, CAP).astype(jnp.int32)
        buffer = jnp.zeros((VALS, N_SECT, N_BLK, CAP + 1), jnp.float32)
        buffer = buffer.at[:, sect_ids, tile_ids, slots].set(values)
        buffer = jnp.roll(buffer[..., :CAP], offset_index - REACH, axis=2)
        blocks.append(buffer)
    arrived = jnp.stack(blocks, axis=3).reshape(VALS, N_SECT * N_BLK * (2 * REACH + 1) * CAP)
    return field, arrived
```

```python
import jax
import jax.numpy as jnp
from jax import lax
from jax.experimental import pallas as pl
from jax.experimental.pallas import tpu as pltpu
from jax.sharding import PartitionSpec as P

REACH = 2
MOVES = 2 * REACH + 1
ITERS = 3
DIFFUSE = (1.0, 0.8, 0.6, 0.9, 0.7)
COMP = 5
GX = 16
GR = 32
GA = 128
TILES = GR // 8
EXT = GX + 2 * ITERS
CHUNKS = 16
VALS = 16
CAP = 1024
SPOTS = CAP // 128

FIELD_COLUMNS = (3, 2, 1, 0, -1)
KAPPA_COLUMNS = (2, 1, 0)
STRIPS = [(c, k) for c in range(COMP) for k in FIELD_COLUMNS] + [(COMP, k) for k in KAPPA_COLUMNS]
STRIP_AT = {key: i for i, key in enumerate(STRIPS)}
CORNERS = [(c, 1) for c in range(COMP)] + [(c, 2) for c in range(COMP)] + [(COMP, 1)] + [(c, 0) for c in range(COMP)]
LAYERS = 3 * COMP + 2 + 1

VMEM = pl.BlockSpec(memory_space=pltpu.VMEM)
SMEM = pl.BlockSpec(memory_space=pltpu.SMEM)


def f32(*shape):
    return jax.ShapeDtypeStruct(shape, jnp.float32)


def i32(*shape):
    return jax.ShapeDtypeStruct(shape, jnp.int32)


def lanes(shape=(8, 128)):
    return lax.broadcasted_iota(jnp.int32, shape, len(shape) - 1)


def pick(x, index):
    return jnp.take_along_axis(x, index, axis=1, mode="promise_in_bounds")


def rows(tile):
    return slice(8 * tile, 8 * tile + 8)


def call(kernel, outs, scratch=(), specs=None, flops=0, moved=0, limit=16):
    return pl.pallas_call(
        kernel,
        out_shape=outs,
        in_specs=specs,
        out_specs=jax.tree.map(lambda _: VMEM, outs),
        scratch_shapes=list(scratch),
        cost_estimate=pl.CostEstimate(flops=flops, bytes_accessed=moved, transcendentals=0),
        compiler_params=pltpu.CompilerParams(vmem_limit_bytes=limit << 20),
    )


def edges_kernel(gas, kappa, to_right, to_left):
    lane = lanes()
    within = lane & 63
    depth, cell = within >> 4, within & 15
    high = jnp.maximum(6 * cell + 2 - depth, 0)
    low = 6 * cell + 3 + depth
    for tile in range(TILES):
        packed = [jnp.zeros((8, 128), jnp.float32) for _ in range(COMP + 1)]
        for x in range(GX):
            here = (lane >= 6 * x) & (lane < 6 * x + 6)
            for q in range(COMP + 1):
                slab = gas[q, x, rows(tile), :] if q < COMP else kappa[x, rows(tile), :]
                packed[q] = jnp.where(here, pltpu.roll(slab, 6 * x + 3, 1), packed[q])
        for s in range((COMP + 1) // 2):
            for out, index in ((to_right, high), (to_left, low)):
                out[s, rows(tile), :] = jnp.where(lane < 64, pick(packed[2 * s], index), pick(packed[2 * s + 1], index))


def strips_kernel(gas, kappa, to_right, to_left, from_left, from_right, strips, send_a, send_wall, send_rest):
    lane = lanes()
    low_side = (lane & 1) == 1
    cell = jnp.clip((lane >> 1) - 3, 0, GX - 1)
    odd = lax.rem(lax.axis_index("sect"), 2)
    even = odd == 0
    for tile in range(TILES):
        held = {}
        for q, k in STRIPS:
            depth = k - 1 if k > 0 else -k
            index = cell + ((q % 2) * 64 + depth * 16)
            low, high = (from_left, from_right) if k > 0 else (to_left, to_right)
            value = jnp.where(low_side, pick(low[q // 2, rows(tile), :], index), pick(high[q // 2, rows(tile), :], index))
            strips[STRIP_AT[q, k], rows(tile), :] = value
            held[q, k] = value
        top = jnp.zeros((8, 128), jnp.float32)
        bottom = top
        for i, key in enumerate(CORNERS):
            here = (lane >> 2) == i
            top = jnp.where(here, pltpu.roll(held[key], (4 * i - 34) % 128, 1), top)
            bottom = jnp.where(here, pltpu.roll(held[key], (4 * i - 6) % 128, 1), bottom)
        for_a = jnp.where(even, top, bottom)
        for_b = jnp.where(even, bottom, top)
        send_a[LAYERS - 1, rows(tile), :] = for_a
        if tile == TILES - 1:
            send_wall[LAYERS - 1] = for_b
        else:
            send_rest[LAYERS - 1, rows(tile), :] = for_b
    at_a, at_b = jnp.where(even, GX - 3, 0), jnp.where(even, 0, GX - 3)
    kappa_a, kappa_b = jnp.where(even, GX - 2, 0), jnp.where(even, 0, GX - 2)
    split = GR - 8
    for c in range(COMP):
        for layer in range(3):
            send_a[3 * c + layer] = gas[c, at_a + layer]
            send_wall[3 * c + layer] = gas[c, at_b + layer, split:, :]
            send_rest[3 * c + layer] = gas[c, at_b + layer, :split, :]
    for layer in range(2):
        send_a[3 * COMP + layer] = kappa[kappa_a + layer]
        send_wall[3 * COMP + layer] = kappa[kappa_b + layer, split:, :]
        send_rest[3 * COMP + layer] = kappa[kappa_b + layer, :split, :]


def coupling(reaction):
    return [[0.3 * reaction[c, d] + (1.0 if c == d else 0.0) for d in range(COMP)] for c in range(COMP)]


def updated(c, values, neighbours, kappa, mix):
    total = mix[c][0] * values[0]
    for d in range(1, COMP):
        total = total + mix[c][d] * values[d]
    rate = kappa if DIFFUSE[c] == 1.0 else DIFFUSE[c] * kappa
    return total + rate * (neighbours - 6.0 * values[c])


def radial_sum(tiles, wall_only):
    sub = lax.broadcasted_iota(jnp.int32, (8, 128), 0)
    down = [pltpu.roll(t, 1, 0) for t in tiles]
    up = [pltpu.roll(t, 7, 0) for t in tiles]
    last = len(tiles) - 1
    sums = []
    for i, t in enumerate(tiles):
        if wall_only:
            below = down[i]
        else:
            below = jnp.where(sub == 0, down[i - 1] if i > 0 else t, down[i])
        above = jnp.where(sub == 7, up[i + 1] if i < last else t, up[i])
        sums.append(below + above)
    return sums


def strip_levels(strips, low_corner, high_corner, mix, edge, tiles):
    lane = lanes()
    wall_only = len(tiles) == 1
    from_low = (lane >= 2) & (lane < 6)
    from_high = (lane >= 38) & (lane < 42)
    held = {}
    for key in STRIPS:
        held[key] = [strips[STRIP_AT[key], rows(t), :] for t in tiles]
    for i, key in enumerate(CORNERS):
        for n in range(len(tiles)):
            value = jnp.where(from_low, pltpu.roll(low_corner[n], (2 - 4 * i) % 128, 1), held[key][n])
            held[key][n] = jnp.where(from_high, pltpu.roll(high_corner[n], (38 - 4 * i) % 128, 1), value)
    for step in range(ITERS):
        for c in range(COMP):
            for n in range(len(tiles)):
                edge[step, c, rows(n), :] = held[c, 1][n]
        if step == ITERS - 1:
            break
        later = {}
        for k in (2, 1, 0) if step == 0 else (1,):
            for c in range(COMP):
                radial = radial_sum(held[c, k], wall_only)
                later[c, k] = []
                for n in range(len(tiles)):
                    value = held[c, k][n]
                    around = held[c, k + 1][n] + held[c, k - 1][n]
                    around = around + pltpu.roll(value, 2, 1) + pltpu.roll(value, 126, 1) + radial[n]
                    later[c, k].append(updated(c, [held[d, k][n] for d in range(COMP)], around, held[COMP, k][n], mix))
        for key in [key for key in held if key[0] == COMP]:
            later[key] = held[key]
        held = later


def plane(src, kappa, edge, step, at, mix, count, wall_only, comps):
    lane = lanes()
    first, last = lane == 0, lane == 127
    shift = 127 - 2 * at
    values = [[src[c, at, rows(t), :] for t in range(count)] for c in range(COMP)]
    kap = [kappa[at, rows(t), :] for t in range(count)]
    out = {}
    for c in comps:
        radial = radial_sum(values[c], wall_only)
        for t in range(count):
            value = values[c][t]
            beyond = pltpu.roll(edge[step, c, rows(t), :], shift, 1)
            around = src[c, at - 1, rows(t), :] + src[c, at + 1, rows(t), :] + radial[t]
            around = around + jnp.where(first, beyond, pltpu.roll(value, 1, 1))
            around = around + jnp.where(last, beyond, pltpu.roll(value, 127, 1))
            out[c, t] = updated(c, [values[d][t] for d in range(COMP)], around, kap[t], mix)
    return out


def steps(count, wall_only, now, later, kappa, edge, mix, finish):
    for step in range(ITERS):
        src, dst = (now, later) if step % 2 == 0 else (later, now)
        final = step == ITERS - 1

        def body(at, carry, step=step, src=src, dst=dst, final=final):
            comps = (0,) if final and wall_only else range(COMP)
            out = plane(src, kappa, edge, step, at, mix, count, wall_only, comps)
            if final:
                finish(at, out)
            else:
                for (c, t), value in out.items():
                    dst[c, at, rows(t), :] = value
            return carry

        lax.fori_loop(step + 1, EXT - 1 - step, body, 0)


def wall_kernel(gas, kappa, strips, recv_a, recv_wall, reaction, wall, now, later, kap, edge):
    odd = lax.rem(lax.axis_index("sect"), 2)
    even = odd == 0
    mix = coupling(reaction)
    top = slice(GR - 8, GR)
    at_a, at_b = jnp.where(even, GX + 3, 0), jnp.where(even, 0, GX + 3)
    kappa_a, kappa_b = jnp.where(even, GX + 3, 1), jnp.where(even, 1, GX + 3)
    for c in range(COMP):
        for x in range(GX):
            now[c, x + 3] = gas[c, x, top, :]
        for layer in range(3):
            now[c, at_a + layer] = recv_a[3 * c + layer, top, :]
            now[c, at_b + layer] = recv_wall[3 * c + layer]
    for x in range(GX):
        kap[x + 3] = kappa[x, top, :]
    for layer in range(2):
        kap[kappa_a + layer] = recv_a[3 * COMP + layer, top, :]
        kap[kappa_b + layer] = recv_wall[3 * COMP + layer]
    corner_a, corner_b = recv_a[LAYERS - 1, top, :], recv_wall[LAYERS - 1]
    low, high = jnp.where(even, corner_b, corner_a), jnp.where(even, corner_a, corner_b)
    strip_levels(strips, [low], [high], mix, edge, [TILES - 1])

    def finish(at, out):
        wall[pl.ds(at - 3, 1), :] = out[0, 0][7:8, :]

    steps(1, True, now, later, kap, edge, mix, finish)


def gas_kernel(gas, kappa, strips, recv_a, recv_wall, recv_rest, reaction, result, now, later, kap, edge):
    odd = lax.rem(lax.axis_index("sect"), 2)
    even = odd == 0
    mix = coupling(reaction)
    split = GR - 8
    at_a, at_b = jnp.where(even, GX + 3, 0), jnp.where(even, 0, GX + 3)
    kappa_a, kappa_b = jnp.where(even, GX + 3, 1), jnp.where(even, 1, GX + 3)
    for c in range(COMP):
        now[c, 3 : GX + 3] = gas[c]
        for layer in range(3):
            now[c, at_a + layer] = recv_a[3 * c + layer]
            now[c, at_b + layer, split:, :] = recv_wall[3 * c + layer]
            now[c, at_b + layer, :split, :] = recv_rest[3 * c + layer]
    kap[3 : GX + 3] = kappa[...]
    for layer in range(2):
        kap[kappa_a + layer] = recv_a[3 * COMP + layer]
        kap[kappa_b + layer, split:, :] = recv_wall[3 * COMP + layer]
        kap[kappa_b + layer, :split, :] = recv_rest[3 * COMP + layer]
    low, high = [], []
    for t in range(TILES):
        corner_a = recv_a[LAYERS - 1, rows(t), :]
        corner_b = recv_wall[LAYERS - 1] if t == TILES - 1 else recv_rest[LAYERS - 1, rows(t), :]
        low.append(jnp.where(even, corner_b, corner_a))
        high.append(jnp.where(even, corner_a, corner_b))
    strip_levels(strips, low, high, mix, edge, list(range(TILES)))

    def finish(at, out):
        for (c, t), value in out.items():
            result[c, at - 3, rows(t), :] = value

    steps(TILES, False, now, later, kap, edge, mix, finish)


def pack_kernel(hop, cell, particles, mixing, heating, packed, cells, spread, ordered, source, begin, end):
    lane = lanes()
    square = (128, 128)
    down, across = lax.broadcasted_iota(jnp.int32, square, 0), lanes(square)
    moves = hop[...]
    named = [moves == j for j in range(MOVES)]
    table = jnp.concatenate(
        [jnp.where(m, 1.0, 0.0) for m in named] + [jnp.zeros((128 - MOVES * CHUNKS, 128), jnp.float32)], axis=0
    )
    running = jnp.dot(table, jnp.where(down <= across, 1.0, 0.0), preferred_element_type=jnp.float32)
    count = jnp.dot(table, jnp.ones(square, jnp.float32), preferred_element_type=jnp.float32)
    before = jnp.where(((down >> 4) == (across >> 4)) & (across < down), 1.0, 0.0)
    base = jnp.dot(before, count, preferred_element_type=jnp.float32)
    offset = jnp.zeros((CHUNKS, 128), jnp.float32)
    place = jnp.zeros((CHUNKS, 128), jnp.float32)
    across16 = lanes((CHUNKS, 128))
    for j in range(MOVES):
        part = slice(CHUNKS * j, CHUNKS * (j + 1))
        place = jnp.where(named[j], offset + running[part] - 1.0, place)
        first = base[part].astype(jnp.int32)
        source[part, :] = (across16 + offset.astype(jnp.int32) - first) & 127
        begin[part, :] = across16 - first
        end[part, :] = across16 - first - count[part].astype(jnp.int32)
        offset = offset + count[part]
    own = lax.broadcasted_iota(jnp.int32, (VALS, VALS), 0) == lax.broadcasted_iota(jnp.int32, (VALS, VALS), 1)
    weights = 0.5 * mixing[...] + jnp.where(own, 1.0, 0.0)
    first_value = lax.broadcasted_iota(jnp.int32, (VALS, VALS), 1) == 0
    weights = weights - jnp.where(first_value, heating[...], 0.0)
    for v in range(VALS):
        spread[v] = jnp.broadcast_to(weights[:, v : v + 1], (VALS, 128))
    place = place.astype(jnp.int32)
    position = lane.astype(jnp.float32)
    for chunk in range(CHUNKS):
        part = slice(128 * chunk, 128 * (chunk + 1))
        total = spread[0] * particles[0:1, part]
        for v in range(1, VALS):
            total = total + spread[v] * particles[v : v + 1, part]
        hot = jnp.where(down == place[chunk : chunk + 1, :], 1.0, 0.0)
        order = lax.dot_general(position, hot, (((1,), (1,)), ((), ())), preferred_element_type=jnp.float32)
        order = order.astype(jnp.int32)
        ordered[chunk, 0:8, :] = pick(total[0:8], order)
        ordered[chunk, 8:16, :] = pick(total[8:16], order)
        ordered[chunk, 16:24, :] = pick(
            jnp.broadcast_to(cell[chunk : chunk + 1, :], (8, 128)).astype(jnp.float32), order
        )

    def block(j, carry):
        held = [[jnp.zeros((8, 128), jnp.float32)] * 2 + [jnp.full((8, 128), -1.0)] for _ in range(SPOTS)]
        for chunk in range(CHUNKS):
            row = pl.ds(CHUNKS * j + chunk, 1)
            index = jnp.broadcast_to(source[row, :], (8, 128))
            parts = [pick(ordered[chunk, rows(n), :], index) for n in range(3)]
            start = jnp.broadcast_to(begin[row, :], (8, 128))
            stop = jnp.broadcast_to(end[row, :], (8, 128))
            for spot in range(SPOTS):
                here = (start >= -128 * spot) & (stop < -128 * spot)
                held[spot] = [jnp.where(here, new, old) for new, old in zip(parts, held[spot])]
        for spot in range(SPOTS):
            part = slice(128 * spot, 128 * (spot + 1))
            packed[j, 0:8, part] = held[spot][0]
            packed[j, 8:16, part] = held[spot][1]
            cells[j, spot : spot + 1, :] = held[spot][2][0:1, :].astype(jnp.int32)
        return carry

    lax.fori_loop(0, MOVES, block, 0)


def heat_kernel(wall, earlier, packed, cells, heating, *refs):
    outs, look = refs[:MOVES], refs[MOVES]
    flux = 0.5 * (wall[...] + earlier[...])
    heat = jnp.broadcast_to(heating[...], (VALS, 128))
    for j in range(MOVES):
        where_to = cells[j]
        row, column = where_to >> 7, where_to & 127
        found = jnp.zeros((8, 128), jnp.float32)
        for x in range(GX):
            line = jnp.broadcast_to(flux[x : x + 1, :], (8, 128))
            found = jnp.where(row == x, pick(line, column), found)
        look[j] = found
    for j in range(MOVES):
        for spot in range(SPOTS):
            part = slice(128 * spot, 128 * (spot + 1))
            outs[j][:, part] = packed[j, :, part] + heat * look[j, spot : spot + 1, :]


def ring(x, axis, by):
    size = lax.axis_size(axis)
    return lax.ppermute(x, axis, [(i, (i + by) % size) for i in range(size)])


def swap(x, axis, first):
    size = lax.axis_size(axis)
    pairs = [(i, i + 1) for i in range(first, size - 1, 2)]
    return lax.ppermute(x, axis, pairs + [(j, i) for i, j in pairs])


def local(gas, kappa, reaction, particles, mixing, heating, wall_cell, tile_hop):
    strip_shape = (3, GR, GA)
    to_right, to_left = call(edges_kernel, (f32(*strip_shape), f32(*strip_shape)), specs=[VMEM] * 2, moved=2 << 20)(gas, kappa)
    from_left = ring(to_right, "blk", 1)
    from_right = ring(to_left, "blk", -1)

    heating_column = heating.reshape(VALS, 1)
    packed, cells = call(
        pack_kernel,
        (f32(MOVES, VALS, CAP), i32(MOVES, SPOTS, 128)),
        scratch=[
            pltpu.VMEM((VALS, VALS, 128), jnp.float32),
            pltpu.VMEM((CHUNKS, 24, 128), jnp.float32),
            pltpu.VMEM((MOVES * CHUNKS, 128), jnp.int32),
            pltpu.VMEM((MOVES * CHUNKS, 128), jnp.int32),
            pltpu.VMEM((MOVES * CHUNKS, 128), jnp.int32),
        ],
        specs=[VMEM] * 5,
        moved=8 << 20,
    )(tile_hop.reshape(CHUNKS, 128), wall_cell.reshape(CHUNKS, 128), particles, mixing, heating_column)

    strips, send_a, send_wall, send_rest = call(
        strips_kernel,
        (f32(len(STRIPS), GR, GA), f32(LAYERS, GR, GA), f32(LAYERS, 8, GA), f32(LAYERS, GR - 8, GA)),
        specs=[VMEM] * 6,
        moved=2 << 20,
    )(gas, kappa, to_right, to_left, from_left, from_right)
    recv_wall = swap(send_wall, "sect", 1)
    recv_a = swap(send_a, "sect", 0)
    recv_rest = swap(send_rest, "sect", 1)

    wall = call(
        wall_kernel,
        f32(GX, GA),
        scratch=[
            pltpu.VMEM((COMP, EXT, 8, GA), jnp.float32),
            pltpu.VMEM((COMP, EXT, 8, GA), jnp.float32),
            pltpu.VMEM((EXT, 8, GA), jnp.float32),
            pltpu.VMEM((ITERS, COMP, 8, GA), jnp.float32),
        ],
        specs=[VMEM] * 5 + [SMEM],
        moved=4 << 20,
    )(gas, kappa, strips, recv_a, recv_wall, reaction)
    size = lax.axis_size("sect")
    earlier = lax.ppermute(wall, "sect", [(i, i + 1) for i in range(size - 1)])

    blocks = call(
        heat_kernel,
        (f32(VALS, CAP),) * MOVES,
        scratch=[pltpu.VMEM((MOVES, SPOTS, 128), jnp.float32)],
        specs=[VMEM] * 5,
        moved=2 << 20,
    )(wall, earlier, packed, cells, heating_column)
    pieces = [block if j == REACH else ring(block, "blk", j - REACH) for j, block in enumerate(blocks)]

    field = call(
        gas_kernel,
        f32(COMP, GX, GR, GA),
        scratch=[
            pltpu.VMEM((COMP, EXT, GR, GA), jnp.float32),
            pltpu.VMEM((COMP, EXT, GR, GA), jnp.float32),
            pltpu.VMEM((EXT, GR, GA), jnp.float32),
            pltpu.VMEM((ITERS, COMP, GR, GA), jnp.float32),
        ],
        specs=[VMEM] * 6 + [SMEM],
        moved=20 << 20,
    )(gas, kappa, strips, recv_a, recv_wall, recv_rest, reaction)
    return field, jnp.concatenate(pieces, axis=1)


def solution(mesh):
    in_specs = (
        P(None, "sect", None, "blk"),
        P("sect", None, "blk"),
        P(),
        P(None, ("sect", "blk")),
        P(),
        P(),
        P(("sect", "blk")),
        P(("sect", "blk"), None),
    )
    out_specs = (P(None, "sect", None, "blk"), P(None, ("sect", "blk")))
    return jax.shard_map(local, mesh=mesh, in_specs=in_specs, out_specs=out_specs, check_vma=False)
```

```python
import jax
import jax.numpy as jnp
from jax import lax
from jax.experimental import pallas as pl
from jax.experimental.pallas import tpu as pltpu
from jax.sharding import PartitionSpec as P

REACH = 2
MOVES = 2 * REACH + 1
ITERS = 3
DIFFUSE = (1.0, 0.8, 0.6, 0.9, 0.7)
COMP = 5
GX = 16
GR = 32
GA = 128
TILES = GR // 8
EXT = GX + 2 * ITERS
CHUNKS = 16
VALS = 16
CAP = 1024
SPOTS = CAP // 128

FIELD_COLUMNS = (3, 2, 1, 0, -1)
KAPPA_COLUMNS = (2, 1, 0)
STRIPS = [(c, k) for c in range(COMP) for k in FIELD_COLUMNS] + [(COMP, k) for k in KAPPA_COLUMNS]
STRIP_AT = {key: i for i, key in enumerate(STRIPS)}
CORNERS = [(c, 1) for c in range(COMP)] + [(c, 2) for c in range(COMP)] + [(COMP, 1)] + [(c, 0) for c in range(COMP)]
LAYERS = 3 * COMP + 2 + 1

VMEM = pl.BlockSpec(memory_space=pltpu.VMEM)
SMEM = pl.BlockSpec(memory_space=pltpu.SMEM)
ANY = pl.BlockSpec(memory_space=pl.ANY)
HBM = pl.BlockSpec(memory_space=pltpu.HBM)


def f32(*shape):
    return jax.ShapeDtypeStruct(shape, jnp.float32)


def i32(*shape):
    return jax.ShapeDtypeStruct(shape, jnp.int32)


def lanes(shape=(8, 128)):
    return lax.broadcasted_iota(jnp.int32, shape, len(shape) - 1)


def pick(x, index):
    return jnp.take_along_axis(x, index, axis=1, mode="promise_in_bounds")


def rows(tile):
    return slice(8 * tile, 8 * tile + 8)


def call(kernel, outs, scratch=(), specs=None, out_specs=None, flops=0, moved=0, limit=16):
    return pl.pallas_call(
        kernel,
        out_shape=outs,
        in_specs=specs,
        out_specs=jax.tree.map(lambda _: VMEM, outs) if out_specs is None else out_specs,
        scratch_shapes=list(scratch),
        cost_estimate=pl.CostEstimate(flops=flops, bytes_accessed=moved, transcendentals=0),
        compiler_params=pltpu.CompilerParams(vmem_limit_bytes=int(limit * 2**20)),
    )


def edges_kernel(gas, kappa, to_right, to_left, held, arrived):
    copies = [pltpu.make_async_copy(gas.at[q], held.at[q], arrived.at[q]) for q in range(COMP)]
    copies.append(pltpu.make_async_copy(kappa, held.at[COMP], arrived.at[COMP]))
    for copy in copies:
        copy.start()
    lane = lanes()
    within = lane & 63
    depth, cell = within >> 4, within & 15
    high = jnp.maximum(6 * cell + 2 - depth, 0)
    low = 6 * cell + 3 + depth
    for pair in range((COMP + 1) // 2):
        packed = {}
        for q in (2 * pair, 2 * pair + 1):
            copies[q].wait()
            for tile in range(TILES):
                total = jnp.zeros((8, 128), jnp.float32)
                for x in range(GX):
                    here = (lane >= 6 * x) & (lane < 6 * x + 6)
                    total = jnp.where(here, pltpu.roll(held[q, x, rows(tile), :], 6 * x + 3, 1), total)
                packed[q, tile] = total
        for tile in range(TILES):
            first, second = packed[2 * pair, tile], packed[2 * pair + 1, tile]
            for out, index in ((to_right, high), (to_left, low)):
                out[pair, rows(tile), :] = jnp.where(lane < 64, pick(first, index), pick(second, index))


def strips_kernel(gas, kappa, to_right, to_left, from_left, from_right, strips, send_a, send_wall):
    lane = lanes()
    low_side = (lane & 1) == 1
    cell = jnp.clip((lane >> 1) - 3, 0, GX - 1)
    odd = lax.rem(lax.axis_index("sect"), 2)
    even = odd == 0
    for tile in range(TILES):
        held = {}
        for q, k in STRIPS:
            depth = k - 1 if k > 0 else -k
            index = cell + ((q % 2) * 64 + depth * 16)
            low, high = (from_left, from_right) if k > 0 else (to_left, to_right)
            value = jnp.where(low_side, pick(low[q // 2, rows(tile), :], index), pick(high[q // 2, rows(tile), :], index))
            strips[STRIP_AT[q, k], rows(tile), :] = value
            held[q, k] = value
        top = jnp.zeros((8, 128), jnp.float32)
        bottom = top
        for i, key in enumerate(CORNERS):
            here = (lane >> 2) == i
            top = jnp.where(here, pltpu.roll(held[key], (4 * i - 34) % 128, 1), top)
            bottom = jnp.where(here, pltpu.roll(held[key], (4 * i - 6) % 128, 1), bottom)
        for_a = jnp.where(even, top, bottom)
        for_b = jnp.where(even, bottom, top)
        send_a[LAYERS - 1, rows(tile), :] = for_a
        send_wall[LAYERS - 1 + tile] = for_b
    at_a, at_b = jnp.where(even, GX - 3, 0), jnp.where(even, 0, GX - 3)
    kappa_a, kappa_b = jnp.where(even, GX - 2, 0), jnp.where(even, 0, GX - 2)
    split = GR - 8
    for c in range(COMP):
        for layer in range(3):
            send_a[3 * c + layer] = gas[c, at_a + layer]
            send_wall[3 * c + layer] = gas[c, at_b + layer, split:, :]
    for layer in range(2):
        send_a[3 * COMP + layer] = kappa[kappa_a + layer]
        send_wall[3 * COMP + layer] = kappa[kappa_b + layer, split:, :]


def rest_kernel(gas, kappa, _, send_rest):
    even = lax.rem(lax.axis_index("sect"), 2) == 0
    split = GR - 8
    from_b, from_kappa = jnp.where(even, 0, GX - 3), jnp.where(even, 0, GX - 2)
    for c in range(COMP):
        for layer in range(3):
            send_rest[3 * c + layer] = gas[c, from_b + layer, :split, :]
    for layer in range(2):
        send_rest[3 * COMP + layer] = kappa[from_kappa + layer, :split, :]


def coupling(reaction):
    return [[0.3 * reaction[c, d] + (1.0 if c == d else 0.0) for d in range(COMP)] for c in range(COMP)]


def updated(c, values, neighbours, kappa, mix):
    total = mix[c][0] * values[0]
    for d in range(1, COMP):
        total = total + mix[c][d] * values[d]
    rate = kappa if DIFFUSE[c] == 1.0 else DIFFUSE[c] * kappa
    return total + rate * (neighbours - 6.0 * values[c])


def radial_sum(tiles, wall_only):
    sub = lax.broadcasted_iota(jnp.int32, (8, 128), 0)
    down = [pltpu.roll(t, 1, 0) for t in tiles]
    up = [pltpu.roll(t, 7, 0) for t in tiles]
    last = len(tiles) - 1
    sums = []
    for i, t in enumerate(tiles):
        if wall_only:
            below = down[i]
        else:
            below = jnp.where(sub == 0, down[i - 1] if i > 0 else t, down[i])
        above = jnp.where(sub == 7, up[i + 1] if i < last else t, up[i])
        sums.append(below + above)
    return sums


def strip_levels(strips, low_corner, high_corner, mix, edge, tiles):
    lane = lanes()
    wall_only = len(tiles) == 1
    from_low = (lane >= 2) & (lane < 6)
    from_high = (lane >= 38) & (lane < 42)
    held = {}
    for key in STRIPS:
        held[key] = [strips[STRIP_AT[key], rows(t), :] for t in tiles]
    for i, key in enumerate(CORNERS):
        for n in range(len(tiles)):
            value = jnp.where(from_low, pltpu.roll(low_corner[n], (2 - 4 * i) % 128, 1), held[key][n])
            held[key][n] = jnp.where(from_high, pltpu.roll(high_corner[n], (38 - 4 * i) % 128, 1), value)
    for step in range(ITERS):
        for c in range(COMP):
            for n in range(len(tiles)):
                edge[step, c, rows(n), :] = held[c, 1][n]
        if step == ITERS - 1:
            break
        later = {}
        for k in (2, 1, 0) if step == 0 else (1,):
            for c in range(COMP):
                radial = radial_sum(held[c, k], wall_only)
                later[c, k] = []
                for n in range(len(tiles)):
                    value = held[c, k][n]
                    around = held[c, k + 1][n] + held[c, k - 1][n]
                    around = around + pltpu.roll(value, 2, 1) + pltpu.roll(value, 126, 1) + radial[n]
                    later[c, k].append(updated(c, [held[d, k][n] for d in range(COMP)], around, held[COMP, k][n], mix))
        for key in [key for key in held if key[0] == COMP]:
            later[key] = held[key]
        held = later


def plane(src, kappa, edge, step, at, mix, count, wall_only, comps):
    lane = lanes()
    first, last = lane == 0, lane == 127
    shift = 127 - 2 * at
    values = [[src[c, at, rows(t), :] for t in range(count)] for c in range(COMP)]
    kap = [kappa[at, rows(t), :] for t in range(count)]
    out = {}
    for c in comps:
        radial = radial_sum(values[c], wall_only)
        for t in range(count):
            value = values[c][t]
            beyond = pltpu.roll(edge[step, c, rows(t), :], shift, 1)
            around = src[c, at - 1, rows(t), :] + src[c, at + 1, rows(t), :] + radial[t]
            around = around + jnp.where(first, beyond, pltpu.roll(value, 1, 1))
            around = around + jnp.where(last, beyond, pltpu.roll(value, 127, 1))
            out[c, t] = updated(c, [values[d][t] for d in range(COMP)], around, kap[t], mix)
    return out


def steps(count, wall_only, now, later, kappa, edge, mix, finish, unroll):
    for step in range(ITERS):
        src, dst = (now, later) if step % 2 == 0 else (later, now)
        final = step == ITERS - 1

        def body(at, carry, step=step, src=src, dst=dst, final=final):
            comps = (0,) if final and wall_only else range(COMP)
            out = plane(src, kappa, edge, step, at, mix, count, wall_only, comps)
            if final:
                finish(at, out)
            else:
                for (c, t), value in out.items():
                    dst[c, at, rows(t), :] = value
            return carry

        if unroll is None:
            for at in range(step + 1, EXT - 1 - step):
                body(at, 0)
        else:
            lax.fori_loop(step + 1, EXT - 1 - step, body, 0, unroll=unroll)


def wall_kernel(gas, kappa, strips, recv_a, recv_wall, reaction, wall, now, later, kap, edge):
    odd = lax.rem(lax.axis_index("sect"), 2)
    even = odd == 0
    mix = coupling(reaction)
    top = slice(GR - 8, GR)
    at_a, at_b = jnp.where(even, GX + 3, 0), jnp.where(even, 0, GX + 3)
    kappa_a, kappa_b = jnp.where(even, GX + 3, 1), jnp.where(even, 1, GX + 3)
    for c in range(COMP):
        for x in range(GX):
            now[c, x + 3] = gas[c, x, top, :]
        for layer in range(3):
            now[c, at_a + layer] = recv_a[3 * c + layer, top, :]
            now[c, at_b + layer] = recv_wall[3 * c + layer]
    for x in range(GX):
        kap[x + 3] = kappa[x, top, :]
    for layer in range(2):
        kap[kappa_a + layer] = recv_a[3 * COMP + layer, top, :]
        kap[kappa_b + layer] = recv_wall[3 * COMP + layer]
    corner_a, corner_b = recv_a[LAYERS - 1, top, :], recv_wall[LAYERS + TILES - 2]
    low, high = jnp.where(even, corner_b, corner_a), jnp.where(even, corner_a, corner_b)
    strip_levels(strips, [low], [high], mix, edge, [TILES - 1])

    def finish(at, out):
        wall[at - 3 : at - 2, :] = out[0, 0][7:8, :]

    steps(1, True, now, later, kap, edge, mix, finish, unroll=None)


def gas_kernel(gas, kappa, strips, recv_a, recv_wall, recv_rest, reaction, _, result, token, now, later, kap, edge):
    token[...] = jnp.zeros((8, 128), jnp.float32)
    odd = lax.rem(lax.axis_index("sect"), 2)
    even = odd == 0
    mix = coupling(reaction)
    split = GR - 8
    at_a, at_b = jnp.where(even, GX + 3, 0), jnp.where(even, 0, GX + 3)
    kappa_a, kappa_b = jnp.where(even, GX + 3, 1), jnp.where(even, 1, GX + 3)
    for c in range(COMP):
        now[c, 3 : GX + 3] = gas[c]
        for layer in range(3):
            now[c, at_a + layer] = recv_a[3 * c + layer]
            now[c, at_b + layer, split:, :] = recv_wall[3 * c + layer]
            now[c, at_b + layer, :split, :] = recv_rest[3 * c + layer]
    kap[3 : GX + 3] = kappa[...]
    for layer in range(2):
        kap[kappa_a + layer] = recv_a[3 * COMP + layer]
        kap[kappa_b + layer, split:, :] = recv_wall[3 * COMP + layer]
        kap[kappa_b + layer, :split, :] = recv_rest[3 * COMP + layer]
    low, high = [], []
    for t in range(TILES):
        corner_a = recv_a[LAYERS - 1, rows(t), :]
        corner_b = recv_wall[LAYERS - 1 + t]
        low.append(jnp.where(even, corner_b, corner_a))
        high.append(jnp.where(even, corner_a, corner_b))
    strip_levels(strips, low, high, mix, edge, list(range(TILES)))

    def finish(at, out):
        for (c, t), value in out.items():
            result[c, at - 3, rows(t), :] = value

    steps(TILES, False, now, later, kap, edge, mix, finish, unroll=2)


def pack_kernel(hop, cell, particles, mixing, heating, _, packed, cells, spread, ordered, source, begin, end):
    lane = lanes()
    square = (128, 128)
    down, across = lax.broadcasted_iota(jnp.int32, square, 0), lanes(square)
    moves = hop[...]
    named = [moves == j for j in range(MOVES)]
    table = jnp.concatenate(
        [jnp.where(m, 1.0, 0.0) for m in named] + [jnp.zeros((128 - MOVES * CHUNKS, 128), jnp.float32)], axis=0
    )
    running = jnp.dot(table, jnp.where(down <= across, 1.0, 0.0), preferred_element_type=jnp.float32)
    count = jnp.dot(table, jnp.ones(square, jnp.float32), preferred_element_type=jnp.float32)
    before = jnp.where(((down >> 4) == (across >> 4)) & (across < down), 1.0, 0.0)
    base = jnp.dot(before, count, preferred_element_type=jnp.float32)
    offset = jnp.zeros((CHUNKS, 128), jnp.float32)
    place = jnp.zeros((CHUNKS, 128), jnp.float32)
    across16 = lanes((CHUNKS, 128))
    for j in range(MOVES):
        part = slice(CHUNKS * j, CHUNKS * (j + 1))
        place = jnp.where(named[j], offset + running[part] - 1.0, place)
        first = base[part].astype(jnp.int32)
        source[part, :] = (across16 + offset.astype(jnp.int32) - first) & 127
        begin[part, :] = across16 - first
        end[part, :] = across16 - first - count[part].astype(jnp.int32)
        offset = offset + count[part]
    own = lax.broadcasted_iota(jnp.int32, (VALS, VALS), 0) == lax.broadcasted_iota(jnp.int32, (VALS, VALS), 1)
    weights = 0.5 * mixing[...] + jnp.where(own, 1.0, 0.0)
    first_value = lax.broadcasted_iota(jnp.int32, (VALS, VALS), 1) == 0
    weights = weights - jnp.where(first_value, heating[...], 0.0)
    for v in range(VALS):
        spread[v] = jnp.broadcast_to(weights[:, v : v + 1], (VALS, 128))
    place = place.astype(jnp.int32)
    position = lane.astype(jnp.float32)
    for chunk in range(CHUNKS):
        part = slice(128 * chunk, 128 * (chunk + 1))
        total = spread[0] * particles[0:1, part]
        for v in range(1, VALS):
            total = total + spread[v] * particles[v : v + 1, part]
        hot = jnp.where(down == place[chunk : chunk + 1, :], 1.0, 0.0)
        order = lax.dot_general(position, hot, (((1,), (1,)), ((), ())), preferred_element_type=jnp.float32)
        order = order.astype(jnp.int32)
        ordered[chunk, 0:8, :] = pick(total[0:8], order)
        ordered[chunk, 8:16, :] = pick(total[8:16], order)
        ordered[chunk, 16:24, :] = pick(
            jnp.broadcast_to(cell[chunk : chunk + 1, :], (8, 128)).astype(jnp.float32), order
        )

    def block(j, carry):
        held = [[jnp.zeros((8, 128), jnp.float32)] * 2 + [jnp.full((8, 128), -1.0)] for _ in range(SPOTS)]
        for chunk in range(CHUNKS):
            row = pl.ds(CHUNKS * j + chunk, 1)
            index = jnp.broadcast_to(source[row, :], (8, 128))
            parts = [pick(ordered[chunk, rows(n), :], index) for n in range(3)]
            start = jnp.broadcast_to(begin[row, :], (8, 128))
            stop = jnp.broadcast_to(end[row, :], (8, 128))
            for spot in range(SPOTS):
                here = (start >= -128 * spot) & (stop < -128 * spot)
                held[spot] = [jnp.where(here, new, old) for new, old in zip(parts, held[spot])]
        for spot in range(SPOTS):
            part = slice(128 * spot, 128 * (spot + 1))
            packed[j, 0:8, part] = held[spot][0]
            packed[j, 8:16, part] = held[spot][1]
            cells[j, spot : spot + 1, :] = held[spot][2][0:1, :].astype(jnp.int32)
        return carry

    lax.fori_loop(0, MOVES, block, 0)


def heat_kernel(wall, earlier, packed, cells, heating, *refs):
    outs, look = refs[:MOVES], refs[MOVES]
    flux = 0.5 * (wall[...] + earlier[...])
    heat = jnp.broadcast_to(heating[...], (VALS, 128))
    for j in range(MOVES):
        where_to = cells[j]
        row, column = where_to >> 7, where_to & 127
        found = jnp.zeros((8, 128), jnp.float32)
        for x in range(GX):
            line = jnp.broadcast_to(flux[x : x + 1, :], (8, 128))
            found = jnp.where(row == x, pick(line, column), found)
        look[j] = found
    for j in range(MOVES):
        for spot in range(SPOTS):
            part = slice(128 * spot, 128 * (spot + 1))
            outs[j][:, part] = packed[j, :, part] + heat * look[j, spot : spot + 1, :]


def join_kernel(*refs):
    pieces, out, done = refs[:MOVES], refs[MOVES + 1], refs[MOVES + 2]
    copies = [
        pltpu.make_async_copy(piece, out.at[:, j * CAP : (j + 1) * CAP], done.at[j]) for j, piece in enumerate(pieces)
    ]
    for copy in copies:
        copy.start()
    for copy in copies:
        copy.wait()


def ring(x, axis, by):
    size = lax.axis_size(axis)
    return lax.ppermute(x, axis, [(i, (i + by) % size) for i in range(size)])


def swap(x, axis, first):
    size = lax.axis_size(axis)
    pairs = [(i, i + 1) for i in range(first, size - 1, 2)]
    return lax.ppermute(x, axis, pairs + [(j, i) for i, j in pairs])


def local(gas, kappa, reaction, particles, mixing, heating, wall_cell, tile_hop):
    strip_shape = (3, GR, GA)
    to_right, to_left = call(
        edges_kernel,
        (f32(*strip_shape), f32(*strip_shape)),
        scratch=[pltpu.VMEM((COMP + 1, GX, GR, GA), jnp.float32), pltpu.SemaphoreType.DMA((COMP + 1,))],
        specs=[HBM] * 2,
        moved=2 << 20,
        limit=53.75,
    )(gas, kappa)
    from_left = ring(to_right, "blk", 1)
    from_right = ring(to_left, "blk", -1)

    strips, send_a, send_wall = call(
        strips_kernel,
        (f32(len(STRIPS), GR, GA), f32(LAYERS, GR, GA), f32(LAYERS - 1 + TILES, 8, GA)),
        specs=[VMEM] * 6,
        moved=2 << 20,
    )(gas, kappa, to_right, to_left, from_left, from_right)
    recv_wall = swap(send_wall, "sect", 1)
    recv_a = swap(send_a, "sect", 0)
    send_rest = call(rest_kernel, f32(LAYERS - 1, GR - 8, GA), specs=[VMEM] * 2 + [ANY], moved=1 << 20)(gas, kappa, recv_wall)
    recv_rest = swap(send_rest, "sect", 1)

    wall = call(
        wall_kernel,
        f32(GX, GA),
        scratch=[
            pltpu.VMEM((COMP, EXT, 8, GA), jnp.float32),
            pltpu.VMEM((COMP, EXT, 8, GA), jnp.float32),
            pltpu.VMEM((EXT, 8, GA), jnp.float32),
            pltpu.VMEM((ITERS, COMP, 8, GA), jnp.float32),
        ],
        specs=[VMEM] * 5 + [SMEM],
        moved=4 << 20,
    )(gas, kappa, strips, recv_a, recv_wall, reaction)
    heating_column = heating.reshape(VALS, 1)
    packed, cells = call(
        pack_kernel,
        (f32(MOVES, VALS, CAP), i32(MOVES, SPOTS, 128)),
        scratch=[
            pltpu.VMEM((VALS, VALS, 128), jnp.float32),
            pltpu.VMEM((CHUNKS, 24, 128), jnp.float32),
            pltpu.VMEM((MOVES * CHUNKS, 128), jnp.int32),
            pltpu.VMEM((MOVES * CHUNKS, 128), jnp.int32),
            pltpu.VMEM((MOVES * CHUNKS, 128), jnp.int32),
        ],
        specs=[VMEM] * 5 + [ANY],
        moved=4 << 20,
    )(tile_hop.reshape(CHUNKS, 128), wall_cell.reshape(CHUNKS, 128), particles, mixing, heating_column, wall)
    size = lax.axis_size("sect")
    earlier = lax.ppermute(wall, "sect", [(i, i + 1) for i in range(size - 1)])

    blocks = call(
        heat_kernel,
        (f32(VALS, CAP),) * MOVES,
        scratch=[pltpu.VMEM((MOVES, SPOTS, 128), jnp.float32)],
        specs=[VMEM] * 5,
        moved=2 << 20,
    )(wall, earlier, packed, cells, heating_column)
    pieces = [block if j == REACH else ring(block, "blk", j - REACH) for j, block in enumerate(blocks)]

    field, token = call(
        gas_kernel,
        (f32(COMP, GX, GR, GA), f32(8, 128)),
        scratch=[
            pltpu.VMEM((COMP, EXT, GR, GA), jnp.float32),
            pltpu.VMEM((COMP, EXT, GR, GA), jnp.float32),
            pltpu.VMEM((EXT, GR, GA), jnp.float32),
            pltpu.VMEM((ITERS, COMP, GR, GA), jnp.float32),
        ],
        specs=[VMEM] * 6 + [SMEM, ANY],
        moved=20 << 20,
    )(gas, kappa, strips, recv_a, recv_wall, recv_rest, reaction, pieces[0])
    arrived = call(
        join_kernel,
        f32(VALS, MOVES * CAP),
        scratch=[pltpu.SemaphoreType.DMA((MOVES,))],
        specs=[VMEM] * MOVES + [ANY],
        out_specs=HBM,
        moved=1 << 20,
    )(*pieces, token)
    return field, arrived


def solution(mesh):
    in_specs = (
        P(None, "sect", None, "blk"),
        P("sect", None, "blk"),
        P(),
        P(None, ("sect", "blk")),
        P(),
        P(),
        P(("sect", "blk")),
        P(("sect", "blk"), None),
    )
    out_specs = (P(None, "sect", None, "blk"), P(None, ("sect", "blk")))
    return jax.shard_map(local, mesh=mesh, in_specs=in_specs, out_specs=out_specs, check_vma=False)
```

```python
import jax
import jax.numpy as jnp
from jax import lax
from jax.experimental import pallas as pl
from jax.experimental.pallas import tpu as pltpu
from jax.sharding import PartitionSpec as P

REACH = 2
MOVES = 2 * REACH + 1
ITERS = 3
DIFFUSE = (1.0, 0.8, 0.6, 0.9, 0.7)
COMP = 5
GX = 16
GR = 32
GA = 128
TILES = GR // 8
EXT = GX + 2 * ITERS
CHUNKS = 16
VALS = 16
CAP = 1024
SPOTS = CAP // 128

FIELD_COLUMNS = (3, 2, 1, 0, -1)
KAPPA_COLUMNS = (2, 1, 0)
STRIPS = [(c, k) for c in range(COMP) for k in FIELD_COLUMNS] + [(COMP, k) for k in KAPPA_COLUMNS]
STRIP_AT = {key: i for i, key in enumerate(STRIPS)}
CORNERS = [(c, 1) for c in range(COMP)] + [(c, 2) for c in range(COMP)] + [(COMP, 1)] + [(c, 0) for c in range(COMP)]
LAYERS = 3 * COMP + 2 + 1

VMEM = pl.BlockSpec(memory_space=pltpu.VMEM)
SMEM = pl.BlockSpec(memory_space=pltpu.SMEM)
ANY = pl.BlockSpec(memory_space=pl.ANY)
HBM = pl.BlockSpec(memory_space=pltpu.HBM)


def f32(*shape):
    return jax.ShapeDtypeStruct(shape, jnp.float32)


def i32(*shape):
    return jax.ShapeDtypeStruct(shape, jnp.int32)


def lanes(shape=(8, 128)):
    return lax.broadcasted_iota(jnp.int32, shape, len(shape) - 1)


def pick(x, index):
    return jnp.take_along_axis(x, index, axis=1, mode="promise_in_bounds")


def rows(tile):
    return slice(8 * tile, 8 * tile + 8)


def call(kernel, outs, scratch=(), specs=None, out_specs=None, flops=0, moved=0, limit=16):
    return pl.pallas_call(
        kernel,
        out_shape=outs,
        in_specs=specs,
        out_specs=jax.tree.map(lambda _: VMEM, outs) if out_specs is None else out_specs,
        scratch_shapes=list(scratch),
        cost_estimate=pl.CostEstimate(flops=flops, bytes_accessed=moved, transcendentals=0),
        compiler_params=pltpu.CompilerParams(vmem_limit_bytes=int(limit * 2**20)),
    )


def edges_kernel(gas, kappa, send_q, send_p, held, arrived):
    copies = [pltpu.make_async_copy(gas.at[q], held.at[q], arrived.at[q]) for q in range(COMP)]
    copies.append(pltpu.make_async_copy(kappa, held.at[COMP], arrived.at[COMP]))
    for copy in copies:
        copy.start()
    lane = lanes()
    within = lane & 63
    depth, cell = within >> 4, within & 15
    high = jnp.maximum(6 * cell + 2 - depth, 0)
    low = 6 * cell + 3 + depth
    odd = lax.rem(lax.axis_index("blk"), 2) == 1
    index_q, index_p = jnp.where(odd, high, low), jnp.where(odd, low, high)
    for pair in range((COMP + 1) // 2):
        packed = {}
        for q in (2 * pair, 2 * pair + 1):
            copies[q].wait()
            for tile in range(TILES):
                total = jnp.zeros((8, 128), jnp.float32)
                for x in range(GX):
                    here = (lane >= 6 * x) & (lane < 6 * x + 6)
                    total = jnp.where(here, pltpu.roll(held[q, x, rows(tile), :], 6 * x + 3, 1), total)
                packed[q, tile] = total
        for tile in range(TILES):
            first, second = packed[2 * pair, tile], packed[2 * pair + 1, tile]
            for out, index in ((send_q, index_q), (send_p, index_p)):
                out[pair, rows(tile), :] = jnp.where(lane < 64, pick(first, index), pick(second, index))


def strips_kernel(gas, kappa, send_q, send_p, recv_q, recv_p, _, strips, send_a, send_wall):
    lane = lanes()
    low_side = (lane & 1) == 1
    cell = jnp.clip((lane >> 1) - 3, 0, GX - 1)
    even = lax.rem(lax.axis_index("sect"), 2) == 0
    odd_tile = lax.rem(lax.axis_index("blk"), 2) == 1
    for tile in range(TILES):
        held = {}
        slabs = [[ref[s, rows(tile), :] for s in range(3)] for ref in (send_q, send_p, recv_q, recv_p)]
        own_q, own_p, got_q, got_p = slabs
        to_left = [jnp.where(odd_tile, p, q) for q, p in zip(own_q, own_p)]
        to_right = [jnp.where(odd_tile, q, p) for q, p in zip(own_q, own_p)]
        from_left = [jnp.where(odd_tile, p, q) for q, p in zip(got_q, got_p)]
        from_right = [jnp.where(odd_tile, q, p) for q, p in zip(got_q, got_p)]
        for q, k in STRIPS:
            depth = k - 1 if k > 0 else -k
            index = cell + ((q % 2) * 64 + depth * 16)
            low, high = (from_left, from_right) if k > 0 else (to_left, to_right)
            value = jnp.where(low_side, pick(low[q // 2], index), pick(high[q // 2], index))
            strips[STRIP_AT[q, k], rows(tile), :] = value
            held[q, k] = value
        top = jnp.zeros((8, 128), jnp.float32)
        bottom = top
        for i, key in enumerate(CORNERS):
            here = (lane >> 2) == i
            top = jnp.where(here, pltpu.roll(held[key], (4 * i - 34) % 128, 1), top)
            bottom = jnp.where(here, pltpu.roll(held[key], (4 * i - 6) % 128, 1), bottom)
        for_a = jnp.where(even, top, bottom)
        for_b = jnp.where(even, bottom, top)
        send_a[LAYERS - 1, rows(tile), :] = for_a
        send_wall[LAYERS - 1 + tile] = for_b
    at_a, at_b = jnp.where(even, GX - 3, 0), jnp.where(even, 0, GX - 3)
    kappa_a, kappa_b = jnp.where(even, GX - 2, 0), jnp.where(even, 0, GX - 2)
    split = GR - 8
    for c in range(COMP):
        for layer in range(3):
            send_a[3 * c + layer] = gas[c, at_a + layer]
            send_wall[3 * c + layer] = gas[c, at_b + layer, split:, :]
    for layer in range(2):
        send_a[3 * COMP + layer] = kappa[kappa_a + layer]
        send_wall[3 * COMP + layer] = kappa[kappa_b + layer, split:, :]


def rest_kernel(gas, kappa, send_rest):
    even = lax.rem(lax.axis_index("sect"), 2) == 0
    split = GR - 8
    from_b, from_kappa = jnp.where(even, 0, GX - 3), jnp.where(even, 0, GX - 2)
    for c in range(COMP):
        for layer in range(3):
            send_rest[3 * c + layer] = gas[c, from_b + layer, :split, :]
    for layer in range(2):
        send_rest[3 * COMP + layer] = kappa[from_kappa + layer, :split, :]


def coupling(reaction):
    return [[0.3 * reaction[c, d] + (1.0 if c == d else 0.0) for d in range(COMP)] for c in range(COMP)]


def updated(c, values, neighbours, kappa, mix):
    total = mix[c][0] * values[0]
    for d in range(1, COMP):
        total = total + mix[c][d] * values[d]
    rate = kappa if DIFFUSE[c] == 1.0 else DIFFUSE[c] * kappa
    return total + rate * (neighbours - 6.0 * values[c])


def radial_sum(tiles, wall_only):
    sub = lax.broadcasted_iota(jnp.int32, (8, 128), 0)
    down = [pltpu.roll(t, 1, 0) for t in tiles]
    up = [pltpu.roll(t, 7, 0) for t in tiles]
    last = len(tiles) - 1
    sums = []
    for i, t in enumerate(tiles):
        if wall_only:
            below = down[i]
        else:
            below = jnp.where(sub == 0, down[i - 1] if i > 0 else t, down[i])
        above = jnp.where(sub == 7, up[i + 1] if i < last else t, up[i])
        sums.append(below + above)
    return sums


def radial_sum_of(src, c, at, values):
    sub = lax.broadcasted_iota(jnp.int32, (8, 128), 0)
    sums = []
    for t in range(TILES):
        first, last = t == 0, t == TILES - 1
        below = jnp.where(sub == 0, values[t], pltpu.roll(values[t], 1, 0)) if first else src[c, at, 8 * t - 1 : 8 * t + 7, :]
        above = jnp.where(sub == 7, values[t], pltpu.roll(values[t], 7, 0)) if last else src[c, at, 8 * t + 1 : 8 * t + 9, :]
        sums.append(below + above)
    return sums


def strip_levels(strips, low_corner, high_corner, mix, edge, tiles):
    lane = lanes()
    wall_only = len(tiles) == 1
    from_low = (lane >= 2) & (lane < 6)
    from_high = (lane >= 38) & (lane < 42)
    held = {}
    for key in STRIPS:
        held[key] = [strips[STRIP_AT[key], rows(t), :] for t in tiles]
    for i, key in enumerate(CORNERS if low_corner else ()):
        for n in range(len(tiles)):
            value = jnp.where(from_low, pltpu.roll(low_corner[n], (2 - 4 * i) % 128, 1), held[key][n])
            held[key][n] = jnp.where(from_high, pltpu.roll(high_corner[n], (38 - 4 * i) % 128, 1), value)
    for step in range(ITERS):
        for c in range(COMP):
            for n in range(len(tiles)):
                edge[step, c, rows(n), :] = held[c, 1][n]
        if step == ITERS - 1:
            break
        later = {}
        for k in (2, 1, 0) if step == 0 else (1,):
            for c in range(COMP):
                radial = radial_sum(held[c, k], wall_only)
                later[c, k] = []
                for n in range(len(tiles)):
                    value = held[c, k][n]
                    around = held[c, k + 1][n] + held[c, k - 1][n]
                    around = around + pltpu.roll(value, 2, 1) + pltpu.roll(value, 126, 1) + radial[n]
                    later[c, k].append(updated(c, [held[d, k][n] for d in range(COMP)], around, held[COMP, k][n], mix))
        for key in [key for key in held if key[0] == COMP]:
            later[key] = held[key]
        held = later


def plane(src, kappa, edge, step, at, x, mix, count, comps):
    lane = lanes()
    first, last = lane == 0, lane == 127
    shift = 121 - 2 * x
    values = [[src[c, at, rows(t), :] for t in range(count)] for c in range(COMP)]
    kap = [kappa[at, rows(t), :] for t in range(count)]
    out = {}
    for c in comps:
        radial = radial_sum(values[c], True) if count == 1 else radial_sum_of(src, c, at, values[c])
        for t in range(count):
            value = values[c][t]
            beyond = pltpu.roll(edge[step, c, rows(t), :], shift, 1)
            around = src[c, at - 1, rows(t), :] + src[c, at + 1, rows(t), :] + radial[t]
            around = around + jnp.where(first, beyond, pltpu.roll(value, 1, 1))
            around = around + jnp.where(last, beyond, pltpu.roll(value, 127, 1))
            out[c, t] = updated(c, [values[d][t] for d in range(COMP)], around, kap[t], mix)
    return out


def wall_kernel(gas, kappa, strips, recv_a, recv_wall, reaction, _, wall, now, later, kap, edge):
    odd = lax.rem(lax.axis_index("sect"), 2)
    even = odd == 0
    mix = coupling(reaction)
    top = slice(GR - 8, GR)
    at_a, at_b = jnp.where(even, GX + 3, 0), jnp.where(even, 0, GX + 3)
    kappa_a, kappa_b = jnp.where(even, GX + 3, 1), jnp.where(even, 1, GX + 3)
    for c in range(COMP):
        for x in range(GX):
            now[c, x + 3] = gas[c, x, top, :]
        for layer in range(3):
            now[c, at_a + layer] = recv_a[3 * c + layer, top, :]
            now[c, at_b + layer] = recv_wall[3 * c + layer]
    for x in range(GX):
        kap[x + 3] = kappa[x, top, :]
    for layer in range(2):
        kap[kappa_a + layer] = recv_a[3 * COMP + layer, top, :]
        kap[kappa_b + layer] = recv_wall[3 * COMP + layer]
    corner_a, corner_b = recv_a[LAYERS - 1, top, :], recv_wall[LAYERS + TILES - 2]
    low, high = jnp.where(even, corner_b, corner_a), jnp.where(even, corner_a, corner_b)
    strip_levels(strips, [low], [high], mix, edge, [TILES - 1])

    for step, (src, dst) in enumerate(((now, later), (later, now), (now, None))):
        comps = (0,) if step == ITERS - 1 else range(COMP)
        for at in range(step + 1, EXT - 1 - step):
            out = plane(src, kap, edge, step, at, at - 3, mix, 1, comps)
            if step == ITERS - 1:
                wall[at - 3 : at - 2, :] = out[0, 0][7:8, :]
                continue
            for c in comps:
                dst[c, at] = out[c, 0]


def inner_kernel(gas, kappa, strips, reaction, first, second, middle, edge):
    mix = coupling(reaction)
    strip_levels(strips, None, None, mix, edge, list(range(TILES)))
    for step, (src, dst) in enumerate(((gas, first), (first, second), (second, middle))):

        def body(x, carry, step=step, src=src, dst=dst):
            out = plane(src, kappa, edge, step, x, x, mix, TILES, range(COMP))
            into = x - 3 if step == ITERS - 1 else x
            for (c, t), value in out.items():
                dst[c, into, rows(t), :] = value
            return carry

        lax.fori_loop(step + 1, GX - 1 - step, body, 0, unroll=2)


def outer_kernel(
    gas, kappa, strips, first, second, middle, recv_a, recv_wall, both_rest, reaction, _, result, token, now, later, kap, edge
):
    token[...] = jnp.zeros((8, 128), jnp.float32)
    even = lax.rem(lax.axis_index("sect"), 2) == 0
    mix = coupling(reaction)
    split = GR - 8
    section, sections = lax.axis_index("sect"), lax.axis_size("sect")
    inside = (section > 0) & (section < sections - 1)
    other = jnp.where(even, 0, 1)

    def recv_rest(layer):
        return jnp.where(inside, both_rest[other, layer], 0.0)

    at_a, at_b = jnp.where(even, GX + 3, 0), jnp.where(even, 0, GX + 3)
    kappa_a, kappa_b = jnp.where(even, GX + 3, 1), jnp.where(even, 1, GX + 3)
    for c in range(COMP):
        for x in (0, 1, GX - 2, GX - 1):
            now[c, x + 3] = gas[c, x]
        for layer in range(3):
            now[c, at_a + layer] = recv_a[3 * c + layer]
            now[c, at_b + layer, split:, :] = recv_wall[3 * c + layer]
            now[c, at_b + layer, :split, :] = recv_rest(3 * c + layer)
        for x in (1, 2, GX - 3, GX - 2):
            later[c, x + 3] = first[c, x]
    for x in (0, 1, 2, GX - 3, GX - 2, GX - 1):
        kap[x + 3] = kappa[x]
    for layer in range(2):
        kap[kappa_a + layer] = recv_a[3 * COMP + layer]
        kap[kappa_b + layer, split:, :] = recv_wall[3 * COMP + layer]
        kap[kappa_b + layer, :split, :] = recv_rest(3 * COMP + layer)
    low, high = [], []
    for t in range(TILES):
        corner_a = recv_a[LAYERS - 1, rows(t), :]
        corner_b = recv_wall[LAYERS - 1 + t]
        low.append(jnp.where(even, corner_b, corner_a))
        high.append(jnp.where(even, corner_a, corner_b))
    strip_levels(strips, low, high, mix, edge, list(range(TILES)))
    for c in range(COMP):
        result[c, 3 : GX - 3] = middle[c]
    for step, (src, dst) in enumerate(((now, later), (later, now), (now, None))):
        if step == ITERS - 1:
            for c in range(COMP):
                for x in (2, 3, GX - 4, GX - 3):
                    now[c, x + 3] = second[c, x]
        for i in range(3):
            for at in (step + 1 + i, GX + 2 - step + i):
                out = plane(src, kap, edge, step, at, at - 3, mix, TILES, range(COMP))
                for (c, t), value in out.items():
                    if step == ITERS - 1:
                        result[c, at - 3, rows(t), :] = value
                    else:
                        dst[c, at, rows(t), :] = value


def pack_kernel(hop, cell, particles, mixing, heating, _, packed, cells, spread, ordered, source, begin, end):
    lane = lanes()
    square = (128, 128)
    down, across = lax.broadcasted_iota(jnp.int32, square, 0), lanes(square)
    moves = hop[...]
    named = [moves == j for j in range(MOVES)]
    table = jnp.concatenate(
        [jnp.where(m, 1.0, 0.0) for m in named] + [jnp.zeros((128 - MOVES * CHUNKS, 128), jnp.float32)], axis=0
    )
    running = jnp.dot(table, jnp.where(down <= across, 1.0, 0.0), preferred_element_type=jnp.float32)
    count = jnp.dot(table, jnp.ones(square, jnp.float32), preferred_element_type=jnp.float32)
    before = jnp.where(((down >> 4) == (across >> 4)) & (across < down), 1.0, 0.0)
    base = jnp.dot(before, count, preferred_element_type=jnp.float32)
    offset = jnp.zeros((CHUNKS, 128), jnp.float32)
    place = jnp.zeros((CHUNKS, 128), jnp.float32)
    across16 = lanes((CHUNKS, 128))
    for j in range(MOVES):
        part = slice(CHUNKS * j, CHUNKS * (j + 1))
        place = jnp.where(named[j], offset + running[part] - 1.0, place)
        first = base[part].astype(jnp.int32)
        source[part, :] = (across16 + offset.astype(jnp.int32) - first) & 127
        begin[part, :] = across16 - first
        end[part, :] = across16 - first - count[part].astype(jnp.int32)
        offset = offset + count[part]
    own = lax.broadcasted_iota(jnp.int32, (VALS, VALS), 0) == lax.broadcasted_iota(jnp.int32, (VALS, VALS), 1)
    weights = 0.5 * mixing[...] + jnp.where(own, 1.0, 0.0)
    first_value = lax.broadcasted_iota(jnp.int32, (VALS, VALS), 1) == 0
    weights = weights - jnp.where(first_value, heating[...], 0.0)
    for v in range(VALS):
        spread[v] = jnp.broadcast_to(weights[:, v : v + 1], (VALS, 128))
    place = place.astype(jnp.int32)
    position = lane.astype(jnp.float32)
    for chunk in range(CHUNKS):
        part = slice(128 * chunk, 128 * (chunk + 1))
        total = spread[0] * particles[0:1, part]
        for v in range(1, VALS):
            total = total + spread[v] * particles[v : v + 1, part]
        hot = jnp.where(down == place[chunk : chunk + 1, :], 1.0, 0.0)
        order = lax.dot_general(position, hot, (((1,), (1,)), ((), ())), preferred_element_type=jnp.float32)
        order = order.astype(jnp.int32)
        ordered[chunk, 0:8, :] = pick(total[0:8], order)
        ordered[chunk, 8:16, :] = pick(total[8:16], order)
        ordered[chunk, 16:24, :] = pick(
            jnp.broadcast_to(cell[chunk : chunk + 1, :], (8, 128)).astype(jnp.float32), order
        )

    def block(j, carry):
        held = [[jnp.zeros((8, 128), jnp.float32)] * 2 + [jnp.full((8, 128), -1.0)] for _ in range(SPOTS)]
        for chunk in range(CHUNKS):
            row = pl.ds(CHUNKS * j + chunk, 1)
            index = jnp.broadcast_to(source[row, :], (8, 128))
            parts = [pick(ordered[chunk, rows(n), :], index) for n in range(3)]
            start = jnp.broadcast_to(begin[row, :], (8, 128))
            stop = jnp.broadcast_to(end[row, :], (8, 128))
            for spot in range(SPOTS):
                here = (start >= -128 * spot) & (stop < -128 * spot)
                held[spot] = [jnp.where(here, new, old) for new, old in zip(parts, held[spot])]
        for spot in range(SPOTS):
            part = slice(128 * spot, 128 * (spot + 1))
            packed[j, 0:8, part] = held[spot][0]
            packed[j, 8:16, part] = held[spot][1]
            cells[j, spot : spot + 1, :] = held[spot][2][0:1, :].astype(jnp.int32)
        return carry

    lax.fori_loop(0, MOVES, block, 0)


def moves_of_swaps():
    tile = lax.axis_index("blk")
    odd, late = lax.rem(tile, 2), lax.rem(tile, 4) >> 1
    return [REACH - 1 + 2 * odd, 2 * REACH * late, 2 * REACH * (1 - late), REACH + 1 - 2 * odd]


def heat_kernel(wall, earlier, packed, cells, heating, own, send_q, send_s, send_r, send_p, look):
    flux = 0.5 * (wall[...] + earlier[...])
    heat = jnp.broadcast_to(heating[...], (VALS, 128))
    for j in range(MOVES):
        where_to = cells[j]
        row, column = where_to >> 7, where_to & 127
        found = jnp.zeros((8, 128), jnp.float32)
        for x in range(GX):
            line = jnp.broadcast_to(flux[x : x + 1, :], (8, 128))
            found = jnp.where(row == x, pick(line, column), found)
        look[j] = found
    for out, j in zip((own, send_q, send_s, send_r, send_p), [REACH] + moves_of_swaps()):
        for spot in range(SPOTS):
            part = slice(128 * spot, 128 * (spot + 1))
            out[:, part] = packed[j, :, part] + heat * look[j, spot : spot + 1, :]


def join_kernel(own, recv_q, recv_s, recv_r, recv_p, _, out, done):
    copies = []
    for n, (piece, j) in enumerate(zip((own, recv_q, recv_s, recv_r, recv_p), [REACH] + moves_of_swaps())):
        place = pl.multiple_of((2 * REACH - j) * CAP, CAP)
        copies.append(pltpu.make_async_copy(piece, out.at[:, pl.ds(place, CAP)], done.at[n]))
    for copy in copies:
        copy.start()
    for copy in copies:
        copy.wait()


def swap(x, axis, pairs):
    return lax.ppermute(x, axis, pairs + [(j, i) for i, j in pairs])


def local(gas, kappa, reaction, particles, mixing, heating, wall_cell, tile_hop):
    sections, tiles = lax.axis_size("sect"), lax.axis_size("blk")
    pairs_a = [(i, i + 1) for i in range(0, sections, 2)]
    pairs_b = [(i, i + 1) for i in range(1, sections - 1, 2)]
    pairs_q = [(i, (i + 1) % tiles) for i in range(1, tiles, 2)]
    pairs_p = [(i, i + 1) for i in range(0, tiles, 2)]
    pairs_s = [(i, (i + 2) % tiles) for i in range(tiles) if i % 4 >= 2]
    pairs_r = [(i, i + 2) for i in range(tiles) if i % 4 < 2]

    send_q, send_p = call(
        edges_kernel,
        (f32(3, GR, GA), f32(3, GR, GA)),
        scratch=[pltpu.VMEM((COMP + 1, GX, GR, GA), jnp.float32), pltpu.SemaphoreType.DMA((COMP + 1,))],
        specs=[HBM] * 2,
        moved=2 << 20,
        limit=53.75,
    )(gas, kappa)
    recv_q = swap(send_q, "blk", pairs_q)
    recv_p = swap(send_p, "blk", pairs_p)
    send_rest = call(rest_kernel, f32(LAYERS - 1, GR - 8, GA), specs=[VMEM] * 2, moved=1 << 18)(gas, kappa)
    groups = [list(pair) for pair in pairs_b] + [[0, sections - 1]]
    both_rest = lax.all_gather(send_rest, "sect", axis_index_groups=groups)

    strips, send_a, send_wall = call(
        strips_kernel,
        (f32(len(STRIPS), GR, GA), f32(LAYERS, GR, GA), f32(LAYERS - 1 + TILES, 8, GA)),
        specs=[VMEM] * 6 + [ANY],
        moved=2 << 20,
    )(gas, kappa, send_q, send_p, recv_q, recv_p, send_rest)
    recv_wall = swap(send_wall, "sect", pairs_b)
    recv_a = swap(send_a, "sect", pairs_a)

    whole = f32(COMP, GX, GR, GA)
    first, second, middle = call(
        inner_kernel,
        (whole, whole, f32(COMP, GX - 6, GR, GA)),
        scratch=[pltpu.VMEM((ITERS, COMP, GR, GA), jnp.float32)],
        specs=[VMEM] * 3 + [SMEM],
        moved=12 << 20,
    )(gas, kappa, strips, reaction)

    wall = call(
        wall_kernel,
        f32(GX, GA),
        scratch=[
            pltpu.VMEM((COMP, EXT, 8, GA), jnp.float32),
            pltpu.VMEM((COMP, EXT, 8, GA), jnp.float32),
            pltpu.VMEM((EXT, 8, GA), jnp.float32),
            pltpu.VMEM((ITERS, COMP, 8, GA), jnp.float32),
        ],
        specs=[VMEM] * 5 + [SMEM, ANY],
        moved=4 << 20,
    )(gas, kappa, strips, recv_a, recv_wall, reaction, middle)
    earlier = lax.ppermute(wall, "sect", [(i, i + 1) for i in range(sections - 1)])

    heating_column = heating.reshape(VALS, 1)
    packed, cells = call(
        pack_kernel,
        (f32(MOVES, VALS, CAP), i32(MOVES, SPOTS, 128)),
        scratch=[
            pltpu.VMEM((VALS, VALS, 128), jnp.float32),
            pltpu.VMEM((CHUNKS, 24, 128), jnp.float32),
            pltpu.VMEM((MOVES * CHUNKS, 128), jnp.int32),
            pltpu.VMEM((MOVES * CHUNKS, 128), jnp.int32),
            pltpu.VMEM((MOVES * CHUNKS, 128), jnp.int32),
        ],
        specs=[VMEM] * 5 + [ANY],
        moved=4 << 20,
    )(tile_hop.reshape(CHUNKS, 128), wall_cell.reshape(CHUNKS, 128), particles, mixing, heating_column, wall)
    own, *sends = call(
        heat_kernel,
        (f32(VALS, CAP),) * MOVES,
        scratch=[pltpu.VMEM((MOVES, SPOTS, 128), jnp.float32)],
        specs=[VMEM] * 5,
        moved=2 << 20,
    )(wall, earlier, packed, cells, heating_column)
    pieces = [swap(x, "blk", pairs) for x, pairs in zip(sends, (pairs_q, pairs_s, pairs_r, pairs_p))]

    field, token = call(
        outer_kernel,
        (whole, f32(8, 128)),
        scratch=[
            pltpu.VMEM((COMP, EXT, GR, GA), jnp.float32),
            pltpu.VMEM((COMP, EXT, GR, GA), jnp.float32),
            pltpu.VMEM((EXT, GR, GA), jnp.float32),
            pltpu.VMEM((ITERS, COMP, GR, GA), jnp.float32),
        ],
        specs=[VMEM] * 9 + [SMEM, ANY],
        moved=8 << 20,
    )(gas, kappa, strips, first, second, middle, recv_a, recv_wall, both_rest, reaction, pieces[0])
    arrived = call(
        join_kernel,
        f32(VALS, MOVES * CAP),
        scratch=[pltpu.SemaphoreType.DMA((MOVES,))],
        specs=[VMEM] * MOVES + [ANY],
        out_specs=HBM,
        moved=1 << 20,
    )(own, *pieces, token)
    return field, arrived


def solution(mesh):
    in_specs = (
        P(None, "sect", None, "blk"),
        P("sect", None, "blk"),
        P(),
        P(None, ("sect", "blk")),
        P(),
        P(),
        P(("sect", "blk")),
        P(("sect", "blk"), None),
    )
    out_specs = (P(None, "sect", None, "blk"), P(None, ("sect", "blk")))
    return jax.shard_map(local, mesh=mesh, in_specs=in_specs, out_specs=out_specs, check_vma=False)
```

```python
import jax
import jax.numpy as jnp
from jax import lax
from jax.experimental import pallas as pl
from jax.experimental.pallas import tpu as pltpu
from jax.sharding import PartitionSpec as P

REACH = 2
MOVES = 2 * REACH + 1
ITERS = 3
DIFFUSE = (1.0, 0.8, 0.6, 0.9, 0.7)
COMP = 5
GX = 16
GR = 32
GA = 128
TILES = GR // 8
EXT = GX + 2 * ITERS
CHUNKS = 16
VALS = 16
CAP = 1024
SPOTS = CAP // 128

FIELD_COLUMNS = (3, 2, 1, 0, -1)
KAPPA_COLUMNS = (2, 1, 0)
STRIPS = [(c, k) for c in range(COMP) for k in FIELD_COLUMNS] + [(COMP, k) for k in KAPPA_COLUMNS]
STRIP_AT = {key: i for i, key in enumerate(STRIPS)}
CORNERS = [(c, 1) for c in range(COMP)] + [(c, 2) for c in range(COMP)] + [(COMP, 1)] + [(c, 0) for c in range(COMP)]
LAYERS = 3 * COMP + 2 + 1
SEAM = (1, 2, GX - 3, GX - 2)

VMEM = pl.BlockSpec(memory_space=pltpu.VMEM)
SMEM = pl.BlockSpec(memory_space=pltpu.SMEM)
ANY = pl.BlockSpec(memory_space=pl.ANY)
HBM = pl.BlockSpec(memory_space=pltpu.HBM)


def f32(*shape):
    return jax.ShapeDtypeStruct(shape, jnp.float32)


def i32(*shape):
    return jax.ShapeDtypeStruct(shape, jnp.int32)


def lanes(shape=(8, 128)):
    return lax.broadcasted_iota(jnp.int32, shape, len(shape) - 1)


def pick(x, index):
    return jnp.take_along_axis(x, index, axis=1, mode="promise_in_bounds")


def rows(tile):
    return slice(8 * tile, 8 * tile + 8)


def call(kernel, outs, scratch=(), specs=None, out_specs=None, flops=0, moved=0, limit=16):
    return pl.pallas_call(
        kernel,
        out_shape=outs,
        in_specs=specs,
        out_specs=jax.tree.map(lambda _: VMEM, outs) if out_specs is None else out_specs,
        scratch_shapes=list(scratch),
        cost_estimate=pl.CostEstimate(flops=flops, bytes_accessed=moved, transcendentals=0),
        compiler_params=pltpu.CompilerParams(vmem_limit_bytes=int(limit * 2**20)),
    )


def edges_kernel(gas, kappa, send_q, send_p, held, arrived):
    copies = [pltpu.make_async_copy(gas.at[q], held.at[q], arrived.at[q]) for q in range(COMP)]
    copies.append(pltpu.make_async_copy(kappa, held.at[COMP], arrived.at[COMP]))
    for copy in copies:
        copy.start()
    lane = lanes()
    within = lane & 63
    depth, cell = within >> 4, within & 15
    high = jnp.maximum(6 * cell + 2 - depth, 0)
    low = 6 * cell + 3 + depth
    odd = lax.rem(lax.axis_index("blk"), 2) == 1
    index_q, index_p = jnp.where(odd, high, low), jnp.where(odd, low, high)
    for pair in range((COMP + 1) // 2):
        packed = {}
        for q in (2 * pair, 2 * pair + 1):
            copies[q].wait()
            for tile in range(TILES):
                total = jnp.zeros((8, 128), jnp.float32)
                for x in range(GX):
                    here = (lane >= 6 * x) & (lane < 6 * x + 6)
                    total = jnp.where(here, pltpu.roll(held[q, x, rows(tile), :], 6 * x + 3, 1), total)
                packed[q, tile] = total
        for tile in range(TILES):
            first, second = packed[2 * pair, tile], packed[2 * pair + 1, tile]
            for out, index in ((send_q, index_q), (send_p, index_p)):
                out[pair, rows(tile), :] = jnp.where(lane < 64, pick(first, index), pick(second, index))


def strips_kernel(gas, kappa, send_q, send_p, recv_q, recv_p, _, strips, send_a, send_wall):
    lane = lanes()
    low_side = (lane & 1) == 1
    cell = jnp.clip((lane >> 1) - 3, 0, GX - 1)
    even = lax.rem(lax.axis_index("sect"), 2) == 0
    odd_tile = lax.rem(lax.axis_index("blk"), 2) == 1
    for tile in range(TILES):
        held = {}
        slabs = [[ref[s, rows(tile), :] for s in range(3)] for ref in (send_q, send_p, recv_q, recv_p)]
        own_q, own_p, got_q, got_p = slabs
        to_left = [jnp.where(odd_tile, p, q) for q, p in zip(own_q, own_p)]
        to_right = [jnp.where(odd_tile, q, p) for q, p in zip(own_q, own_p)]
        from_left = [jnp.where(odd_tile, p, q) for q, p in zip(got_q, got_p)]
        from_right = [jnp.where(odd_tile, q, p) for q, p in zip(got_q, got_p)]
        for q, k in STRIPS:
            depth = k - 1 if k > 0 else -k
            index = cell + ((q % 2) * 64 + depth * 16)
            low, high = (from_left, from_right) if k > 0 else (to_left, to_right)
            value = jnp.where(low_side, pick(low[q // 2], index), pick(high[q // 2], index))
            strips[STRIP_AT[q, k], rows(tile), :] = value
            held[q, k] = value
        top = jnp.zeros((8, 128), jnp.float32)
        bottom = top
        for i, key in enumerate(CORNERS):
            here = (lane >> 2) == i
            top = jnp.where(here, pltpu.roll(held[key], (4 * i - 34) % 128, 1), top)
            bottom = jnp.where(here, pltpu.roll(held[key], (4 * i - 6) % 128, 1), bottom)
        for_a = jnp.where(even, top, bottom)
        for_b = jnp.where(even, bottom, top)
        send_a[LAYERS - 1, rows(tile), :] = for_a
        send_wall[2 * (LAYERS - 1) + tile] = for_b
    at_a, at_b = jnp.where(even, GX - 3, 0), jnp.where(even, 0, GX - 3)
    kappa_a, kappa_b = jnp.where(even, GX - 2, 0), jnp.where(even, 0, GX - 2)
    for c in range(COMP):
        for layer in range(3):
            send_a[3 * c + layer] = gas[c, at_a + layer]
            for half in range(2):
                send_wall[2 * (3 * c + layer) + half] = gas[c, at_b + layer, rows(2 + half), :]
    for layer in range(2):
        send_a[3 * COMP + layer] = kappa[kappa_a + layer]
        for half in range(2):
            send_wall[2 * (3 * COMP + layer) + half] = kappa[kappa_b + layer, rows(2 + half), :]


def rest_kernel(gas, kappa, _, send_rest):
    even = lax.rem(lax.axis_index("sect"), 2) == 0
    split = GR // 2
    from_b, from_kappa = jnp.where(even, 0, GX - 3), jnp.where(even, 0, GX - 2)
    for c in range(COMP):
        for layer in range(3):
            send_rest[3 * c + layer] = gas[c, from_b + layer, :split, :]
    for layer in range(2):
        send_rest[3 * COMP + layer] = kappa[from_kappa + layer, :split, :]


def coupling(reaction):
    return [[0.3 * reaction[c, d] + (1.0 if c == d else 0.0) for d in range(COMP)] for c in range(COMP)]


def updated(c, values, neighbours, kappa, mix):
    total = mix[c][0] * values[0]
    for d in range(1, COMP):
        total = total + mix[c][d] * values[d]
    rate = kappa if DIFFUSE[c] == 1.0 else DIFFUSE[c] * kappa
    return total + rate * (neighbours - 6.0 * values[c])


def radial_sum(tiles, wall_only):
    sub = lax.broadcasted_iota(jnp.int32, (8, 128), 0)
    down = [pltpu.roll(t, 1, 0) for t in tiles]
    up = [pltpu.roll(t, 7, 0) for t in tiles]
    last = len(tiles) - 1
    sums = []
    for i, t in enumerate(tiles):
        if wall_only:
            below = down[i]
        else:
            below = jnp.where(sub == 0, down[i - 1] if i > 0 else t, down[i])
        above = jnp.where(sub == 7, up[i + 1] if i < last else t, up[i])
        sums.append(below + above)
    return sums


def radial_sum_of(src, c, at, values):
    sub = lax.broadcasted_iota(jnp.int32, (8, 128), 0)
    sums = []
    for t in range(TILES):
        first, last = t == 0, t == TILES - 1
        below = jnp.where(sub == 0, values[t], pltpu.roll(values[t], 1, 0)) if first else src[c, at, 8 * t - 1 : 8 * t + 7, :]
        above = jnp.where(sub == 7, values[t], pltpu.roll(values[t], 7, 0)) if last else src[c, at, 8 * t + 1 : 8 * t + 9, :]
        sums.append(below + above)
    return sums


def strip_levels(strips, low_corner, high_corner, mix, edge, tiles):
    lane = lanes()
    wall_only = len(tiles) == 1
    from_low = (lane >= 2) & (lane < 6)
    from_high = (lane >= 38) & (lane < 42)
    held = {}
    for key in STRIPS:
        held[key] = [strips[STRIP_AT[key], rows(t), :] for t in tiles]
    for i, key in enumerate(CORNERS if low_corner else ()):
        for n in range(len(tiles)):
            value = jnp.where(from_low, pltpu.roll(low_corner[n], (2 - 4 * i) % 128, 1), held[key][n])
            held[key][n] = jnp.where(from_high, pltpu.roll(high_corner[n], (38 - 4 * i) % 128, 1), value)
    for step in range(ITERS):
        for c in range(COMP):
            for n in range(len(tiles)):
                edge[step, c, rows(n), :] = held[c, 1][n]
        if step == ITERS - 1:
            break
        later = {}
        for k in (2, 1, 0) if step == 0 else (1,):
            for c in range(COMP):
                radial = radial_sum(held[c, k], wall_only)
                later[c, k] = []
                for n in range(len(tiles)):
                    value = held[c, k][n]
                    around = held[c, k + 1][n] + held[c, k - 1][n]
                    around = around + pltpu.roll(value, 2, 1) + pltpu.roll(value, 126, 1) + radial[n]
                    later[c, k].append(updated(c, [held[d, k][n] for d in range(COMP)], around, held[COMP, k][n], mix))
        for key in [key for key in held if key[0] == COMP]:
            later[key] = held[key]
        held = later


def plane(src, kappa, edge, step, at, x, mix, count, comps):
    lane = lanes()
    first, last = lane == 0, lane == 127
    shift = 121 - 2 * x
    values = [[src[c, at, rows(t), :] for t in range(count)] for c in range(COMP)]
    kap = [kappa[at, rows(t), :] for t in range(count)]
    out = {}
    for c in comps:
        radial = radial_sum(values[c], True) if count == 1 else radial_sum_of(src, c, at, values[c])
        for t in range(count):
            value = values[c][t]
            beyond = pltpu.roll(edge[step, c, rows(t), :], shift, 1)
            around = src[c, at - 1, rows(t), :] + src[c, at + 1, rows(t), :] + radial[t]
            around = around + jnp.where(first, beyond, pltpu.roll(value, 1, 1))
            around = around + jnp.where(last, beyond, pltpu.roll(value, 127, 1))
            out[c, t] = updated(c, [values[d][t] for d in range(COMP)], around, kap[t], mix)
    return out


def wall_kernel(gas, kappa, strips, recv_wall, recv_a, reaction, _, wall, now, later, kap, edge):
    odd = lax.rem(lax.axis_index("sect"), 2)
    even = odd == 0
    mix = coupling(reaction)
    top = slice(GR - 8, GR)
    at_a, at_b = jnp.where(even, GX + 3, 0), jnp.where(even, 0, GX + 3)
    kappa_a, kappa_b = jnp.where(even, GX + 3, 1), jnp.where(even, 1, GX + 3)
    for c in range(COMP):
        for x in range(GX):
            now[c, x + 3] = gas[c, x, top, :]
        for layer in range(3):
            now[c, at_a + layer] = recv_a[3 * c + layer, top, :]
            now[c, at_b + layer] = recv_wall[2 * (3 * c + layer) + 1]
    for x in range(GX):
        kap[x + 3] = kappa[x, top, :]
    for layer in range(2):
        kap[kappa_a + layer] = recv_a[3 * COMP + layer, top, :]
        kap[kappa_b + layer] = recv_wall[2 * (3 * COMP + layer) + 1]
    corner_a, corner_b = recv_a[LAYERS - 1, top, :], recv_wall[2 * (LAYERS - 1) + TILES - 1]
    low, high = jnp.where(even, corner_b, corner_a), jnp.where(even, corner_a, corner_b)
    strip_levels(strips, [low], [high], mix, edge, [TILES - 1])

    for step, (src, dst) in enumerate(((now, later), (later, now), (now, None))):
        comps = (0,) if step == ITERS - 1 else range(COMP)
        for at in range(step + 1, EXT - 1 - step):
            out = plane(src, kap, edge, step, at, at - 3, mix, 1, comps)
            if step == ITERS - 1:
                wall[at - 3 : at - 2, :] = out[0, 0][7:8, :]
                continue
            for c in comps:
                dst[c, at] = out[c, 0]


def inner_kernel(gas, kappa, strips, reaction, first, second, middle, one, two, edge):
    mix = coupling(reaction)
    strip_levels(strips, None, None, mix, edge, list(range(TILES)))
    for step, (src, dst) in enumerate(((gas, one), (one, two), (two, middle))):

        def body(x, carry, step=step, src=src, dst=dst):
            out = plane(src, kappa, edge, step, x, x, mix, TILES, range(COMP))
            into = x - 3 if step == ITERS - 1 else x
            for (c, t), value in out.items():
                dst[c, into, rows(t), :] = value
            return carry

        lax.fori_loop(step + 1, GX - 1 - step, body, 0, unroll=2)
    for c in range(COMP):
        for i, x in enumerate(SEAM):
            first[c, i] = one[c, x]
            second[c, i] = two[c, x + 1 if i < 2 else x - 1]


def outer_kernel(
    _, gas, kappa, strips, first, second, middle, recv_wall, recv_a, recv_rest, reaction, result, token, now, later, kap, edge
):
    token[...] = jnp.zeros((8, 128), jnp.float32)
    even = lax.rem(lax.axis_index("sect"), 2) == 0
    mix = coupling(reaction)
    split = GR // 2
    at_a, at_b = jnp.where(even, GX + 3, 0), jnp.where(even, 0, GX + 3)
    kappa_a, kappa_b = jnp.where(even, GX + 3, 1), jnp.where(even, 1, GX + 3)
    for c in range(COMP):
        for x in (0, 1, GX - 2, GX - 1):
            now[c, x + 3] = gas[c, x]
        for layer in range(3):
            now[c, at_a + layer] = recv_a[3 * c + layer]
            for half in range(2):
                now[c, at_b + layer, rows(2 + half), :] = recv_wall[2 * (3 * c + layer) + half]
            now[c, at_b + layer, :split, :] = recv_rest[3 * c + layer]
        for i, x in enumerate(SEAM):
            later[c, x + 3] = first[c, i]
    for x in (0, 1, 2, GX - 3, GX - 2, GX - 1):
        kap[x + 3] = kappa[x]
    for layer in range(2):
        kap[kappa_a + layer] = recv_a[3 * COMP + layer]
        for half in range(2):
            kap[kappa_b + layer, rows(2 + half), :] = recv_wall[2 * (3 * COMP + layer) + half]
        kap[kappa_b + layer, :split, :] = recv_rest[3 * COMP + layer]
    low, high = [], []
    for t in range(TILES):
        corner_a = recv_a[LAYERS - 1, rows(t), :]
        corner_b = recv_wall[2 * (LAYERS - 1) + t]
        low.append(jnp.where(even, corner_b, corner_a))
        high.append(jnp.where(even, corner_a, corner_b))
    strip_levels(strips, low, high, mix, edge, list(range(TILES)))
    for c in range(COMP):
        result[c, 3 : GX - 3] = middle[c]
    for step, (src, dst) in enumerate(((now, later), (later, now), (now, None))):
        if step == ITERS - 1:
            for c in range(COMP):
                for i, x in enumerate(SEAM):
                    now[c, (x + 1 if i < 2 else x - 1) + 3] = second[c, i]
        for i in range(3):
            for at in (step + 1 + i, GX + 2 - step + i):
                out = plane(src, kap, edge, step, at, at - 3, mix, TILES, range(COMP))
                for (c, t), value in out.items():
                    if step == ITERS - 1:
                        result[c, at - 3, rows(t), :] = value
                    else:
                        dst[c, at, rows(t), :] = value


def pack_kernel(hop, cell, particles, mixing, heating, _, packed, cells, spread, ordered, source, begin, end):
    lane = lanes()
    square = (128, 128)
    down, across = lax.broadcasted_iota(jnp.int32, square, 0), lanes(square)
    moves = hop[...]
    named = [moves == j for j in range(MOVES)]
    table = jnp.concatenate(
        [jnp.where(m, 1.0, 0.0) for m in named] + [jnp.zeros((128 - MOVES * CHUNKS, 128), jnp.float32)], axis=0
    )
    running = jnp.dot(table, jnp.where(down <= across, 1.0, 0.0), preferred_element_type=jnp.float32)
    count = jnp.dot(table, jnp.ones(square, jnp.float32), preferred_element_type=jnp.float32)
    before = jnp.where(((down >> 4) == (across >> 4)) & (across < down), 1.0, 0.0)
    base = jnp.dot(before, count, preferred_element_type=jnp.float32)
    offset = jnp.zeros((CHUNKS, 128), jnp.float32)
    place = jnp.zeros((CHUNKS, 128), jnp.float32)
    across16 = lanes((CHUNKS, 128))
    for j in range(MOVES):
        part = slice(CHUNKS * j, CHUNKS * (j + 1))
        place = jnp.where(named[j], offset + running[part] - 1.0, place)
        first = base[part].astype(jnp.int32)
        source[part, :] = (across16 + offset.astype(jnp.int32) - first) & 127
        begin[part, :] = across16 - first
        end[part, :] = across16 - first - count[part].astype(jnp.int32)
        offset = offset + count[part]
    own = lax.broadcasted_iota(jnp.int32, (VALS, VALS), 0) == lax.broadcasted_iota(jnp.int32, (VALS, VALS), 1)
    weights = 0.5 * mixing[...] + jnp.where(own, 1.0, 0.0)
    first_value = lax.broadcasted_iota(jnp.int32, (VALS, VALS), 1) == 0
    weights = weights - jnp.where(first_value, heating[...], 0.0)
    for v in range(VALS):
        spread[v] = jnp.broadcast_to(weights[:, v : v + 1], (VALS, 128))
    place = place.astype(jnp.int32)
    position = lane.astype(jnp.float32)
    for chunk in range(CHUNKS):
        part = slice(128 * chunk, 128 * (chunk + 1))
        total = spread[0] * particles[0:1, part]
        for v in range(1, VALS):
            total = total + spread[v] * particles[v : v + 1, part]
        hot = jnp.where(down == place[chunk : chunk + 1, :], 1.0, 0.0)
        order = lax.dot_general(position, hot, (((1,), (1,)), ((), ())), preferred_element_type=jnp.float32)
        order = order.astype(jnp.int32)
        ordered[chunk, 0:8, :] = pick(total[0:8], order)
        ordered[chunk, 8:16, :] = pick(total[8:16], order)
        ordered[chunk, 16:24, :] = pick(
            jnp.broadcast_to(cell[chunk : chunk + 1, :], (8, 128)).astype(jnp.float32), order
        )

    def block(j, carry):
        held = [[jnp.zeros((8, 128), jnp.float32)] * 2 + [jnp.full((8, 128), -1.0)] for _ in range(SPOTS)]
        for chunk in range(CHUNKS):
            row = pl.ds(CHUNKS * j + chunk, 1)
            index = jnp.broadcast_to(source[row, :], (8, 128))
            parts = [pick(ordered[chunk, rows(n), :], index) for n in range(3)]
            start = jnp.broadcast_to(begin[row, :], (8, 128))
            stop = jnp.broadcast_to(end[row, :], (8, 128))
            for spot in range(SPOTS):
                here = (start >= -128 * spot) & (stop < -128 * spot)
                held[spot] = [jnp.where(here, new, old) for new, old in zip(parts, held[spot])]
        for spot in range(SPOTS):
            part = slice(128 * spot, 128 * (spot + 1))
            packed[j, 0:8, part] = held[spot][0]
            packed[j, 8:16, part] = held[spot][1]
            cells[j, spot : spot + 1, :] = held[spot][2][0:1, :].astype(jnp.int32)
        return carry

    lax.fori_loop(0, MOVES, block, 0)


def moves_of_swaps():
    tile = lax.axis_index("blk")
    odd, late = lax.rem(tile, 2), lax.rem(tile, 4) >> 1
    return [REACH - 1 + 2 * odd, 2 * REACH * late, 2 * REACH * (1 - late), REACH + 1 - 2 * odd]


def heat_kernel(wall, earlier, packed, cells, heating, own, send_q, send_s, send_r, send_p, look):
    flux = 0.5 * (wall[...] + earlier[...])
    heat = jnp.broadcast_to(heating[...], (VALS, 128))
    for j in range(MOVES):
        where_to = cells[j]
        row, column = where_to >> 7, where_to & 127
        found = jnp.zeros((8, 128), jnp.float32)
        for x in range(GX):
            line = jnp.broadcast_to(flux[x : x + 1, :], (8, 128))
            found = jnp.where(row == x, pick(line, column), found)
        look[j] = found
    for out, j in zip((own, send_q, send_s, send_r, send_p), [REACH] + moves_of_swaps()):
        for spot in range(SPOTS):
            part = slice(128 * spot, 128 * (spot + 1))
            out[:, part] = packed[j, :, part] + heat * look[j, spot : spot + 1, :]


def join_kernel(own, recv_q, recv_s, recv_r, recv_p, _, out, done):
    copies = []
    for n, (piece, j) in enumerate(zip((own, recv_q, recv_s, recv_r, recv_p), [REACH] + moves_of_swaps())):
        place = pl.multiple_of((2 * REACH - j) * CAP, CAP)
        copies.append(pltpu.make_async_copy(piece, out.at[:, pl.ds(place, CAP)], done.at[n]))
    for copy in copies:
        copy.start()
    for copy in copies:
        copy.wait()


def swap(x, axis, pairs):
    return lax.ppermute(x, axis, pairs + [(j, i) for i, j in pairs])


def local(gas, kappa, reaction, particles, mixing, heating, wall_cell, tile_hop):
    sections, tiles = lax.axis_size("sect"), lax.axis_size("blk")
    pairs_a = [(i, i + 1) for i in range(0, sections, 2)]
    pairs_b = [(i, i + 1) for i in range(1, sections - 1, 2)]
    pairs_q = [(i, (i + 1) % tiles) for i in range(1, tiles, 2)]
    pairs_p = [(i, i + 1) for i in range(0, tiles, 2)]
    pairs_s = [(i, (i + 2) % tiles) for i in range(tiles) if i % 4 >= 2]
    pairs_r = [(i, i + 2) for i in range(tiles) if i % 4 < 2]

    send_q, send_p = call(
        edges_kernel,
        (f32(3, GR, GA), f32(3, GR, GA)),
        scratch=[pltpu.VMEM((COMP + 1, GX, GR, GA), jnp.float32), pltpu.SemaphoreType.DMA((COMP + 1,))],
        specs=[HBM] * 2,
        moved=2 << 20,
        limit=53.75,
    )(gas, kappa)
    recv_q = swap(send_q, "blk", pairs_q)
    recv_p = swap(send_p, "blk", pairs_p)
    heating_column = heating.reshape(VALS, 1)
    packed, cells = call(
        pack_kernel,
        (f32(MOVES, VALS, CAP), i32(MOVES, SPOTS, 128)),
        scratch=[
            pltpu.VMEM((VALS, VALS, 128), jnp.float32),
            pltpu.VMEM((CHUNKS, 24, 128), jnp.float32),
            pltpu.VMEM((MOVES * CHUNKS, 128), jnp.int32),
            pltpu.VMEM((MOVES * CHUNKS, 128), jnp.int32),
            pltpu.VMEM((MOVES * CHUNKS, 128), jnp.int32),
        ],
        specs=[VMEM] * 5 + [ANY],
        moved=4 << 20,
    )(tile_hop.reshape(CHUNKS, 128), wall_cell.reshape(CHUNKS, 128), particles, mixing, heating_column, send_p)

    strips, send_a, send_wall = call(
        strips_kernel,
        (f32(len(STRIPS), GR, GA), f32(LAYERS, GR, GA), f32(2 * (LAYERS - 1) + TILES, 8, GA)),
        specs=[VMEM] * 6 + [ANY],
        moved=2 << 20,
    )(gas, kappa, send_q, send_p, recv_q, recv_p, cells)
    recv_wall = swap(send_wall, "sect", pairs_b)
    recv_a = swap(send_a, "sect", pairs_a)

    whole = f32(COMP, GX, GR, GA)
    first, second, middle = call(
        inner_kernel,
        (f32(COMP, len(SEAM), GR, GA), f32(COMP, len(SEAM), GR, GA), f32(COMP, GX - 6, GR, GA)),
        scratch=[
            pltpu.VMEM((COMP, GX, GR, GA), jnp.float32),
            pltpu.VMEM((COMP, GX, GR, GA), jnp.float32),
            pltpu.VMEM((ITERS, COMP, GR, GA), jnp.float32),
        ],
        specs=[VMEM] * 3 + [SMEM],
        moved=12 << 20,
    )(gas, kappa, strips, reaction)

    send_rest = call(rest_kernel, f32(LAYERS - 1, GR // 2, GA), specs=[VMEM] * 2 + [ANY], moved=1 << 18)(gas, kappa, middle)
    recv_rest = swap(send_rest, "sect", pairs_b)

    wall = call(
        wall_kernel,
        f32(GX, GA),
        scratch=[
            pltpu.VMEM((COMP, EXT, 8, GA), jnp.float32),
            pltpu.VMEM((COMP, EXT, 8, GA), jnp.float32),
            pltpu.VMEM((EXT, 8, GA), jnp.float32),
            pltpu.VMEM((ITERS, COMP, 8, GA), jnp.float32),
        ],
        specs=[VMEM] * 5 + [SMEM, ANY],
        moved=4 << 20,
    )(gas, kappa, strips, recv_wall, recv_a, reaction, send_rest)
    earlier = lax.ppermute(wall, "sect", [(i, i + 1) for i in range(sections - 1)])

    own, *sends = call(
        heat_kernel,
        (f32(VALS, CAP),) * MOVES,
        scratch=[pltpu.VMEM((MOVES, SPOTS, 128), jnp.float32)],
        specs=[VMEM] * 5,
        moved=2 << 20,
    )(wall, earlier, packed, cells, heating_column)
    pieces = [swap(x, "blk", pairs) for x, pairs in zip(sends, (pairs_q, pairs_s, pairs_r, pairs_p))]

    field, token = call(
        outer_kernel,
        (whole, f32(8, 128)),
        scratch=[
            pltpu.VMEM((COMP, EXT, GR, GA), jnp.float32),
            pltpu.VMEM((COMP, EXT, GR, GA), jnp.float32),
            pltpu.VMEM((EXT, GR, GA), jnp.float32),
            pltpu.VMEM((ITERS, COMP, GR, GA), jnp.float32),
        ],
        specs=[ANY] + [VMEM] * 9 + [SMEM],
        moved=8 << 20,
    )(pieces[0], gas, kappa, strips, first, second, middle, recv_wall, recv_a, recv_rest, reaction)
    arrived = call(
        join_kernel,
        f32(VALS, MOVES * CAP),
        scratch=[pltpu.SemaphoreType.DMA((MOVES,))],
        specs=[VMEM] * MOVES + [ANY],
        out_specs=HBM,
        moved=1 << 20,
    )(own, *pieces, token)
    return field, arrived


def solution(mesh):
    in_specs = (
        P(None, "sect", None, "blk"),
        P("sect", None, "blk"),
        P(),
        P(None, ("sect", "blk")),
        P(),
        P(),
        P(("sect", "blk")),
        P(("sect", "blk"), None),
    )
    out_specs = (P(None, "sect", None, "blk"), P(None, ("sect", "blk")))
    return jax.shard_map(local, mesh=mesh, in_specs=in_specs, out_specs=out_specs, check_vma=False)
```

```python
import jax
import jax.numpy as jnp
from jax import lax
from jax.experimental import pallas as pl
from jax.experimental.pallas import tpu as pltpu
from jax.sharding import PartitionSpec as P

REACH = 2
MOVES = 2 * REACH + 1
ITERS = 3
DIFFUSE = (1.0, 0.8, 0.6, 0.9, 0.7)
COMP = 5
GX = 16
GR = 32
GA = 128
TILES = GR // 8
EXT = GX + 2 * ITERS
CHUNKS = 16
VALS = 16
CAP = 1024
SPOTS = CAP // 128

FIELD_COLUMNS = (3, 2, 1, 0, -1)
KAPPA_COLUMNS = (2, 1, 0)
STRIPS = [(c, k) for c in range(COMP) for k in FIELD_COLUMNS] + [(COMP, k) for k in KAPPA_COLUMNS]
STRIP_AT = {key: i for i, key in enumerate(STRIPS)}
CORNERS = [(c, 1) for c in range(COMP)] + [(c, 2) for c in range(COMP)] + [(COMP, 1)] + [(c, 0) for c in range(COMP)]
LAYERS = 3 * COMP + 2 + 1
SEAM = (1, 2, GX - 3, GX - 2)

VMEM = pl.BlockSpec(memory_space=pltpu.VMEM)
SMEM = pl.BlockSpec(memory_space=pltpu.SMEM)
ANY = pl.BlockSpec(memory_space=pl.ANY)
HBM = pl.BlockSpec(memory_space=pltpu.HBM)


def f32(*shape):
    return jax.ShapeDtypeStruct(shape, jnp.float32)


def i32(*shape):
    return jax.ShapeDtypeStruct(shape, jnp.int32)


def lanes(shape=(8, 128)):
    return lax.broadcasted_iota(jnp.int32, shape, len(shape) - 1)


def pick(x, index):
    return jnp.take_along_axis(x, index, axis=1, mode="promise_in_bounds")


def rows(tile):
    return slice(8 * tile, 8 * tile + 8)


def call(kernel, outs, scratch=(), specs=None, out_specs=None, flops=0, moved=0, limit=16):
    return pl.pallas_call(
        kernel,
        out_shape=outs,
        in_specs=specs,
        out_specs=jax.tree.map(lambda _: VMEM, outs) if out_specs is None else out_specs,
        scratch_shapes=list(scratch),
        cost_estimate=pl.CostEstimate(flops=flops, bytes_accessed=moved, transcendentals=0),
        compiler_params=pltpu.CompilerParams(vmem_limit_bytes=int(limit * 2**20)),
    )


def edges_kernel(gas, kappa, send_q, send_p, held, arrived):
    copies = [pltpu.make_async_copy(gas.at[q], held.at[q], arrived.at[q]) for q in range(COMP)]
    copies.append(pltpu.make_async_copy(kappa, held.at[COMP], arrived.at[COMP]))
    for copy in copies:
        copy.start()
    lane = lanes()
    within = lane & 63
    depth, cell = within >> 4, within & 15
    high = jnp.maximum(6 * cell + 2 - depth, 0)
    low = 6 * cell + 3 + depth
    odd = lax.rem(lax.axis_index("blk"), 2) == 1
    index_q, index_p = jnp.where(odd, high, low), jnp.where(odd, low, high)
    for pair in range((COMP + 1) // 2):
        packed = {}
        for q in (2 * pair, 2 * pair + 1):
            copies[q].wait()
            for tile in range(TILES):
                total = jnp.zeros((8, 128), jnp.float32)
                for x in range(GX):
                    here = (lane >= 6 * x) & (lane < 6 * x + 6)
                    total = jnp.where(here, pltpu.roll(held[q, x, rows(tile), :], 6 * x + 3, 1), total)
                packed[q, tile] = total
        for tile in range(TILES):
            first, second = packed[2 * pair, tile], packed[2 * pair + 1, tile]
            for out, index in ((send_q, index_q), (send_p, index_p)):
                out[pair, rows(tile), :] = jnp.where(lane < 64, pick(first, index), pick(second, index))


def strips_kernel(gas, kappa, send_q, send_p, recv_q, recv_p, strips, send_a, send_wall):
    lane = lanes()
    low_side = (lane & 1) == 1
    cell = jnp.clip((lane >> 1) - 3, 0, GX - 1)
    even = lax.rem(lax.axis_index("sect"), 2) == 0
    odd_tile = lax.rem(lax.axis_index("blk"), 2) == 1
    for tile in range(TILES):
        held = {}
        slabs = [[ref[s, rows(tile), :] for s in range(3)] for ref in (send_q, send_p, recv_q, recv_p)]
        own_q, own_p, got_q, got_p = slabs
        to_left = [jnp.where(odd_tile, p, q) for q, p in zip(own_q, own_p)]
        to_right = [jnp.where(odd_tile, q, p) for q, p in zip(own_q, own_p)]
        from_left = [jnp.where(odd_tile, p, q) for q, p in zip(got_q, got_p)]
        from_right = [jnp.where(odd_tile, q, p) for q, p in zip(got_q, got_p)]
        for q, k in STRIPS:
            depth = k - 1 if k > 0 else -k
            index = cell + ((q % 2) * 64 + depth * 16)
            low, high = (from_left, from_right) if k > 0 else (to_left, to_right)
            value = jnp.where(low_side, pick(low[q // 2], index), pick(high[q // 2], index))
            strips[STRIP_AT[q, k], rows(tile), :] = value
            held[q, k] = value
        top = jnp.zeros((8, 128), jnp.float32)
        bottom = top
        for i, key in enumerate(CORNERS):
            here = (lane >> 2) == i
            top = jnp.where(here, pltpu.roll(held[key], (4 * i - 34) % 128, 1), top)
            bottom = jnp.where(here, pltpu.roll(held[key], (4 * i - 6) % 128, 1), bottom)
        for_a = jnp.where(even, top, bottom)
        for_b = jnp.where(even, bottom, top)
        send_a[LAYERS - 1, rows(tile), :] = for_a
        send_wall[2 * (LAYERS - 1) + tile] = for_b
    at_a, at_b = jnp.where(even, GX - 3, 0), jnp.where(even, 0, GX - 3)
    kappa_a, kappa_b = jnp.where(even, GX - 2, 0), jnp.where(even, 0, GX - 2)
    for c in range(COMP):
        for layer in range(3):
            send_a[3 * c + layer] = gas[c, at_a + layer]
            for half in range(2):
                send_wall[2 * (3 * c + layer) + half] = gas[c, at_b + layer, rows(2 + half), :]
    for layer in range(2):
        send_a[3 * COMP + layer] = kappa[kappa_a + layer]
        for half in range(2):
            send_wall[2 * (3 * COMP + layer) + half] = kappa[kappa_b + layer, rows(2 + half), :]


def rest_kernel(gas, kappa, _, send_rest):
    even = lax.rem(lax.axis_index("sect"), 2) == 0
    split = GR // 2
    from_b, from_kappa = jnp.where(even, 0, GX - 3), jnp.where(even, 0, GX - 2)
    for c in range(COMP):
        for layer in range(3):
            send_rest[3 * c + layer] = gas[c, from_b + layer, :split, :]
    for layer in range(2):
        send_rest[3 * COMP + layer] = kappa[from_kappa + layer, :split, :]


def coupling(reaction):
    return [[0.3 * reaction[c, d] + (1.0 if c == d else 0.0) for d in range(COMP)] for c in range(COMP)]


def updated(c, values, neighbours, kappa, mix):
    total = mix[c][0] * values[0]
    for d in range(1, COMP):
        total = total + mix[c][d] * values[d]
    rate = kappa if DIFFUSE[c] == 1.0 else DIFFUSE[c] * kappa
    return total + rate * (neighbours - 6.0 * values[c])


def radial_sum(tiles, wall_only):
    sub = lax.broadcasted_iota(jnp.int32, (8, 128), 0)
    down = [pltpu.roll(t, 1, 0) for t in tiles]
    up = [pltpu.roll(t, 7, 0) for t in tiles]
    last = len(tiles) - 1
    sums = []
    for i, t in enumerate(tiles):
        if wall_only:
            below = down[i]
        else:
            below = jnp.where(sub == 0, down[i - 1] if i > 0 else t, down[i])
        above = jnp.where(sub == 7, up[i + 1] if i < last else t, up[i])
        sums.append(below + above)
    return sums


def radial_sum_of(src, c, at, t, value):
    sub = lax.broadcasted_iota(jnp.int32, (8, 128), 0)
    if t == 0:
        below = jnp.where(sub == 0, value, pltpu.roll(value, 1, 0))
    else:
        below = src[c, at, 8 * t - 1 : 8 * t + 7, :]
    if t == TILES - 1:
        above = jnp.where(sub == 7, value, pltpu.roll(value, 7, 0))
    else:
        above = src[c, at, 8 * t + 1 : 8 * t + 9, :]
    return below + above


def strip_levels(strips, low_corner, high_corner, mix, edge, tiles):
    lane = lanes()
    wall_only = len(tiles) == 1
    from_low = (lane >= 2) & (lane < 6)
    from_high = (lane >= 38) & (lane < 42)
    held = {}
    for key in STRIPS:
        held[key] = [strips[STRIP_AT[key], rows(t), :] for t in tiles]
    for i, key in enumerate(CORNERS if low_corner else ()):
        for n in range(len(tiles)):
            value = jnp.where(from_low, pltpu.roll(low_corner[n], (2 - 4 * i) % 128, 1), held[key][n])
            held[key][n] = jnp.where(from_high, pltpu.roll(high_corner[n], (38 - 4 * i) % 128, 1), value)
    for step in range(ITERS):
        for c in range(COMP):
            for n in range(len(tiles)):
                edge[step, c, rows(n), :] = held[c, 1][n]
        if step == ITERS - 1:
            break
        later = {}
        for k in (2, 1, 0) if step == 0 else (1,):
            for c in range(COMP):
                radial = radial_sum(held[c, k], wall_only)
                later[c, k] = []
                for n in range(len(tiles)):
                    value = held[c, k][n]
                    around = held[c, k + 1][n] + held[c, k - 1][n]
                    around = around + pltpu.roll(value, 2, 1) + pltpu.roll(value, 126, 1) + radial[n]
                    later[c, k].append(updated(c, [held[d, k][n] for d in range(COMP)], around, held[COMP, k][n], mix))
        for key in [key for key in held if key[0] == COMP]:
            later[key] = held[key]
        held = later


def plane(src, kappa, edge, step, at, x, mix, count, comps):
    lane = lanes()
    first, last = lane == 0, lane == 127
    shift = 121 - 2 * x
    kap = [kappa[at, rows(t), :] for t in range(count)]
    out = {}
    for t in range(count):
        values = [src[c, at, rows(t), :] for c in range(COMP)]
        for c in comps:
            value = values[c]
            beyond = pltpu.roll(edge[step, c, rows(t), :], shift, 1)
            around = src[c, at - 1, rows(t), :] + src[c, at + 1, rows(t), :]
            around = around + (radial_sum([value], True)[0] if count == 1 else radial_sum_of(src, c, at, t, value))
            around = around + jnp.where(first, beyond, pltpu.roll(value, 1, 1))
            around = around + jnp.where(last, beyond, pltpu.roll(value, 127, 1))
            out[c, t] = updated(c, values, around, kap[t], mix)
    return out


def wall_kernel(gas, kappa, strips, recv_wall, recv_a, reaction, _, wall, now, later, kap, edge):
    odd = lax.rem(lax.axis_index("sect"), 2)
    even = odd == 0
    mix = coupling(reaction)
    top = slice(GR - 8, GR)
    at_a, at_b = jnp.where(even, GX + 3, 0), jnp.where(even, 0, GX + 3)
    kappa_a, kappa_b = jnp.where(even, GX + 3, 1), jnp.where(even, 1, GX + 3)
    for c in range(COMP):
        for x in range(GX):
            now[c, x + 3] = gas[c, x, top, :]
        for layer in range(3):
            now[c, at_a + layer] = recv_a[3 * c + layer, top, :]
            now[c, at_b + layer] = recv_wall[2 * (3 * c + layer) + 1]
    for x in range(GX):
        kap[x + 3] = kappa[x, top, :]
    for layer in range(2):
        kap[kappa_a + layer] = recv_a[3 * COMP + layer, top, :]
        kap[kappa_b + layer] = recv_wall[2 * (3 * COMP + layer) + 1]
    corner_a, corner_b = recv_a[LAYERS - 1, top, :], recv_wall[2 * (LAYERS - 1) + TILES - 1]
    low, high = jnp.where(even, corner_b, corner_a), jnp.where(even, corner_a, corner_b)
    strip_levels(strips, [low], [high], mix, edge, [TILES - 1])

    for step, (src, dst) in enumerate(((now, later), (later, now), (now, None))):
        comps = (0,) if step == ITERS - 1 else range(COMP)
        for at in range(step + 1, EXT - 1 - step):
            out = plane(src, kap, edge, step, at, at - 3, mix, 1, comps)
            if step == ITERS - 1:
                wall[at - 3 : at - 2, :] = out[0, 0][7:8, :]
                continue
            for c in comps:
                dst[c, at] = out[c, 0]


def inner_kernel(gas, kappa, strips, reaction, first, second, middle, one, two, edge):
    mix = coupling(reaction)
    strip_levels(strips, None, None, mix, edge, list(range(TILES)))
    for step, (src, dst) in enumerate(((gas, one), (one, two), (two, middle))):

        def body(x, carry, step=step, src=src, dst=dst):
            out = plane(src, kappa, edge, step, x, x, mix, TILES, range(COMP))
            into = x - 3 if step == ITERS - 1 else x
            for (c, t), value in out.items():
                dst[c, into, rows(t), :] = value
            return carry

        lax.fori_loop(step + 1, GX - 1 - step, body, 0, unroll=2)
    for c in range(COMP):
        for i, x in enumerate(SEAM):
            first[c, i] = one[c, x]
            second[c, i] = two[c, x + 1 if i < 2 else x - 1]


def outer_kernel(
    _, gas, kappa, strips, first, second, middle, recv_wall, recv_a, recv_rest, reaction, result, token, now, later, kap, edge
):
    token[...] = jnp.zeros((8, 128), jnp.float32)
    even = lax.rem(lax.axis_index("sect"), 2) == 0
    mix = coupling(reaction)
    split = GR // 2
    at_a, at_b = jnp.where(even, GX + 3, 0), jnp.where(even, 0, GX + 3)
    kappa_a, kappa_b = jnp.where(even, GX + 3, 1), jnp.where(even, 1, GX + 3)
    for c in range(COMP):
        for x in (0, 1, GX - 2, GX - 1):
            now[c, x + 3] = gas[c, x]
        for layer in range(3):
            now[c, at_a + layer] = recv_a[3 * c + layer]
            for half in range(2):
                now[c, at_b + layer, rows(2 + half), :] = recv_wall[2 * (3 * c + layer) + half]
            now[c, at_b + layer, :split, :] = recv_rest[3 * c + layer]
        for i, x in enumerate(SEAM):
            later[c, x + 3] = first[c, i]
    for x in (0, 1, 2, GX - 3, GX - 2, GX - 1):
        kap[x + 3] = kappa[x]
    for layer in range(2):
        kap[kappa_a + layer] = recv_a[3 * COMP + layer]
        for half in range(2):
            kap[kappa_b + layer, rows(2 + half), :] = recv_wall[2 * (3 * COMP + layer) + half]
        kap[kappa_b + layer, :split, :] = recv_rest[3 * COMP + layer]
    low, high = [], []
    for t in range(TILES):
        corner_a = recv_a[LAYERS - 1, rows(t), :]
        corner_b = recv_wall[2 * (LAYERS - 1) + t]
        low.append(jnp.where(even, corner_b, corner_a))
        high.append(jnp.where(even, corner_a, corner_b))
    strip_levels(strips, low, high, mix, edge, list(range(TILES)))
    for c in range(COMP):
        result[c, 3 : GX - 3] = middle[c]
    for step, (src, dst) in enumerate(((now, later), (later, now), (now, None))):
        if step == ITERS - 1:
            for c in range(COMP):
                for i, x in enumerate(SEAM):
                    now[c, (x + 1 if i < 2 else x - 1) + 3] = second[c, i]
        for i in range(3):
            for at in (step + 1 + i, GX + 2 - step + i):
                out = plane(src, kap, edge, step, at, at - 3, mix, TILES, range(COMP))
                for (c, t), value in out.items():
                    if step == ITERS - 1:
                        result[c, at - 3, rows(t), :] = value
                    else:
                        dst[c, at, rows(t), :] = value


def pack_kernel(hop, cell, particles, mixing, heating, _, packed, cells, spread, ordered, source, begin, end):
    lane = lanes()
    square = (128, 128)
    down, across = lax.broadcasted_iota(jnp.int32, square, 0), lanes(square)
    moves = hop[...]
    named = [moves == j for j in range(MOVES)]
    table = jnp.concatenate(
        [jnp.where(m, 1.0, 0.0) for m in named] + [jnp.zeros((128 - MOVES * CHUNKS, 128), jnp.float32)], axis=0
    )
    running = jnp.dot(table, jnp.where(down <= across, 1.0, 0.0), preferred_element_type=jnp.float32)
    count = jnp.dot(table, jnp.ones(square, jnp.float32), preferred_element_type=jnp.float32)
    before = jnp.where(((down >> 4) == (across >> 4)) & (across < down), 1.0, 0.0)
    base = jnp.dot(before, count, preferred_element_type=jnp.float32)
    offset = jnp.zeros((CHUNKS, 128), jnp.float32)
    place = jnp.zeros((CHUNKS, 128), jnp.float32)
    across16 = lanes((CHUNKS, 128))
    for j in range(MOVES):
        part = slice(CHUNKS * j, CHUNKS * (j + 1))
        place = jnp.where(named[j], offset + running[part] - 1.0, place)
        first = base[part].astype(jnp.int32)
        source[part, :] = (across16 + offset.astype(jnp.int32) - first) & 127
        begin[part, :] = across16 - first
        end[part, :] = across16 - first - count[part].astype(jnp.int32)
        offset = offset + count[part]
    own = lax.broadcasted_iota(jnp.int32, (VALS, VALS), 0) == lax.broadcasted_iota(jnp.int32, (VALS, VALS), 1)
    weights = 0.5 * mixing[...] + jnp.where(own, 1.0, 0.0)
    first_value = lax.broadcasted_iota(jnp.int32, (VALS, VALS), 1) == 0
    weights = weights - jnp.where(first_value, heating[...], 0.0)
    for v in range(VALS):
        spread[v] = jnp.broadcast_to(weights[:, v : v + 1], (VALS, 128))
    place = place.astype(jnp.int32)
    position = lane.astype(jnp.float32)
    for chunk in range(CHUNKS):
        part = slice(128 * chunk, 128 * (chunk + 1))
        total = spread[0] * particles[0:1, part]
        for v in range(1, VALS):
            total = total + spread[v] * particles[v : v + 1, part]
        hot = jnp.where(down == place[chunk : chunk + 1, :], 1.0, 0.0)
        order = lax.dot_general(position, hot, (((1,), (1,)), ((), ())), preferred_element_type=jnp.float32)
        order = order.astype(jnp.int32)
        ordered[chunk, 0:8, :] = pick(total[0:8], order)
        ordered[chunk, 8:16, :] = pick(total[8:16], order)
        ordered[chunk, 16:24, :] = pick(
            jnp.broadcast_to(cell[chunk : chunk + 1, :], (8, 128)).astype(jnp.float32), order
        )

    def block(j, carry):
        held = [[jnp.zeros((8, 128), jnp.float32)] * 2 + [jnp.full((8, 128), -1.0)] for _ in range(SPOTS)]
        for chunk in range(CHUNKS):
            row = pl.ds(CHUNKS * j + chunk, 1)
            index = jnp.broadcast_to(source[row, :], (8, 128))
            parts = [pick(ordered[chunk, rows(n), :], index) for n in range(3)]
            start = jnp.broadcast_to(begin[row, :], (8, 128))
            stop = jnp.broadcast_to(end[row, :], (8, 128))
            for spot in range(SPOTS):
                here = (start >= -128 * spot) & (stop < -128 * spot)
                held[spot] = [jnp.where(here, new, old) for new, old in zip(parts, held[spot])]
        for spot in range(SPOTS):
            part = slice(128 * spot, 128 * (spot + 1))
            packed[j, 0:8, part] = held[spot][0]
            packed[j, 8:16, part] = held[spot][1]
            cells[j, spot : spot + 1, :] = held[spot][2][0:1, :].astype(jnp.int32)
        return carry

    lax.fori_loop(0, MOVES, block, 0)


def moves_of_swaps():
    tile = lax.axis_index("blk")
    odd, late = lax.rem(tile, 2), lax.rem(tile, 4) >> 1
    return [REACH - 1 + 2 * odd, 2 * REACH * late, 2 * REACH * (1 - late), REACH + 1 - 2 * odd]


def heat_kernel(wall, earlier, packed, cells, heating, own, send_q, send_s, send_r, send_p, look):
    flux = 0.5 * (wall[...] + earlier[...])
    heat = jnp.broadcast_to(heating[...], (VALS, 128))
    for j in range(MOVES):
        where_to = cells[j]
        row, column = where_to >> 7, where_to & 127
        found = jnp.zeros((8, 128), jnp.float32)
        for x in range(GX):
            line = jnp.broadcast_to(flux[x : x + 1, :], (8, 128))
            found = jnp.where(row == x, pick(line, column), found)
        look[j] = found
    for out, j in zip((own, send_q, send_s, send_r, send_p), [REACH] + moves_of_swaps()):
        for spot in range(SPOTS):
            part = slice(128 * spot, 128 * (spot + 1))
            out[:, part] = packed[j, :, part] + heat * look[j, spot : spot + 1, :]


def join_kernel(own, recv_q, recv_s, recv_r, recv_p, _, out, done):
    copies = []
    for n, (piece, j) in enumerate(zip((own, recv_q, recv_s, recv_r, recv_p), [REACH] + moves_of_swaps())):
        place = pl.multiple_of((2 * REACH - j) * CAP, CAP)
        copies.append(pltpu.make_async_copy(piece, out.at[:, pl.ds(place, CAP)], done.at[n]))
    for copy in copies:
        copy.start()
    for copy in copies:
        copy.wait()


def swap(x, axis, pairs):
    return lax.ppermute(x, axis, pairs + [(j, i) for i, j in pairs])


def local(gas, kappa, reaction, particles, mixing, heating, wall_cell, tile_hop):
    sections, tiles = lax.axis_size("sect"), lax.axis_size("blk")
    pairs_a = [(i, i + 1) for i in range(0, sections, 2)]
    pairs_b = [(i, i + 1) for i in range(1, sections - 1, 2)]
    pairs_q = [(i, (i + 1) % tiles) for i in range(1, tiles, 2)]
    pairs_p = [(i, i + 1) for i in range(0, tiles, 2)]
    pairs_s = [(i, (i + 2) % tiles) for i in range(tiles) if i % 4 >= 2]
    pairs_r = [(i, i + 2) for i in range(tiles) if i % 4 < 2]

    send_q, send_p = call(
        edges_kernel,
        (f32(3, GR, GA), f32(3, GR, GA)),
        scratch=[pltpu.VMEM((COMP + 1, GX, GR, GA), jnp.float32), pltpu.SemaphoreType.DMA((COMP + 1,))],
        specs=[HBM] * 2,
        moved=2 << 20,
        limit=53.75,
    )(gas, kappa)
    recv_q = swap(send_q, "blk", pairs_q)
    recv_p = swap(send_p, "blk", pairs_p)
    strips, send_a, send_wall = call(
        strips_kernel,
        (f32(len(STRIPS), GR, GA), f32(LAYERS, GR, GA), f32(2 * (LAYERS - 1) + TILES, 8, GA)),
        specs=[VMEM] * 6,
        moved=2 << 20,
    )(gas, kappa, send_q, send_p, recv_q, recv_p)
    recv_wall = swap(send_wall, "sect", pairs_b)
    recv_a = swap(send_a, "sect", pairs_a)

    whole = f32(COMP, GX, GR, GA)
    first, second, middle = call(
        inner_kernel,
        (f32(COMP, len(SEAM), GR, GA), f32(COMP, len(SEAM), GR, GA), f32(COMP, GX - 6, GR, GA)),
        scratch=[
            pltpu.VMEM((COMP, GX, GR, GA), jnp.float32),
            pltpu.VMEM((COMP, GX, GR, GA), jnp.float32),
            pltpu.VMEM((ITERS, COMP, GR, GA), jnp.float32),
        ],
        specs=[VMEM] * 3 + [SMEM],
        moved=12 << 20,
    )(gas, kappa, strips, reaction)

    send_rest = call(rest_kernel, f32(LAYERS - 1, GR // 2, GA), specs=[VMEM] * 2 + [ANY], moved=1 << 18)(gas, kappa, middle)
    recv_rest = swap(send_rest, "sect", pairs_b)

    wall = call(
        wall_kernel,
        f32(GX, GA),
        scratch=[
            pltpu.VMEM((COMP, EXT, 8, GA), jnp.float32),
            pltpu.VMEM((COMP, EXT, 8, GA), jnp.float32),
            pltpu.VMEM((EXT, 8, GA), jnp.float32),
            pltpu.VMEM((ITERS, COMP, 8, GA), jnp.float32),
        ],
        specs=[VMEM] * 5 + [SMEM, ANY],
        moved=4 << 20,
    )(gas, kappa, strips, recv_wall, recv_a, reaction, send_rest)
    earlier = lax.ppermute(wall, "sect", [(i, i + 1) for i in range(sections - 1)])

    heating_column = heating.reshape(VALS, 1)
    packed, cells = call(
        pack_kernel,
        (f32(MOVES, VALS, CAP), i32(MOVES, SPOTS, 128)),
        scratch=[
            pltpu.VMEM((VALS, VALS, 128), jnp.float32),
            pltpu.VMEM((CHUNKS, 24, 128), jnp.float32),
            pltpu.VMEM((MOVES * CHUNKS, 128), jnp.int32),
            pltpu.VMEM((MOVES * CHUNKS, 128), jnp.int32),
            pltpu.VMEM((MOVES * CHUNKS, 128), jnp.int32),
        ],
        specs=[VMEM] * 5 + [ANY],
        moved=4 << 20,
    )(tile_hop.reshape(CHUNKS, 128), wall_cell.reshape(CHUNKS, 128), particles, mixing, heating_column, wall)
    own, *sends = call(
        heat_kernel,
        (f32(VALS, CAP),) * MOVES,
        scratch=[pltpu.VMEM((MOVES, SPOTS, 128), jnp.float32)],
        specs=[VMEM] * 5,
        moved=2 << 20,
    )(wall, earlier, packed, cells, heating_column)
    pieces = [swap(x, "blk", pairs) for x, pairs in zip(sends, (pairs_q, pairs_s, pairs_r, pairs_p))]

    field, token = call(
        outer_kernel,
        (whole, f32(8, 128)),
        scratch=[
            pltpu.VMEM((COMP, EXT, GR, GA), jnp.float32),
            pltpu.VMEM((COMP, EXT, GR, GA), jnp.float32),
            pltpu.VMEM((EXT, GR, GA), jnp.float32),
            pltpu.VMEM((ITERS, COMP, GR, GA), jnp.float32),
        ],
        specs=[ANY] + [VMEM] * 9 + [SMEM],
        moved=8 << 20,
    )(pieces[0], gas, kappa, strips, first, second, middle, recv_wall, recv_a, recv_rest, reaction)
    arrived = call(
        join_kernel,
        f32(VALS, MOVES * CAP),
        scratch=[pltpu.SemaphoreType.DMA((MOVES,))],
        specs=[VMEM] * MOVES + [ANY],
        out_specs=HBM,
        moved=1 << 20,
    )(own, *pieces, token)
    return field, arrived


def solution(mesh):
    in_specs = (
        P(None, "sect", None, "blk"),
        P("sect", None, "blk"),
        P(),
        P(None, ("sect", "blk")),
        P(),
        P(),
        P(("sect", "blk")),
        P(("sect", "blk"), None),
    )
    out_specs = (P(None, "sect", None, "blk"), P(None, ("sect", "blk")))
    return jax.shard_map(local, mesh=mesh, in_specs=in_specs, out_specs=out_specs, check_vma=False)
```

```python
import jax
import jax.numpy as jnp
from jax import lax
from jax.experimental import pallas as pl
from jax.experimental.pallas import tpu as pltpu
from jax.sharding import PartitionSpec as P

REACH = 2
MOVES = 2 * REACH + 1
ITERS = 3
DIFFUSE = (1.0, 0.8, 0.6, 0.9, 0.7)
COMP = 5
GX = 16
GR = 32
GA = 128
TILES = GR // 8
EXT = GX + 2 * ITERS
CHUNKS = 16
VALS = 16
CAP = 1024
SPOTS = CAP // 128

FIELD_COLUMNS = (3, 2, 1, 0, -1)
KAPPA_COLUMNS = (2, 1, 0)
STRIPS = [(c, k) for c in range(COMP) for k in FIELD_COLUMNS] + [(COMP, k) for k in KAPPA_COLUMNS]
STRIP_AT = {key: i for i, key in enumerate(STRIPS)}
CORNERS = [(c, 1) for c in range(COMP)] + [(c, 2) for c in range(COMP)] + [(COMP, 1)] + [(c, 0) for c in range(COMP)]
LAYERS = 3 * COMP + 2 + 1
SEAM = (1, 2, GX - 3, GX - 2)

VMEM = pl.BlockSpec(memory_space=pltpu.VMEM)
SMEM = pl.BlockSpec(memory_space=pltpu.SMEM)
ANY = pl.BlockSpec(memory_space=pl.ANY)
HBM = pl.BlockSpec(memory_space=pltpu.HBM)


def f32(*shape):
    return jax.ShapeDtypeStruct(shape, jnp.float32)


def i32(*shape):
    return jax.ShapeDtypeStruct(shape, jnp.int32)


def lanes(shape=(8, 128)):
    return lax.broadcasted_iota(jnp.int32, shape, len(shape) - 1)


def pick(x, index):
    return jnp.take_along_axis(x, index, axis=1, mode="promise_in_bounds")


def rows(tile):
    return slice(8 * tile, 8 * tile + 8)


def call(kernel, outs, scratch=(), specs=None, out_specs=None, flops=0, moved=0, limit=16):
    return pl.pallas_call(
        kernel,
        out_shape=outs,
        in_specs=specs,
        out_specs=jax.tree.map(lambda _: VMEM, outs) if out_specs is None else out_specs,
        scratch_shapes=list(scratch),
        cost_estimate=pl.CostEstimate(flops=flops, bytes_accessed=moved, transcendentals=0),
        compiler_params=pltpu.CompilerParams(vmem_limit_bytes=int(limit * 2**20)),
    )


def edges_kernel(gas, kappa, send_q, send_p, held, arrived):
    copies = [pltpu.make_async_copy(gas.at[q], held.at[q], arrived.at[q]) for q in range(COMP)]
    copies.append(pltpu.make_async_copy(kappa, held.at[COMP], arrived.at[COMP]))
    for copy in copies:
        copy.start()
    lane = lanes()
    within = lane & 63
    depth, cell = within >> 4, within & 15
    high = jnp.maximum(6 * cell + 2 - depth, 0)
    low = 6 * cell + 3 + depth
    odd = lax.rem(lax.axis_index("blk"), 2) == 1
    index_q, index_p = jnp.where(odd, high, low), jnp.where(odd, low, high)
    for pair in range((COMP + 1) // 2):
        packed = {}
        for q in (2 * pair, 2 * pair + 1):
            copies[q].wait()
            for tile in range(TILES):
                total = jnp.zeros((8, 128), jnp.float32)
                for x in range(GX):
                    here = (lane >= 6 * x) & (lane < 6 * x + 6)
                    total = jnp.where(here, pltpu.roll(held[q, x, rows(tile), :], 6 * x + 3, 1), total)
                packed[q, tile] = total
        for tile in range(TILES):
            first, second = packed[2 * pair, tile], packed[2 * pair + 1, tile]
            for out, index in ((send_q, index_q), (send_p, index_p)):
                out[pair, rows(tile), :] = jnp.where(lane < 64, pick(first, index), pick(second, index))


def strips_kernel(gas, kappa, send_q, send_p, recv_q, recv_p, _, strips, send_a, send_wall):
    lane = lanes()
    low_side = (lane & 1) == 1
    cell = jnp.clip((lane >> 1) - 3, 0, GX - 1)
    even = lax.rem(lax.axis_index("sect"), 2) == 0
    odd_tile = lax.rem(lax.axis_index("blk"), 2) == 1
    for tile in range(TILES):
        held = {}
        slabs = [[ref[s, rows(tile), :] for s in range(3)] for ref in (send_q, send_p, recv_q, recv_p)]
        own_q, own_p, got_q, got_p = slabs
        to_left = [jnp.where(odd_tile, p, q) for q, p in zip(own_q, own_p)]
        to_right = [jnp.where(odd_tile, q, p) for q, p in zip(own_q, own_p)]
        from_left = [jnp.where(odd_tile, p, q) for q, p in zip(got_q, got_p)]
        from_right = [jnp.where(odd_tile, q, p) for q, p in zip(got_q, got_p)]
        for q, k in STRIPS:
            depth = k - 1 if k > 0 else -k
            index = cell + ((q % 2) * 64 + depth * 16)
            low, high = (from_left, from_right) if k > 0 else (to_left, to_right)
            value = jnp.where(low_side, pick(low[q // 2], index), pick(high[q // 2], index))
            strips[STRIP_AT[q, k], rows(tile), :] = value
            held[q, k] = value
        top = jnp.zeros((8, 128), jnp.float32)
        bottom = top
        for i, key in enumerate(CORNERS):
            here = (lane >> 2) == i
            top = jnp.where(here, pltpu.roll(held[key], (4 * i - 34) % 128, 1), top)
            bottom = jnp.where(here, pltpu.roll(held[key], (4 * i - 6) % 128, 1), bottom)
        for_a = jnp.where(even, top, bottom)
        for_b = jnp.where(even, bottom, top)
        send_a[LAYERS - 1, rows(tile), :] = for_a
        send_wall[2 * (LAYERS - 1) + tile] = for_b
    at_a, at_b = jnp.where(even, GX - 3, 0), jnp.where(even, 0, GX - 3)
    kappa_a, kappa_b = jnp.where(even, GX - 2, 0), jnp.where(even, 0, GX - 2)
    for c in range(COMP):
        for layer in range(3):
            send_a[3 * c + layer] = gas[c, at_a + layer]
            for half in range(2):
                send_wall[2 * (3 * c + layer) + half] = gas[c, at_b + layer, rows(2 + half), :]
    for layer in range(2):
        send_a[3 * COMP + layer] = kappa[kappa_a + layer]
        for half in range(2):
            send_wall[2 * (3 * COMP + layer) + half] = kappa[kappa_b + layer, rows(2 + half), :]


def rest_kernel(gas, kappa, _, send_rest):
    even = lax.rem(lax.axis_index("sect"), 2) == 0
    split = GR // 2
    from_b, from_kappa = jnp.where(even, 0, GX - 3), jnp.where(even, 0, GX - 2)
    for c in range(COMP):
        for layer in range(3):
            send_rest[3 * c + layer] = gas[c, from_b + layer, :split, :]
    for layer in range(2):
        send_rest[3 * COMP + layer] = kappa[from_kappa + layer, :split, :]


def coupling(reaction):
    return [[0.3 * reaction[c, d] + (1.0 if c == d else 0.0) for d in range(COMP)] for c in range(COMP)]


def updated(c, values, neighbours, kappa, mix):
    total = mix[c][0] * values[0]
    for d in range(1, COMP):
        total = total + mix[c][d] * values[d]
    rate = kappa if DIFFUSE[c] == 1.0 else DIFFUSE[c] * kappa
    return total + rate * (neighbours - 6.0 * values[c])


def radial_sum(tiles, wall_only):
    sub = lax.broadcasted_iota(jnp.int32, (8, 128), 0)
    down = [pltpu.roll(t, 1, 0) for t in tiles]
    up = [pltpu.roll(t, 7, 0) for t in tiles]
    last = len(tiles) - 1
    sums = []
    for i, t in enumerate(tiles):
        if wall_only:
            below = down[i]
        else:
            below = jnp.where(sub == 0, down[i - 1] if i > 0 else t, down[i])
        above = jnp.where(sub == 7, up[i + 1] if i < last else t, up[i])
        sums.append(below + above)
    return sums


def radial_sum_of(src, c, at, values):
    sub = lax.broadcasted_iota(jnp.int32, (8, 128), 0)
    sums = []
    for t in range(TILES):
        first, last = t == 0, t == TILES - 1
        below = jnp.where(sub == 0, values[t], pltpu.roll(values[t], 1, 0)) if first else src[c, at, 8 * t - 1 : 8 * t + 7, :]
        above = jnp.where(sub == 7, values[t], pltpu.roll(values[t], 7, 0)) if last else src[c, at, 8 * t + 1 : 8 * t + 9, :]
        sums.append(below + above)
    return sums


def strip_levels(strips, low_corner, high_corner, mix, edge, tiles):
    lane = lanes()
    wall_only = len(tiles) == 1
    from_low = (lane >= 2) & (lane < 6)
    from_high = (lane >= 38) & (lane < 42)
    held = {}
    for key in STRIPS:
        held[key] = [strips[STRIP_AT[key], rows(t), :] for t in tiles]
    for i, key in enumerate(CORNERS if low_corner else ()):
        for n in range(len(tiles)):
            value = jnp.where(from_low, pltpu.roll(low_corner[n], (2 - 4 * i) % 128, 1), held[key][n])
            held[key][n] = jnp.where(from_high, pltpu.roll(high_corner[n], (38 - 4 * i) % 128, 1), value)
    for step in range(ITERS):
        for c in range(COMP):
            for n in range(len(tiles)):
                edge[step, c, rows(n), :] = held[c, 1][n]
        if step == ITERS - 1:
            break
        later = {}
        for k in (2, 1, 0) if step == 0 else (1,):
            for c in range(COMP):
                radial = radial_sum(held[c, k], wall_only)
                later[c, k] = []
                for n in range(len(tiles)):
                    value = held[c, k][n]
                    around = held[c, k + 1][n] + held[c, k - 1][n]
                    around = around + pltpu.roll(value, 2, 1) + pltpu.roll(value, 126, 1) + radial[n]
                    later[c, k].append(updated(c, [held[d, k][n] for d in range(COMP)], around, held[COMP, k][n], mix))
        for key in [key for key in held if key[0] == COMP]:
            later[key] = held[key]
        held = later


class Shifted:
    def __init__(self, ref, offset):
        self.ref, self.offset = ref, offset

    def __getitem__(self, index):
        return self.ref[(index[0] + self.offset,) + index[1:]]


class Wrapped:
    def __init__(self, ref):
        self.ref = ref

    def __getitem__(self, index):
        return self.ref[index[1:]]


def plane(src, kappa, edge, step, at, x, mix, count, comps):
    lane = lanes()
    first, last = lane == 0, lane == 127
    shift = 121 - 2 * x
    values = [[src[c, at, rows(t), :] for t in range(count)] for c in range(COMP)]
    kap = [kappa[at, rows(t), :] for t in range(count)]
    out = {}
    for c in comps:
        radial = radial_sum(values[c], True) if count == 1 else radial_sum_of(src, c, at, values[c])
        for t in range(count):
            value = values[c][t]
            beyond = pltpu.roll(edge[step, c, rows(t), :], shift, 1)
            around = src[c, at - 1, rows(t), :] + src[c, at + 1, rows(t), :] + radial[t]
            around = around + jnp.where(first, beyond, pltpu.roll(value, 1, 1))
            around = around + jnp.where(last, beyond, pltpu.roll(value, 127, 1))
            out[c, t] = updated(c, [values[d][t] for d in range(COMP)], around, kap[t], mix)
    return out


def wall_kernel(gas, kappa, strips, recv_wall, recv_a, reaction, _, wall, now, later, kap, edge):
    odd = lax.rem(lax.axis_index("sect"), 2)
    even = odd == 0
    mix = coupling(reaction)
    top = slice(GR - 8, GR)
    at_a, at_b = jnp.where(even, GX + 3, 0), jnp.where(even, 0, GX + 3)
    kappa_a, kappa_b = jnp.where(even, GX + 3, 1), jnp.where(even, 1, GX + 3)
    for c in range(COMP):
        for x in range(GX):
            now[c, x + 3] = gas[c, x, top, :]
        for layer in range(3):
            now[c, at_a + layer] = recv_a[3 * c + layer, top, :]
            now[c, at_b + layer] = recv_wall[2 * (3 * c + layer) + 1]
    for x in range(GX):
        kap[x + 3] = kappa[x, top, :]
    for layer in range(2):
        kap[kappa_a + layer] = recv_a[3 * COMP + layer, top, :]
        kap[kappa_b + layer] = recv_wall[2 * (3 * COMP + layer) + 1]
    corner_a, corner_b = recv_a[LAYERS - 1, top, :], recv_wall[2 * (LAYERS - 1) + TILES - 1]
    low, high = jnp.where(even, corner_b, corner_a), jnp.where(even, corner_a, corner_b)
    strip_levels(strips, [low], [high], mix, edge, [TILES - 1])

    for step, (src, dst) in enumerate(((now, later), (later, now), (now, None))):
        comps = (0,) if step == ITERS - 1 else range(COMP)
        for at in range(step + 1, EXT - 1 - step):
            out = plane(src, kap, edge, step, at, at - 3, mix, 1, comps)
            if step == ITERS - 1:
                wall[at - 3 : at - 2, :] = out[0, 0][7:8, :]
                continue
            for c in comps:
                dst[c, at] = out[c, 0]


def inner_kernel(gas, kappa, strips, reaction, first, second, edges, one, edge):
    mix = coupling(reaction)
    strip_levels(strips, None, None, mix, edge, list(range(TILES)))
    edges[...] = edge[ITERS - 1]
    for step, (src, dst) in enumerate(((gas, one), (one, second))):

        def body(x, carry, step=step, src=src, dst=dst):
            out = plane(src, kappa, edge, step, x, x, mix, TILES, range(COMP))
            for (c, t), value in out.items():
                dst[c, x - 2 * step, rows(t), :] = value
            return carry

        lax.fori_loop(step + 1, GX - 1 - step, body, 0, unroll=2)
    for c in range(COMP):
        for i, x in enumerate(SEAM):
            first[c, i] = one[c, x]


def outer_kernel(
    _, gas, kappa, strips, first, second, edges, recv_wall, recv_a, recv_rest, reaction, result, token, now, later, now_two, kap, edge
):
    token[...] = jnp.zeros((8, 128), jnp.float32)
    even = lax.rem(lax.axis_index("sect"), 2) == 0
    mix = coupling(reaction)
    split = GR // 2
    at_a, at_b = jnp.where(even, GX + 3, 0), jnp.where(even, 0, GX + 3)
    kappa_a, kappa_b = jnp.where(even, GX + 3, 1), jnp.where(even, 1, GX + 3)
    for c in range(COMP):
        for x in (0, 1, GX - 2, GX - 1):
            now[c, x + 3] = gas[c, x]
        for layer in range(3):
            now[c, at_a + layer] = recv_a[3 * c + layer]
            for half in range(2):
                now[c, at_b + layer, rows(2 + half), :] = recv_wall[2 * (3 * c + layer) + half]
            now[c, at_b + layer, :split, :] = recv_rest[3 * c + layer]
        for i, x in enumerate(SEAM):
            later[c, x + 3] = first[c, i]
    for x in (0, 1, 2, GX - 3, GX - 2, GX - 1):
        kap[x + 3] = kappa[x]
    for layer in range(2):
        kap[kappa_a + layer] = recv_a[3 * COMP + layer]
        for half in range(2):
            kap[kappa_b + layer, rows(2 + half), :] = recv_wall[2 * (3 * COMP + layer) + half]
        kap[kappa_b + layer, :split, :] = recv_rest[3 * COMP + layer]
    low, high = [], []
    for t in range(TILES):
        corner_a = recv_a[LAYERS - 1, rows(t), :]
        corner_b = recv_wall[2 * (LAYERS - 1) + t]
        low.append(jnp.where(even, corner_b, corner_a))
        high.append(jnp.where(even, corner_a, corner_b))
    strip_levels(strips, low, high, mix, edge, list(range(TILES)))
    for c in range(COMP):
        for x in (2, 3, GX - 4, GX - 3):
            now_two[c, x + 3] = second[c, x - 2]

    def store(at, out, dst, shift):
        for (c, t), value in out.items():
            dst[c, at - shift, rows(t), :] = value

    for step, (src, dst, shift) in enumerate(((now, later, 0), (later, now_two, 0), (now_two, result, 3))):

        def body(i, carry, step=step, src=src, dst=dst, shift=shift):
            for at in (step + 1 + i, GX + 2 - step + i):
                store(at, plane(src, kap, edge, step, at, at - 3, mix, TILES, range(COMP)), dst, shift)
            return carry

        lax.fori_loop(0, 3, body, 0)

    def body(x, carry):
        out = third_plane(x)
        store(x, out, result, 0)
        return carry

    def third_plane(x):
        return plane(second, kap_inner, edge_inner, 0, x - 2, x, mix, TILES, range(COMP))

    kap_inner = Shifted(kappa, 2)
    edge_inner = Wrapped(edges)
    lax.fori_loop(3, GX - 3, body, 0, unroll=2)


def pack_kernel(hop, cell, particles, mixing, heating, _, packed, cells, spread, ordered, source, begin, end):
    lane = lanes()
    square = (128, 128)
    down, across = lax.broadcasted_iota(jnp.int32, square, 0), lanes(square)
    moves = hop[...]
    named = [moves == j for j in range(MOVES)]
    table = jnp.concatenate(
        [jnp.where(m, 1.0, 0.0) for m in named] + [jnp.zeros((128 - MOVES * CHUNKS, 128), jnp.float32)], axis=0
    )
    running = jnp.dot(table, jnp.where(down <= across, 1.0, 0.0), preferred_element_type=jnp.float32)
    count = jnp.dot(table, jnp.ones(square, jnp.float32), preferred_element_type=jnp.float32)
    before = jnp.where(((down >> 4) == (across >> 4)) & (across < down), 1.0, 0.0)
    base = jnp.dot(before, count, preferred_element_type=jnp.float32)
    offset = jnp.zeros((CHUNKS, 128), jnp.float32)
    place = jnp.zeros((CHUNKS, 128), jnp.float32)
    across16 = lanes((CHUNKS, 128))
    for j in range(MOVES):
        part = slice(CHUNKS * j, CHUNKS * (j + 1))
        place = jnp.where(named[j], offset + running[part] - 1.0, place)
        first = base[part].astype(jnp.int32)
        source[part, :] = (across16 + offset.astype(jnp.int32) - first) & 127
        begin[part, :] = across16 - first
        end[part, :] = across16 - first - count[part].astype(jnp.int32)
        offset = offset + count[part]
    own = lax.broadcasted_iota(jnp.int32, (VALS, VALS), 0) == lax.broadcasted_iota(jnp.int32, (VALS, VALS), 1)
    weights = 0.5 * mixing[...] + jnp.where(own, 1.0, 0.0)
    first_value = lax.broadcasted_iota(jnp.int32, (VALS, VALS), 1) == 0
    weights = weights - jnp.where(first_value, heating[...], 0.0)
    for v in range(VALS):
        spread[v] = jnp.broadcast_to(weights[:, v : v + 1], (VALS, 128))
    place = place.astype(jnp.int32)
    position = lane.astype(jnp.float32)
    for chunk in range(CHUNKS):
        part = slice(128 * chunk, 128 * (chunk + 1))
        total = spread[0] * particles[0:1, part]
        for v in range(1, VALS):
            total = total + spread[v] * particles[v : v + 1, part]
        hot = jnp.where(down == place[chunk : chunk + 1, :], 1.0, 0.0)
        order = lax.dot_general(position, hot, (((1,), (1,)), ((), ())), preferred_element_type=jnp.float32)
        order = order.astype(jnp.int32)
        ordered[chunk, 0:8, :] = pick(total[0:8], order)
        ordered[chunk, 8:16, :] = pick(total[8:16], order)
        ordered[chunk, 16:24, :] = pick(
            jnp.broadcast_to(cell[chunk : chunk + 1, :], (8, 128)).astype(jnp.float32), order
        )

    def block(j, carry):
        held = [[jnp.zeros((8, 128), jnp.float32)] * 2 + [jnp.full((8, 128), -1.0)] for _ in range(SPOTS)]
        for chunk in range(CHUNKS):
            row = pl.ds(CHUNKS * j + chunk, 1)
            index = jnp.broadcast_to(source[row, :], (8, 128))
            parts = [pick(ordered[chunk, rows(n), :], index) for n in range(3)]
            start = jnp.broadcast_to(begin[row, :], (8, 128))
            stop = jnp.broadcast_to(end[row, :], (8, 128))
            for spot in range(SPOTS):
                here = (start >= -128 * spot) & (stop < -128 * spot)
                held[spot] = [jnp.where(here, new, old) for new, old in zip(parts, held[spot])]
        for spot in range(SPOTS):
            part = slice(128 * spot, 128 * (spot + 1))
            packed[j, 0:8, part] = held[spot][0]
            packed[j, 8:16, part] = held[spot][1]
            cells[j, spot : spot + 1, :] = held[spot][2][0:1, :].astype(jnp.int32)
        return carry

    lax.fori_loop(0, MOVES, block, 0)


def moves_of_swaps():
    tile = lax.axis_index("blk")
    odd, late = lax.rem(tile, 2), lax.rem(tile, 4) >> 1
    return [REACH - 1 + 2 * odd, 2 * REACH * late, 2 * REACH * (1 - late), REACH + 1 - 2 * odd]


def heat_kernel(wall, earlier, packed, cells, heating, own, send_q, send_s, send_r, send_p, look):
    flux = 0.5 * (wall[...] + earlier[...])
    heat = jnp.broadcast_to(heating[...], (VALS, 128))
    for j in range(MOVES):
        where_to = cells[j]
        row, column = where_to >> 7, where_to & 127
        found = jnp.zeros((8, 128), jnp.float32)
        for x in range(GX):
            line = jnp.broadcast_to(flux[x : x + 1, :], (8, 128))
            found = jnp.where(row == x, pick(line, column), found)
        look[j] = found
    for out, j in zip((own, send_q, send_s, send_r, send_p), [REACH] + moves_of_swaps()):
        for spot in range(SPOTS):
            part = slice(128 * spot, 128 * (spot + 1))
            out[:, part] = packed[j, :, part] + heat * look[j, spot : spot + 1, :]


def join_kernel(own, recv_q, recv_s, recv_r, recv_p, _, out, done):
    copies = []
    for n, (piece, j) in enumerate(zip((own, recv_q, recv_s, recv_r, recv_p), [REACH] + moves_of_swaps())):
        place = pl.multiple_of((2 * REACH - j) * CAP, CAP)
        copies.append(pltpu.make_async_copy(piece, out.at[:, pl.ds(place, CAP)], done.at[n]))
    for copy in copies:
        copy.start()
    for copy in copies:
        copy.wait()


def swap(x, axis, pairs):
    return lax.ppermute(x, axis, pairs + [(j, i) for i, j in pairs])


def local(gas, kappa, reaction, particles, mixing, heating, wall_cell, tile_hop):
    sections, tiles = lax.axis_size("sect"), lax.axis_size("blk")
    pairs_a = [(i, i + 1) for i in range(0, sections, 2)]
    pairs_b = [(i, i + 1) for i in range(1, sections - 1, 2)]
    pairs_q = [(i, (i + 1) % tiles) for i in range(1, tiles, 2)]
    pairs_p = [(i, i + 1) for i in range(0, tiles, 2)]
    pairs_s = [(i, (i + 2) % tiles) for i in range(tiles) if i % 4 >= 2]
    pairs_r = [(i, i + 2) for i in range(tiles) if i % 4 < 2]

    send_q, send_p = call(
        edges_kernel,
        (f32(3, GR, GA), f32(3, GR, GA)),
        scratch=[pltpu.VMEM((COMP + 1, GX, GR, GA), jnp.float32), pltpu.SemaphoreType.DMA((COMP + 1,))],
        specs=[HBM] * 2,
        moved=2 << 20,
        limit=53.75,
    )(gas, kappa)
    recv_q = swap(send_q, "blk", pairs_q)
    recv_p = swap(send_p, "blk", pairs_p)
    heating_column = heating.reshape(VALS, 1)
    packed, cells = call(
        pack_kernel,
        (f32(MOVES, VALS, CAP), i32(MOVES, SPOTS, 128)),
        scratch=[
            pltpu.VMEM((VALS, VALS, 128), jnp.float32),
            pltpu.VMEM((CHUNKS, 24, 128), jnp.float32),
            pltpu.VMEM((MOVES * CHUNKS, 128), jnp.int32),
            pltpu.VMEM((MOVES * CHUNKS, 128), jnp.int32),
            pltpu.VMEM((MOVES * CHUNKS, 128), jnp.int32),
        ],
        specs=[VMEM] * 5 + [ANY],
        moved=4 << 20,
    )(tile_hop.reshape(CHUNKS, 128), wall_cell.reshape(CHUNKS, 128), particles, mixing, heating_column, send_p)

    strips, send_a, send_wall = call(
        strips_kernel,
        (f32(len(STRIPS), GR, GA), f32(LAYERS, GR, GA), f32(2 * (LAYERS - 1) + TILES, 8, GA)),
        specs=[VMEM] * 6 + [ANY],
        moved=2 << 20,
    )(gas, kappa, send_q, send_p, recv_q, recv_p, cells)
    recv_wall = swap(send_wall, "sect", pairs_b)
    recv_a = swap(send_a, "sect", pairs_a)

    whole = f32(COMP, GX, GR, GA)
    first, second, edges = call(
        inner_kernel,
        (f32(COMP, len(SEAM), GR, GA), f32(COMP, GX - 4, GR, GA), f32(COMP, GR, GA)),
        scratch=[
            pltpu.VMEM((COMP, GX, GR, GA), jnp.float32),
            pltpu.VMEM((ITERS, COMP, GR, GA), jnp.float32),
        ],
        specs=[VMEM] * 3 + [SMEM],
        moved=12 << 20,
    )(gas, kappa, strips, reaction)

    send_rest = call(rest_kernel, f32(LAYERS - 1, GR // 2, GA), specs=[VMEM] * 2 + [ANY], moved=1 << 18)(gas, kappa, second)
    recv_rest = swap(send_rest, "sect", pairs_b)

    wall = call(
        wall_kernel,
        f32(GX, GA),
        scratch=[
            pltpu.VMEM((COMP, EXT, 8, GA), jnp.float32),
            pltpu.VMEM((COMP, EXT, 8, GA), jnp.float32),
            pltpu.VMEM((EXT, 8, GA), jnp.float32),
            pltpu.VMEM((ITERS, COMP, 8, GA), jnp.float32),
        ],
        specs=[VMEM] * 5 + [SMEM, ANY],
        moved=4 << 20,
    )(gas, kappa, strips, recv_wall, recv_a, reaction, send_rest)
    earlier = lax.ppermute(wall, "sect", [(i, i + 1) for i in range(sections - 1)])

    own, *sends = call(
        heat_kernel,
        (f32(VALS, CAP),) * MOVES,
        scratch=[pltpu.VMEM((MOVES, SPOTS, 128), jnp.float32)],
        specs=[VMEM] * 5,
        moved=2 << 20,
    )(wall, earlier, packed, cells, heating_column)
    pieces = [swap(x, "blk", pairs) for x, pairs in zip(sends, (pairs_q, pairs_s, pairs_r, pairs_p))]

    field, token = call(
        outer_kernel,
        (whole, f32(8, 128)),
        scratch=[
            pltpu.VMEM((COMP, EXT, GR, GA), jnp.float32),
            pltpu.VMEM((COMP, EXT, GR, GA), jnp.float32),
            pltpu.VMEM((COMP, EXT, GR, GA), jnp.float32),
            pltpu.VMEM((EXT, GR, GA), jnp.float32),
            pltpu.VMEM((ITERS, COMP, GR, GA), jnp.float32),
        ],
        specs=[ANY] + [VMEM] * 9 + [SMEM],
        moved=8 << 20,
    )(pieces[0], gas, kappa, strips, first, second, edges, recv_wall, recv_a, recv_rest, reaction)
    arrived = call(
        join_kernel,
        f32(VALS, MOVES * CAP),
        scratch=[pltpu.SemaphoreType.DMA((MOVES,))],
        specs=[VMEM] * MOVES + [ANY],
        out_specs=HBM,
        moved=1 << 20,
    )(own, *pieces, token)
    return field, arrived


def solution(mesh):
    in_specs = (
        P(None, "sect", None, "blk"),
        P("sect", None, "blk"),
        P(),
        P(None, ("sect", "blk")),
        P(),
        P(),
        P(("sect", "blk")),
        P(("sect", "blk"), None),
    )
    out_specs = (P(None, "sect", None, "blk"), P(None, ("sect", "blk")))
    return jax.shard_map(local, mesh=mesh, in_specs=in_specs, out_specs=out_specs, check_vma=False)
```

```python
import jax
import jax.numpy as jnp
from jax import lax
from jax.experimental import pallas as pl
from jax.experimental.pallas import tpu as pltpu
from jax.sharding import PartitionSpec as P

REACH = 2
MOVES = 2 * REACH + 1
ITERS = 3
DIFFUSE = (1.0, 0.8, 0.6, 0.9, 0.7)
COMP = 5
GX = 16
GR = 32
GA = 128
TILES = GR // 8
EXT = GX + 2 * ITERS
CHUNKS = 16
VALS = 16
CAP = 1024
SPOTS = CAP // 128

FIELD_COLUMNS = (3, 2, 1, 0, -1)
KAPPA_COLUMNS = (2, 1, 0)
STRIPS = [(c, k) for c in range(COMP) for k in FIELD_COLUMNS] + [(COMP, k) for k in KAPPA_COLUMNS]
STRIP_AT = {key: i for i, key in enumerate(STRIPS)}
CORNERS = [(c, 1) for c in range(COMP)] + [(c, 2) for c in range(COMP)] + [(COMP, 1)] + [(c, 0) for c in range(COMP)]
LAYERS = 3 * COMP + 2 + 1
SEAM = (1, 2, GX - 3, GX - 2)

VMEM = pl.BlockSpec(memory_space=pltpu.VMEM)
SMEM = pl.BlockSpec(memory_space=pltpu.SMEM)
ANY = pl.BlockSpec(memory_space=pl.ANY)
HBM = pl.BlockSpec(memory_space=pltpu.HBM)


def f32(*shape):
    return jax.ShapeDtypeStruct(shape, jnp.float32)


def i32(*shape):
    return jax.ShapeDtypeStruct(shape, jnp.int32)


def lanes(shape=(8, 128)):
    return lax.broadcasted_iota(jnp.int32, shape, len(shape) - 1)


def pick(x, index):
    return jnp.take_along_axis(x, index, axis=1, mode="promise_in_bounds")


def rows(tile):
    return slice(8 * tile, 8 * tile + 8)


def call(kernel, outs, scratch=(), specs=None, out_specs=None, flops=0, moved=0, limit=16):
    return pl.pallas_call(
        kernel,
        out_shape=outs,
        in_specs=specs,
        out_specs=jax.tree.map(lambda _: VMEM, outs) if out_specs is None else out_specs,
        scratch_shapes=list(scratch),
        cost_estimate=pl.CostEstimate(flops=flops, bytes_accessed=moved, transcendentals=0),
        compiler_params=pltpu.CompilerParams(vmem_limit_bytes=int(limit * 2**20)),
    )


def edges_kernel(gas, kappa, send_q, send_p, held, arrived):
    copies = [pltpu.make_async_copy(gas.at[q], held.at[q], arrived.at[q]) for q in range(COMP)]
    copies.append(pltpu.make_async_copy(kappa, held.at[COMP], arrived.at[COMP]))
    for copy in copies:
        copy.start()
    lane = lanes()
    within = lane & 63
    depth, cell = within >> 4, within & 15
    high = jnp.maximum(6 * cell + 2 - depth, 0)
    low = 6 * cell + 3 + depth
    odd = lax.rem(lax.axis_index("blk"), 2) == 1
    index_q, index_p = jnp.where(odd, high, low), jnp.where(odd, low, high)
    for pair in range((COMP + 1) // 2):
        packed = {}
        for q in (2 * pair, 2 * pair + 1):
            copies[q].wait()
            for tile in range(TILES):
                total = jnp.zeros((8, 128), jnp.float32)
                for x in range(GX):
                    here = (lane >= 6 * x) & (lane < 6 * x + 6)
                    total = jnp.where(here, pltpu.roll(held[q, x, rows(tile), :], 6 * x + 3, 1), total)
                packed[q, tile] = total
        for tile in range(TILES):
            first, second = packed[2 * pair, tile], packed[2 * pair + 1, tile]
            for out, index in ((send_q, index_q), (send_p, index_p)):
                out[pair, rows(tile), :] = jnp.where(lane < 64, pick(first, index), pick(second, index))


def strips_kernel(gas, kappa, send_q, send_p, recv_q, recv_p, _, strips, send_a, send_wall):
    lane = lanes()
    low_side = (lane & 1) == 1
    cell = jnp.clip((lane >> 1) - 3, 0, GX - 1)
    even = lax.rem(lax.axis_index("sect"), 2) == 0
    odd_tile = lax.rem(lax.axis_index("blk"), 2) == 1
    for tile in range(TILES):
        held = {}
        slabs = [[ref[s, rows(tile), :] for s in range(3)] for ref in (send_q, send_p, recv_q, recv_p)]
        own_q, own_p, got_q, got_p = slabs
        to_left = [jnp.where(odd_tile, p, q) for q, p in zip(own_q, own_p)]
        to_right = [jnp.where(odd_tile, q, p) for q, p in zip(own_q, own_p)]
        from_left = [jnp.where(odd_tile, p, q) for q, p in zip(got_q, got_p)]
        from_right = [jnp.where(odd_tile, q, p) for q, p in zip(got_q, got_p)]
        for q, k in STRIPS:
            depth = k - 1 if k > 0 else -k
            index = cell + ((q % 2) * 64 + depth * 16)
            low, high = (from_left, from_right) if k > 0 else (to_left, to_right)
            value = jnp.where(low_side, pick(low[q // 2], index), pick(high[q // 2], index))
            strips[STRIP_AT[q, k], rows(tile), :] = value
            held[q, k] = value
        top = jnp.zeros((8, 128), jnp.float32)
        bottom = top
        for i, key in enumerate(CORNERS):
            here = (lane >> 2) == i
            top = jnp.where(here, pltpu.roll(held[key], (4 * i - 34) % 128, 1), top)
            bottom = jnp.where(here, pltpu.roll(held[key], (4 * i - 6) % 128, 1), bottom)
        for_a = jnp.where(even, top, bottom)
        for_b = jnp.where(even, bottom, top)
        send_a[LAYERS - 1, rows(tile), :] = for_a
        send_wall[LAYERS - 1 + tile] = for_b
    at_a, at_b = jnp.where(even, GX - 3, 0), jnp.where(even, 0, GX - 3)
    kappa_a, kappa_b = jnp.where(even, GX - 2, 0), jnp.where(even, 0, GX - 2)
    for c in range(COMP):
        for layer in range(3):
            send_a[3 * c + layer] = gas[c, at_a + layer]
            send_wall[3 * c + layer] = gas[c, at_b + layer, GR - 8 :, :]
    for layer in range(2):
        send_a[3 * COMP + layer] = kappa[kappa_a + layer]
        send_wall[3 * COMP + layer] = kappa[kappa_b + layer, GR - 8 :, :]


def rest_kernel(gas, kappa, _, send_rest):
    even = lax.rem(lax.axis_index("sect"), 2) == 0
    split = GR - 8
    from_b, from_kappa = jnp.where(even, 0, GX - 3), jnp.where(even, 0, GX - 2)
    for c in range(COMP):
        for layer in range(3):
            send_rest[3 * c + layer] = gas[c, from_b + layer, :split, :]
    for layer in range(2):
        send_rest[3 * COMP + layer] = kappa[from_kappa + layer, :split, :]


def coupling(reaction):
    return [[0.3 * reaction[c, d] + (1.0 if c == d else 0.0) for d in range(COMP)] for c in range(COMP)]


def updated(c, values, neighbours, kappa, mix):
    total = mix[c][0] * values[0]
    for d in range(1, COMP):
        total = total + mix[c][d] * values[d]
    rate = kappa if DIFFUSE[c] == 1.0 else DIFFUSE[c] * kappa
    return total + rate * (neighbours - 6.0 * values[c])


def radial_sum(tiles, wall_only):
    sub = lax.broadcasted_iota(jnp.int32, (8, 128), 0)
    down = [pltpu.roll(t, 1, 0) for t in tiles]
    up = [pltpu.roll(t, 7, 0) for t in tiles]
    last = len(tiles) - 1
    sums = []
    for i, t in enumerate(tiles):
        if wall_only:
            below = down[i]
        else:
            below = jnp.where(sub == 0, down[i - 1] if i > 0 else t, down[i])
        above = jnp.where(sub == 7, up[i + 1] if i < last else t, up[i])
        sums.append(below + above)
    return sums


def radial_sum_of(src, c, at, values):
    sub = lax.broadcasted_iota(jnp.int32, (8, 128), 0)
    sums = []
    for t in range(TILES):
        first, last = t == 0, t == TILES - 1
        below = jnp.where(sub == 0, values[t], pltpu.roll(values[t], 1, 0)) if first else src[c, at, 8 * t - 1 : 8 * t + 7, :]
        above = jnp.where(sub == 7, values[t], pltpu.roll(values[t], 7, 0)) if last else src[c, at, 8 * t + 1 : 8 * t + 9, :]
        sums.append(below + above)
    return sums


def strip_levels(strips, low_corner, high_corner, mix, edge, tiles):
    lane = lanes()
    wall_only = len(tiles) == 1
    from_low = (lane >= 2) & (lane < 6)
    from_high = (lane >= 38) & (lane < 42)
    held = {}
    for key in STRIPS:
        held[key] = [strips[STRIP_AT[key], rows(t), :] for t in tiles]
    for i, key in enumerate(CORNERS if low_corner else ()):
        for n in range(len(tiles)):
            value = jnp.where(from_low, pltpu.roll(low_corner[n], (2 - 4 * i) % 128, 1), held[key][n])
            held[key][n] = jnp.where(from_high, pltpu.roll(high_corner[n], (38 - 4 * i) % 128, 1), value)
    for step in range(ITERS):
        for c in range(COMP):
            for n in range(len(tiles)):
                edge[step, c, rows(n), :] = held[c, 1][n]
        if step == ITERS - 1:
            break
        later = {}
        for k in (2, 1, 0) if step == 0 else (1,):
            for c in range(COMP):
                radial = radial_sum(held[c, k], wall_only)
                later[c, k] = []
                for n in range(len(tiles)):
                    value = held[c, k][n]
                    around = held[c, k + 1][n] + held[c, k - 1][n]
                    around = around + pltpu.roll(value, 2, 1) + pltpu.roll(value, 126, 1) + radial[n]
                    later[c, k].append(updated(c, [held[d, k][n] for d in range(COMP)], around, held[COMP, k][n], mix))
        for key in [key for key in held if key[0] == COMP]:
            later[key] = held[key]
        held = later


def plane(src, kappa, edge, step, at, x, mix, count, comps):
    lane = lanes()
    first, last = lane == 0, lane == 127
    shift = 121 - 2 * x
    values = [[src[c, at, rows(t), :] for t in range(count)] for c in range(COMP)]
    kap = [kappa[at, rows(t), :] for t in range(count)]
    out = {}
    for c in comps:
        radial = radial_sum(values[c], True) if count == 1 else radial_sum_of(src, c, at, values[c])
        for t in range(count):
            value = values[c][t]
            beyond = pltpu.roll(edge[step, c, rows(t), :], shift, 1)
            around = src[c, at - 1, rows(t), :] + src[c, at + 1, rows(t), :] + radial[t]
            around = around + jnp.where(first, beyond, pltpu.roll(value, 1, 1))
            around = around + jnp.where(last, beyond, pltpu.roll(value, 127, 1))
            out[c, t] = updated(c, [values[d][t] for d in range(COMP)], around, kap[t], mix)
    return out


def wall_kernel(gas, kappa, strips, recv_wall, recv_a, reaction, _, wall, now, later, kap, edge):
    odd = lax.rem(lax.axis_index("sect"), 2)
    even = odd == 0
    mix = coupling(reaction)
    top = slice(GR - 8, GR)
    at_a, at_b = jnp.where(even, GX + 3, 0), jnp.where(even, 0, GX + 3)
    kappa_a, kappa_b = jnp.where(even, GX + 3, 1), jnp.where(even, 1, GX + 3)
    for c in range(COMP):
        for x in range(GX):
            now[c, x + 3] = gas[c, x, top, :]
        for layer in range(3):
            now[c, at_a + layer] = recv_a[3 * c + layer, top, :]
            now[c, at_b + layer] = recv_wall[3 * c + layer]
    for x in range(GX):
        kap[x + 3] = kappa[x, top, :]
    for layer in range(2):
        kap[kappa_a + layer] = recv_a[3 * COMP + layer, top, :]
        kap[kappa_b + layer] = recv_wall[3 * COMP + layer]
    corner_a, corner_b = recv_a[LAYERS - 1, top, :], recv_wall[LAYERS - 1 + TILES - 1]
    low, high = jnp.where(even, corner_b, corner_a), jnp.where(even, corner_a, corner_b)
    strip_levels(strips, [low], [high], mix, edge, [TILES - 1])

    for step, (src, dst) in enumerate(((now, later), (later, now), (now, None))):
        comps = (0,) if step == ITERS - 1 else range(COMP)
        for at in range(step + 1, EXT - 1 - step):
            out = plane(src, kap, edge, step, at, at - 3, mix, 1, comps)
            if step == ITERS - 1:
                wall[at - 3 : at - 2, :] = out[0, 0][7:8, :]
                continue
            for c in comps:
                dst[c, at] = out[c, 0]


def inner_kernel(gas, kappa, strips, reaction, first, second, middle, one, two, edge):
    mix = coupling(reaction)
    strip_levels(strips, None, None, mix, edge, list(range(TILES)))
    for step, (src, dst) in enumerate(((gas, one), (one, two), (two, middle))):

        def body(x, carry, step=step, src=src, dst=dst):
            out = plane(src, kappa, edge, step, x, x, mix, TILES, range(COMP))
            into = x - 3 if step == ITERS - 1 else x
            for (c, t), value in out.items():
                dst[c, into, rows(t), :] = value
            return carry

        lax.fori_loop(step + 1, GX - 1 - step, body, 0, unroll=2)
    for c in range(COMP):
        for i, x in enumerate(SEAM):
            first[c, i] = one[c, x]
            second[c, i] = two[c, x + 1 if i < 2 else x - 1]


def outer_kernel(
    _, gas, kappa, strips, first, second, middle, recv_wall, recv_a, recv_rest, reaction, result, token, now, later, kap, edge
):
    token[...] = jnp.zeros((8, 128), jnp.float32)
    even = lax.rem(lax.axis_index("sect"), 2) == 0
    mix = coupling(reaction)
    split = GR - 8
    at_a, at_b = jnp.where(even, GX + 3, 0), jnp.where(even, 0, GX + 3)
    kappa_a, kappa_b = jnp.where(even, GX + 3, 1), jnp.where(even, 1, GX + 3)
    for c in range(COMP):
        for x in (0, 1, GX - 2, GX - 1):
            now[c, x + 3] = gas[c, x]
        for layer in range(3):
            now[c, at_a + layer] = recv_a[3 * c + layer]
            now[c, at_b + layer, split:, :] = recv_wall[3 * c + layer]
            now[c, at_b + layer, :split, :] = recv_rest[3 * c + layer]
        for i, x in enumerate(SEAM):
            later[c, x + 3] = first[c, i]
    for x in (0, 1, 2, GX - 3, GX - 2, GX - 1):
        kap[x + 3] = kappa[x]
    for layer in range(2):
        kap[kappa_a + layer] = recv_a[3 * COMP + layer]
        kap[kappa_b + layer, split:, :] = recv_wall[3 * COMP + layer]
        kap[kappa_b + layer, :split, :] = recv_rest[3 * COMP + layer]
    low, high = [], []
    for t in range(TILES):
        corner_a = recv_a[LAYERS - 1, rows(t), :]
        corner_b = recv_wall[LAYERS - 1 + t]
        low.append(jnp.where(even, corner_b, corner_a))
        high.append(jnp.where(even, corner_a, corner_b))
    strip_levels(strips, low, high, mix, edge, list(range(TILES)))
    for c in range(COMP):
        result[c, 3 : GX - 3] = middle[c]
    for step, (src, dst) in enumerate(((now, later), (later, now), (now, None))):
        if step == ITERS - 1:
            for c in range(COMP):
                for i, x in enumerate(SEAM):
                    now[c, (x + 1 if i < 2 else x - 1) + 3] = second[c, i]
        for i in range(3):
            for at in (step + 1 + i, GX + 2 - step + i):
                out = plane(src, kap, edge, step, at, at - 3, mix, TILES, range(COMP))
                for (c, t), value in out.items():
                    if step == ITERS - 1:
                        result[c, at - 3, rows(t), :] = value
                    else:
                        dst[c, at, rows(t), :] = value


def pack_kernel(hop, cell, particles, mixing, heating, _, packed, cells, spread, ordered, source, begin, end):
    lane = lanes()
    square = (128, 128)
    down, across = lax.broadcasted_iota(jnp.int32, square, 0), lanes(square)
    moves = hop[...]
    named = [moves == j for j in range(MOVES)]
    table = jnp.concatenate(
        [jnp.where(m, 1.0, 0.0) for m in named] + [jnp.zeros((128 - MOVES * CHUNKS, 128), jnp.float32)], axis=0
    )
    running = jnp.dot(table, jnp.where(down <= across, 1.0, 0.0), preferred_element_type=jnp.float32)
    count = jnp.dot(table, jnp.ones(square, jnp.float32), preferred_element_type=jnp.float32)
    before = jnp.where(((down >> 4) == (across >> 4)) & (across < down), 1.0, 0.0)
    base = jnp.dot(before, count, preferred_element_type=jnp.float32)
    offset = jnp.zeros((CHUNKS, 128), jnp.float32)
    place = jnp.zeros((CHUNKS, 128), jnp.float32)
    across16 = lanes((CHUNKS, 128))
    for j in range(MOVES):
        part = slice(CHUNKS * j, CHUNKS * (j + 1))
        place = jnp.where(named[j], offset + running[part] - 1.0, place)
        first = base[part].astype(jnp.int32)
        source[part, :] = (across16 + offset.astype(jnp.int32) - first) & 127
        begin[part, :] = across16 - first
        end[part, :] = across16 - first - count[part].astype(jnp.int32)
        offset = offset + count[part]
    own = lax.broadcasted_iota(jnp.int32, (VALS, VALS), 0) == lax.broadcasted_iota(jnp.int32, (VALS, VALS), 1)
    weights = 0.5 * mixing[...] + jnp.where(own, 1.0, 0.0)
    first_value = lax.broadcasted_iota(jnp.int32, (VALS, VALS), 1) == 0
    weights = weights - jnp.where(first_value, heating[...], 0.0)
    for v in range(VALS):
        spread[v] = jnp.broadcast_to(weights[:, v : v + 1], (VALS, 128))
    place = place.astype(jnp.int32)
    position = lane.astype(jnp.float32)
    for chunk in range(CHUNKS):
        part = slice(128 * chunk, 128 * (chunk + 1))
        total = spread[0] * particles[0:1, part]
        for v in range(1, VALS):
            total = total + spread[v] * particles[v : v + 1, part]
        hot = jnp.where(down == place[chunk : chunk + 1, :], 1.0, 0.0)
        order = lax.dot_general(position, hot, (((1,), (1,)), ((), ())), preferred_element_type=jnp.float32)
        order = order.astype(jnp.int32)
        ordered[chunk, 0:8, :] = pick(total[0:8], order)
        ordered[chunk, 8:16, :] = pick(total[8:16], order)
        ordered[chunk, 16:24, :] = pick(
            jnp.broadcast_to(cell[chunk : chunk + 1, :], (8, 128)).astype(jnp.float32), order
        )

    def block(j, carry):
        held = [[jnp.zeros((8, 128), jnp.float32)] * 2 + [jnp.full((8, 128), -1.0)] for _ in range(SPOTS)]
        for chunk in range(CHUNKS):
            row = pl.ds(CHUNKS * j + chunk, 1)
            index = jnp.broadcast_to(source[row, :], (8, 128))
            parts = [pick(ordered[chunk, rows(n), :], index) for n in range(3)]
            start = jnp.broadcast_to(begin[row, :], (8, 128))
            stop = jnp.broadcast_to(end[row, :], (8, 128))
            for spot in range(SPOTS):
                here = (start >= -128 * spot) & (stop < -128 * spot)
                held[spot] = [jnp.where(here, new, old) for new, old in zip(parts, held[spot])]
        for spot in range(SPOTS):
            part = slice(128 * spot, 128 * (spot + 1))
            packed[j, 0:8, part] = held[spot][0]
            packed[j, 8:16, part] = held[spot][1]
            cells[j, spot : spot + 1, :] = held[spot][2][0:1, :].astype(jnp.int32)
        return carry

    lax.fori_loop(0, MOVES, block, 0)


def moves_of_swaps():
    tile = lax.axis_index("blk")
    odd, late = lax.rem(tile, 2), lax.rem(tile, 4) >> 1
    return [REACH - 1 + 2 * odd, 2 * REACH * late, 2 * REACH * (1 - late), REACH + 1 - 2 * odd]


def heat_kernel(wall, earlier, packed, cells, heating, own, send_q, send_s, send_r, send_p, look):
    flux = 0.5 * (wall[...] + earlier[...])
    heat = jnp.broadcast_to(heating[...], (VALS, 128))
    for j in range(MOVES):
        where_to = cells[j]
        row, column = where_to >> 7, where_to & 127
        found = jnp.zeros((8, 128), jnp.float32)
        for x in range(GX):
            line = jnp.broadcast_to(flux[x : x + 1, :], (8, 128))
            found = jnp.where(row == x, pick(line, column), found)
        look[j] = found
    for out, j in zip((own, send_q, send_s, send_r, send_p), [REACH] + moves_of_swaps()):
        for spot in range(SPOTS):
            part = slice(128 * spot, 128 * (spot + 1))
            out[:, part] = packed[j, :, part] + heat * look[j, spot : spot + 1, :]


def join_kernel(own, recv_q, recv_s, recv_r, recv_p, _, out, done):
    copies = []
    for n, (piece, j) in enumerate(zip((own, recv_q, recv_s, recv_r, recv_p), [REACH] + moves_of_swaps())):
        place = pl.multiple_of((2 * REACH - j) * CAP, CAP)
        copies.append(pltpu.make_async_copy(piece, out.at[:, pl.ds(place, CAP)], done.at[n]))
    for copy in copies:
        copy.start()
    for copy in copies:
        copy.wait()


def swap(x, axis, pairs):
    return lax.ppermute(x, axis, pairs + [(j, i) for i, j in pairs])


def local(gas, kappa, reaction, particles, mixing, heating, wall_cell, tile_hop):
    sections, tiles = lax.axis_size("sect"), lax.axis_size("blk")
    pairs_a = [(i, i + 1) for i in range(0, sections, 2)]
    pairs_b = [(i, i + 1) for i in range(1, sections - 1, 2)]
    pairs_q = [(i, (i + 1) % tiles) for i in range(1, tiles, 2)]
    pairs_p = [(i, i + 1) for i in range(0, tiles, 2)]
    pairs_s = [(i, (i + 2) % tiles) for i in range(tiles) if i % 4 >= 2]
    pairs_r = [(i, i + 2) for i in range(tiles) if i % 4 < 2]

    send_q, send_p = call(
        edges_kernel,
        (f32(3, GR, GA), f32(3, GR, GA)),
        scratch=[pltpu.VMEM((COMP + 1, GX, GR, GA), jnp.float32), pltpu.SemaphoreType.DMA((COMP + 1,))],
        specs=[HBM] * 2,
        moved=2 << 20,
        limit=53.75,
    )(gas, kappa)
    recv_q = swap(send_q, "blk", pairs_q)
    recv_p = swap(send_p, "blk", pairs_p)
    heating_column = heating.reshape(VALS, 1)
    packed, cells = call(
        pack_kernel,
        (f32(MOVES, VALS, CAP), i32(MOVES, SPOTS, 128)),
        scratch=[
            pltpu.VMEM((VALS, VALS, 128), jnp.float32),
            pltpu.VMEM((CHUNKS, 24, 128), jnp.float32),
            pltpu.VMEM((MOVES * CHUNKS, 128), jnp.int32),
            pltpu.VMEM((MOVES * CHUNKS, 128), jnp.int32),
            pltpu.VMEM((MOVES * CHUNKS, 128), jnp.int32),
        ],
        specs=[VMEM] * 5 + [ANY],
        moved=4 << 20,
    )(tile_hop.reshape(CHUNKS, 128), wall_cell.reshape(CHUNKS, 128), particles, mixing, heating_column, send_p)

    strips, send_a, send_wall = call(
        strips_kernel,
        (f32(len(STRIPS), GR, GA), f32(LAYERS, GR, GA), f32(LAYERS - 1 + TILES, 8, GA)),
        specs=[VMEM] * 6 + [ANY],
        moved=2 << 20,
    )(gas, kappa, send_q, send_p, recv_q, recv_p, cells)
    recv_wall = swap(send_wall, "sect", pairs_b)
    recv_a = swap(send_a, "sect", pairs_a)

    whole = f32(COMP, GX, GR, GA)
    first, second, middle = call(
        inner_kernel,
        (f32(COMP, len(SEAM), GR, GA), f32(COMP, len(SEAM), GR, GA), f32(COMP, GX - 6, GR, GA)),
        scratch=[
            pltpu.VMEM((COMP, GX, GR, GA), jnp.float32),
            pltpu.VMEM((COMP, GX, GR, GA), jnp.float32),
            pltpu.VMEM((ITERS, COMP, GR, GA), jnp.float32),
        ],
        specs=[VMEM] * 3 + [SMEM],
        moved=12 << 20,
    )(gas, kappa, strips, reaction)

    send_rest = call(rest_kernel, f32(LAYERS - 1, GR - 8, GA), specs=[VMEM] * 2 + [ANY], moved=1 << 18)(gas, kappa, middle)
    recv_rest = swap(send_rest, "sect", pairs_b)

    wall = call(
        wall_kernel,
        f32(GX, GA),
        scratch=[
            pltpu.VMEM((COMP, EXT, 8, GA), jnp.float32),
            pltpu.VMEM((COMP, EXT, 8, GA), jnp.float32),
            pltpu.VMEM((EXT, 8, GA), jnp.float32),
            pltpu.VMEM((ITERS, COMP, 8, GA), jnp.float32),
        ],
        specs=[VMEM] * 5 + [SMEM, ANY],
        moved=4 << 20,
    )(gas, kappa, strips, recv_wall, recv_a, reaction, send_rest)
    earlier = lax.ppermute(wall, "sect", [(i, i + 1) for i in range(sections - 1)])

    own, *sends = call(
        heat_kernel,
        (f32(VALS, CAP),) * MOVES,
        scratch=[pltpu.VMEM((MOVES, SPOTS, 128), jnp.float32)],
        specs=[VMEM] * 5,
        moved=2 << 20,
        flops=1 << 34,
    )(wall, earlier, packed, cells, heating_column)
    pieces = [swap(x, "blk", pairs) for x, pairs in zip(sends, (pairs_q, pairs_s, pairs_r, pairs_p))]

    field, token = call(
        outer_kernel,
        (whole, f32(8, 128)),
        scratch=[
            pltpu.VMEM((COMP, EXT, GR, GA), jnp.float32),
            pltpu.VMEM((COMP, EXT, GR, GA), jnp.float32),
            pltpu.VMEM((EXT, GR, GA), jnp.float32),
            pltpu.VMEM((ITERS, COMP, GR, GA), jnp.float32),
        ],
        specs=[ANY] + [VMEM] * 9 + [SMEM],
        moved=8 << 20,
    )(pieces[0], gas, kappa, strips, first, second, middle, recv_wall, recv_a, recv_rest, reaction)
    arrived = call(
        join_kernel,
        f32(VALS, MOVES * CAP),
        scratch=[pltpu.SemaphoreType.DMA((MOVES,))],
        specs=[VMEM] * MOVES + [ANY],
        out_specs=HBM,
        moved=1 << 20,
    )(own, *pieces, token)
    return field, arrived


def solution(mesh):
    in_specs = (
        P(None, "sect", None, "blk"),
        P("sect", None, "blk"),
        P(),
        P(None, ("sect", "blk")),
        P(),
        P(),
        P(("sect", "blk")),
        P(("sect", "blk"), None),
    )
    out_specs = (P(None, "sect", None, "blk"), P(None, ("sect", "blk")))
    return jax.shard_map(local, mesh=mesh, in_specs=in_specs, out_specs=out_specs, check_vma=False)
```

```python
import jax
import jax.numpy as jnp
from jax import lax
from jax.experimental import pallas as pl
from jax.experimental.pallas import tpu as pltpu
from jax.sharding import PartitionSpec as P

REACH = 2
MOVES = 2 * REACH + 1
ITERS = 3
DIFFUSE = (1.0, 0.8, 0.6, 0.9, 0.7)
COMP = 5
GX = 16
GR = 32
GA = 128
TILES = GR // 8
EXT = GX + 2 * ITERS
CHUNKS = 16
VALS = 16
CAP = 1024
SPOTS = CAP // 128

FIELD_COLUMNS = (3, 2, 1, 0, -1)
KAPPA_COLUMNS = (2, 1, 0)
STRIPS = [(c, k) for c in range(COMP) for k in FIELD_COLUMNS] + [(COMP, k) for k in KAPPA_COLUMNS]
STRIP_AT = {key: i for i, key in enumerate(STRIPS)}
CORNERS = [(c, 1) for c in range(COMP)] + [(c, 2) for c in range(COMP)] + [(COMP, 1)] + [(c, 0) for c in range(COMP)]
LAYERS = 3 * COMP + 2 + 1
SEAM = (1, 2, GX - 3, GX - 2)

VMEM = pl.BlockSpec(memory_space=pltpu.VMEM)
SMEM = pl.BlockSpec(memory_space=pltpu.SMEM)
ANY = pl.BlockSpec(memory_space=pl.ANY)
HBM = pl.BlockSpec(memory_space=pltpu.HBM)


def f32(*shape):
    return jax.ShapeDtypeStruct(shape, jnp.float32)


def i32(*shape):
    return jax.ShapeDtypeStruct(shape, jnp.int32)


def lanes(shape=(8, 128)):
    return lax.broadcasted_iota(jnp.int32, shape, len(shape) - 1)


def pick(x, index):
    return jnp.take_along_axis(x, index, axis=1, mode="promise_in_bounds")


def rows(tile):
    return slice(8 * tile, 8 * tile + 8)


def call(kernel, outs, scratch=(), specs=None, out_specs=None, flops=0, moved=0, limit=16):
    return pl.pallas_call(
        kernel,
        out_shape=outs,
        in_specs=specs,
        out_specs=jax.tree.map(lambda _: VMEM, outs) if out_specs is None else out_specs,
        scratch_shapes=list(scratch),
        cost_estimate=pl.CostEstimate(flops=flops, bytes_accessed=moved, transcendentals=0),
        compiler_params=pltpu.CompilerParams(vmem_limit_bytes=int(limit * 2**20)),
    )


def edges_kernel(gas, kappa, send_q, send_p, held, arrived):
    copies = [pltpu.make_async_copy(gas.at[q], held.at[q], arrived.at[q]) for q in range(COMP)]
    copies.append(pltpu.make_async_copy(kappa, held.at[COMP], arrived.at[COMP]))
    for copy in copies:
        copy.start()
    lane = lanes()
    within = lane & 63
    depth, cell = within >> 4, within & 15
    high = jnp.maximum(6 * cell + 2 - depth, 0)
    low = 6 * cell + 3 + depth
    odd = lax.rem(lax.axis_index("blk"), 2) == 1
    index_q, index_p = jnp.where(odd, high, low), jnp.where(odd, low, high)
    for pair in range((COMP + 1) // 2):
        packed = {}
        for q in (2 * pair, 2 * pair + 1):
            copies[q].wait()
            for tile in range(TILES):
                total = jnp.zeros((8, 128), jnp.float32)
                for x in range(GX):
                    here = (lane >= 6 * x) & (lane < 6 * x + 6)
                    total = jnp.where(here, pltpu.roll(held[q, x, rows(tile), :], 6 * x + 3, 1), total)
                packed[q, tile] = total
        for tile in range(TILES):
            first, second = packed[2 * pair, tile], packed[2 * pair + 1, tile]
            for out, index in ((send_q, index_q), (send_p, index_p)):
                out[pair, rows(tile), :] = jnp.where(lane < 64, pick(first, index), pick(second, index))


def edge_sides(send_q, send_p, recv_q, recv_p, tile):
    odd = lax.rem(lax.axis_index("blk"), 2) == 1
    slabs = [[ref[s, rows(tile), :] for s in range(3)] for ref in (send_q, send_p, recv_q, recv_p)]
    own_q, own_p, got_q, got_p = slabs
    left = [jnp.where(odd, p, q) for q, p in zip(own_q, own_p)]
    right = [jnp.where(odd, q, p) for q, p in zip(own_q, own_p)]
    from_left = [jnp.where(odd, p, q) for q, p in zip(got_q, got_p)]
    from_right = [jnp.where(odd, q, p) for q, p in zip(got_q, got_p)]
    return (left, right), (from_left, from_right)


def strip_of(sides, q, k):
    lane = lanes()
    own, got = sides
    low, high = got if k > 0 else own
    depth = k - 1 if k > 0 else -k
    index = jnp.clip((lane >> 1) - 3, 0, GX - 1) + ((q % 2) * 64 + depth * 16)
    return jnp.where((lane & 1) == 1, pick(low[q // 2], index), pick(high[q // 2], index))


def strips_kernel(send_q, send_p, recv_q, recv_p, _, strips):
    for tile in range(TILES):
        sides = edge_sides(send_q, send_p, recv_q, recv_p, tile)
        for i, (q, k) in enumerate(STRIPS):
            strips[i, rows(tile), :] = strip_of(sides, q, k)


def sends_kernel(gas, kappa, send_q, send_p, recv_q, recv_p, _, send_a, send_wall):
    lane = lanes()
    even = lax.rem(lax.axis_index("sect"), 2) == 0
    for tile in range(TILES):
        sides = edge_sides(send_q, send_p, recv_q, recv_p, tile)
        top = jnp.zeros((8, 128), jnp.float32)
        bottom = top
        for i, (q, k) in enumerate(CORNERS):
            here = (lane >> 2) == i
            strip = strip_of(sides, q, k)
            top = jnp.where(here, pltpu.roll(strip, (4 * i - 34) % 128, 1), top)
            bottom = jnp.where(here, pltpu.roll(strip, (4 * i - 6) % 128, 1), bottom)
        send_a[LAYERS - 1, rows(tile), :] = jnp.where(even, top, bottom)
        send_wall[LAYERS - 1 + tile] = jnp.where(even, bottom, top)
    at_a, at_b = jnp.where(even, GX - 3, 0), jnp.where(even, 0, GX - 3)
    kappa_a, kappa_b = jnp.where(even, GX - 2, 0), jnp.where(even, 0, GX - 2)
    for c in range(COMP):
        for layer in range(3):
            send_a[3 * c + layer] = gas[c, at_a + layer]
            send_wall[3 * c + layer] = gas[c, at_b + layer, GR - 8 :, :]
    for layer in range(2):
        send_a[3 * COMP + layer] = kappa[kappa_a + layer]
        send_wall[3 * COMP + layer] = kappa[kappa_b + layer, GR - 8 :, :]


def rest_kernel(gas, kappa, _, send_rest):
    even = lax.rem(lax.axis_index("sect"), 2) == 0
    split = GR - 8
    from_b, from_kappa = jnp.where(even, 0, GX - 3), jnp.where(even, 0, GX - 2)
    for c in range(COMP):
        for layer in range(3):
            send_rest[3 * c + layer] = gas[c, from_b + layer, :split, :]
    for layer in range(2):
        send_rest[3 * COMP + layer] = kappa[from_kappa + layer, :split, :]


def coupling(reaction):
    return [[0.3 * reaction[c, d] + (1.0 if c == d else 0.0) for d in range(COMP)] for c in range(COMP)]


def updated(c, values, neighbours, kappa, mix):
    total = mix[c][0] * values[0]
    for d in range(1, COMP):
        total = total + mix[c][d] * values[d]
    rate = kappa if DIFFUSE[c] == 1.0 else DIFFUSE[c] * kappa
    return total + rate * (neighbours - 6.0 * values[c])


def radial_sum(tiles, wall_only):
    sub = lax.broadcasted_iota(jnp.int32, (8, 128), 0)
    down = [pltpu.roll(t, 1, 0) for t in tiles]
    up = [pltpu.roll(t, 7, 0) for t in tiles]
    last = len(tiles) - 1
    sums = []
    for i, t in enumerate(tiles):
        if wall_only:
            below = down[i]
        else:
            below = jnp.where(sub == 0, down[i - 1] if i > 0 else t, down[i])
        above = jnp.where(sub == 7, up[i + 1] if i < last else t, up[i])
        sums.append(below + above)
    return sums


def radial_sum_of(src, c, at, values):
    sub = lax.broadcasted_iota(jnp.int32, (8, 128), 0)
    sums = []
    for t in range(TILES):
        first, last = t == 0, t == TILES - 1
        below = jnp.where(sub == 0, values[t], pltpu.roll(values[t], 1, 0)) if first else src[c, at, 8 * t - 1 : 8 * t + 7, :]
        above = jnp.where(sub == 7, values[t], pltpu.roll(values[t], 7, 0)) if last else src[c, at, 8 * t + 1 : 8 * t + 9, :]
        sums.append(below + above)
    return sums


def strip_levels(strips, low_corner, high_corner, mix, edge, tiles):
    lane = lanes()
    wall_only = len(tiles) == 1
    from_low = (lane >= 2) & (lane < 6)
    from_high = (lane >= 38) & (lane < 42)
    held = {}
    for key in STRIPS:
        held[key] = [strips[STRIP_AT[key], rows(t), :] for t in tiles]
    for i, key in enumerate(CORNERS if low_corner else ()):
        for n in range(len(tiles)):
            value = jnp.where(from_low, pltpu.roll(low_corner[n], (2 - 4 * i) % 128, 1), held[key][n])
            held[key][n] = jnp.where(from_high, pltpu.roll(high_corner[n], (38 - 4 * i) % 128, 1), value)
    for step in range(ITERS):
        for c in range(COMP):
            for n in range(len(tiles)):
                edge[step, c, rows(n), :] = held[c, 1][n]
        if step == ITERS - 1:
            break
        later = {}
        for k in (2, 1, 0) if step == 0 else (1,):
            for c in range(COMP):
                radial = radial_sum(held[c, k], wall_only)
                later[c, k] = []
                for n in range(len(tiles)):
                    value = held[c, k][n]
                    around = held[c, k + 1][n] + held[c, k - 1][n]
                    around = around + pltpu.roll(value, 2, 1) + pltpu.roll(value, 126, 1) + radial[n]
                    later[c, k].append(updated(c, [held[d, k][n] for d in range(COMP)], around, held[COMP, k][n], mix))
        for key in [key for key in held if key[0] == COMP]:
            later[key] = held[key]
        held = later


def plane(src, kappa, edge, step, at, x, mix, count, comps):
    lane = lanes()
    first, last = lane == 0, lane == 127
    shift = 121 - 2 * x
    values = [[src[c, at, rows(t), :] for t in range(count)] for c in range(COMP)]
    kap = [kappa[at, rows(t), :] for t in range(count)]
    out = {}
    for c in comps:
        radial = radial_sum(values[c], True) if count == 1 else radial_sum_of(src, c, at, values[c])
        for t in range(count):
            value = values[c][t]
            beyond = pltpu.roll(edge[step, c, rows(t), :], shift, 1)
            around = src[c, at - 1, rows(t), :] + src[c, at + 1, rows(t), :] + radial[t]
            around = around + jnp.where(first, beyond, pltpu.roll(value, 1, 1))
            around = around + jnp.where(last, beyond, pltpu.roll(value, 127, 1))
            out[c, t] = updated(c, [values[d][t] for d in range(COMP)], around, kap[t], mix)
    return out


def wall_kernel(
    gas, kappa, strips, recv_wall, recv_a, first, second, middle, reaction, _, wall, now, later, kap, edge
):
    even = lax.rem(lax.axis_index("sect"), 2) == 0
    mix = coupling(reaction)
    top = slice(GR - 8, GR)
    at_a, at_b = jnp.where(even, GX + 3, 0), jnp.where(even, 0, GX + 3)
    kappa_a, kappa_b = jnp.where(even, GX + 3, 1), jnp.where(even, 1, GX + 3)
    for c in range(COMP):
        for x in (0, 1, GX - 2, GX - 1):
            now[c, x + 3] = gas[c, x, top, :]
        for layer in range(3):
            now[c, at_a + layer] = recv_a[3 * c + layer, top, :]
            now[c, at_b + layer] = recv_wall[3 * c + layer]
        for i, x in enumerate(SEAM):
            later[c, x + 3] = first[c, i, top, :]
    for x in (0, 1, 2, GX - 3, GX - 2, GX - 1):
        kap[x + 3] = kappa[x, top, :]
    for layer in range(2):
        kap[kappa_a + layer] = recv_a[3 * COMP + layer, top, :]
        kap[kappa_b + layer] = recv_wall[3 * COMP + layer]
    corner_a, corner_b = recv_a[LAYERS - 1, top, :], recv_wall[LAYERS - 1 + TILES - 1]
    low, high = jnp.where(even, corner_b, corner_a), jnp.where(even, corner_a, corner_b)
    strip_levels(strips, [low], [high], mix, edge, [TILES - 1])
    wall[3 : GX - 3, :] = middle[0, :, GR - 1, :]
    for step, (src, dst) in enumerate(((now, later), (later, now), (now, None))):
        last = step == ITERS - 1
        if last:
            for c in range(COMP):
                for i, x in enumerate(SEAM):
                    now[c, (x + 1 if i < 2 else x - 1) + 3] = second[c, i, top, :]
        for i in range(3):
            for at in (step + 1 + i, GX + 2 - step + i):
                out = plane(src, kap, edge, step, at, at - 3, mix, 1, (0,) if last else range(COMP))
                if last:
                    wall[at - 3 : at - 2, :] = out[0, 0][7:8, :]
                    continue
                for c in range(COMP):
                    dst[c, at] = out[c, 0]


def inner_kernel(gas, kappa, strips, reaction, first, second, middle, one, two, edge):
    mix = coupling(reaction)
    strip_levels(strips, None, None, mix, edge, list(range(TILES)))
    for step, (src, dst) in enumerate(((gas, one), (one, two), (two, middle))):

        def body(x, carry, step=step, src=src, dst=dst):
            out = plane(src, kappa, edge, step, x, x, mix, TILES, range(COMP))
            into = x - 3 if step == ITERS - 1 else x
            for (c, t), value in out.items():
                dst[c, into, rows(t), :] = value
            return carry

        lax.fori_loop(step + 1, GX - 1 - step, body, 0, unroll=2)
    for c in range(COMP):
        for i, x in enumerate(SEAM):
            first[c, i] = one[c, x]
            second[c, i] = two[c, x + 1 if i < 2 else x - 1]


def outer_kernel(
    _, gas, kappa, strips, first, second, middle, recv_wall, recv_a, recv_rest, reaction, result, token, now, later, kap, edge
):
    token[...] = jnp.zeros((8, 128), jnp.float32)
    even = lax.rem(lax.axis_index("sect"), 2) == 0
    mix = coupling(reaction)
    split = GR - 8
    at_a, at_b = jnp.where(even, GX + 3, 0), jnp.where(even, 0, GX + 3)
    kappa_a, kappa_b = jnp.where(even, GX + 3, 1), jnp.where(even, 1, GX + 3)
    for c in range(COMP):
        for x in (0, 1, GX - 2, GX - 1):
            now[c, x + 3] = gas[c, x]
        for layer in range(3):
            now[c, at_a + layer] = recv_a[3 * c + layer]
            now[c, at_b + layer, split:, :] = recv_wall[3 * c + layer]
            now[c, at_b + layer, :split, :] = recv_rest[3 * c + layer]
        for i, x in enumerate(SEAM):
            later[c, x + 3] = first[c, i]
    for x in (0, 1, 2, GX - 3, GX - 2, GX - 1):
        kap[x + 3] = kappa[x]
    for layer in range(2):
        kap[kappa_a + layer] = recv_a[3 * COMP + layer]
        kap[kappa_b + layer, split:, :] = recv_wall[3 * COMP + layer]
        kap[kappa_b + layer, :split, :] = recv_rest[3 * COMP + layer]
    low, high = [], []
    for t in range(TILES):
        corner_a = recv_a[LAYERS - 1, rows(t), :]
        corner_b = recv_wall[LAYERS - 1 + t]
        low.append(jnp.where(even, corner_b, corner_a))
        high.append(jnp.where(even, corner_a, corner_b))
    strip_levels(strips, low, high, mix, edge, list(range(TILES)))
    for c in range(COMP):
        result[c, 3 : GX - 3] = middle[c]
    for step, (src, dst) in enumerate(((now, later), (later, now), (now, None))):
        if step == ITERS - 1:
            for c in range(COMP):
                for i, x in enumerate(SEAM):
                    now[c, (x + 1 if i < 2 else x - 1) + 3] = second[c, i]
        for i in range(3):
            for at in (step + 1 + i, GX + 2 - step + i):
                out = plane(src, kap, edge, step, at, at - 3, mix, TILES, range(COMP))
                for (c, t), value in out.items():
                    if step == ITERS - 1:
                        result[c, at - 3, rows(t), :] = value
                    else:
                        dst[c, at, rows(t), :] = value


def pack_kernel(hop, cell, particles, mixing, heating, _, packed, cells, spread, ordered, source, begin, end):
    lane = lanes()
    square = (128, 128)
    down, across = lax.broadcasted_iota(jnp.int32, square, 0), lanes(square)
    moves = hop[...]
    named = [moves == j for j in range(MOVES)]
    table = jnp.concatenate(
        [jnp.where(m, 1.0, 0.0) for m in named] + [jnp.zeros((128 - MOVES * CHUNKS, 128), jnp.float32)], axis=0
    )
    running = jnp.dot(table, jnp.where(down <= across, 1.0, 0.0), preferred_element_type=jnp.float32)
    count = jnp.dot(table, jnp.ones(square, jnp.float32), preferred_element_type=jnp.float32)
    before = jnp.where(((down >> 4) == (across >> 4)) & (across < down), 1.0, 0.0)
    base = jnp.dot(before, count, preferred_element_type=jnp.float32)
    offset = jnp.zeros((CHUNKS, 128), jnp.float32)
    place = jnp.zeros((CHUNKS, 128), jnp.float32)
    across16 = lanes((CHUNKS, 128))
    for j in range(MOVES):
        part = slice(CHUNKS * j, CHUNKS * (j + 1))
        place = jnp.where(named[j], offset + running[part] - 1.0, place)
        first = base[part].astype(jnp.int32)
        source[part, :] = (across16 + offset.astype(jnp.int32) - first) & 127
        begin[part, :] = across16 - first
        end[part, :] = across16 - first - count[part].astype(jnp.int32)
        offset = offset + count[part]
    own = lax.broadcasted_iota(jnp.int32, (VALS, VALS), 0) == lax.broadcasted_iota(jnp.int32, (VALS, VALS), 1)
    weights = 0.5 * mixing[...] + jnp.where(own, 1.0, 0.0)
    first_value = lax.broadcasted_iota(jnp.int32, (VALS, VALS), 1) == 0
    weights = weights - jnp.where(first_value, heating[...], 0.0)
    for v in range(VALS):
        spread[v] = jnp.broadcast_to(weights[:, v : v + 1], (VALS, 128))
    place = place.astype(jnp.int32)
    position = lane.astype(jnp.float32)
    for chunk in range(CHUNKS):
        part = slice(128 * chunk, 128 * (chunk + 1))
        total = spread[0] * particles[0:1, part]
        for v in range(1, VALS):
            total = total + spread[v] * particles[v : v + 1, part]
        hot = jnp.where(down == place[chunk : chunk + 1, :], 1.0, 0.0)
        order = lax.dot_general(position, hot, (((1,), (1,)), ((), ())), preferred_element_type=jnp.float32)
        order = order.astype(jnp.int32)
        ordered[chunk, 0:8, :] = pick(total[0:8], order)
        ordered[chunk, 8:16, :] = pick(total[8:16], order)
        ordered[chunk, 16:24, :] = pick(
            jnp.broadcast_to(cell[chunk : chunk + 1, :], (8, 128)).astype(jnp.float32), order
        )

    def block(j, carry):
        held = [[jnp.zeros((8, 128), jnp.float32)] * 2 + [jnp.full((8, 128), -1.0)] for _ in range(SPOTS)]
        for chunk in range(CHUNKS):
            row = pl.ds(CHUNKS * j + chunk, 1)
            index = jnp.broadcast_to(source[row, :], (8, 128))
            parts = [pick(ordered[chunk, rows(n), :], index) for n in range(3)]
            start = jnp.broadcast_to(begin[row, :], (8, 128))
            stop = jnp.broadcast_to(end[row, :], (8, 128))
            for spot in range(SPOTS):
                here = (start >= -128 * spot) & (stop < -128 * spot)
                held[spot] = [jnp.where(here, new, old) for new, old in zip(parts, held[spot])]
        for spot in range(SPOTS):
            part = slice(128 * spot, 128 * (spot + 1))
            packed[j, 0:8, part] = held[spot][0]
            packed[j, 8:16, part] = held[spot][1]
            cells[j, spot : spot + 1, :] = held[spot][2][0:1, :].astype(jnp.int32)
        return carry

    lax.fori_loop(0, MOVES, block, 0)


def moves_of_swaps():
    tile = lax.axis_index("blk")
    odd, late = lax.rem(tile, 2), lax.rem(tile, 4) >> 1
    return [REACH - 1 + 2 * odd, 2 * REACH * late, 2 * REACH * (1 - late), REACH + 1 - 2 * odd]


def heat_kernel(wall, earlier, packed, cells, heating, own, send_q, send_s, send_r, send_p, look):
    flux = 0.5 * (wall[...] + earlier[...])
    heat = jnp.broadcast_to(heating[...], (VALS, 128))
    for j in range(MOVES):
        where_to = cells[j]
        row, column = where_to >> 7, where_to & 127
        found = jnp.zeros((8, 128), jnp.float32)
        for x in range(GX):
            line = jnp.broadcast_to(flux[x : x + 1, :], (8, 128))
            found = jnp.where(row == x, pick(line, column), found)
        look[j] = found
    for out, j in zip((own, send_q, send_s, send_r, send_p), [REACH] + moves_of_swaps()):
        for spot in range(SPOTS):
            part = slice(128 * spot, 128 * (spot + 1))
            out[:, part] = packed[j, :, part] + heat * look[j, spot : spot + 1, :]


def join_kernel(own, recv_q, recv_s, recv_r, recv_p, _, out, done):
    copies = []
    for n, (piece, j) in enumerate(zip((own, recv_q, recv_s, recv_r, recv_p), [REACH] + moves_of_swaps())):
        place = pl.multiple_of((2 * REACH - j) * CAP, CAP)
        copies.append(pltpu.make_async_copy(piece, out.at[:, pl.ds(place, CAP)], done.at[n]))
    for copy in copies:
        copy.start()
    for copy in copies:
        copy.wait()


def swap(x, axis, pairs):
    return lax.ppermute(x, axis, pairs + [(j, i) for i, j in pairs])


def local(gas, kappa, reaction, particles, mixing, heating, wall_cell, tile_hop):
    sections, tiles = lax.axis_size("sect"), lax.axis_size("blk")
    pairs_a = [(i, i + 1) for i in range(0, sections, 2)]
    pairs_b = [(i, i + 1) for i in range(1, sections - 1, 2)]
    pairs_q = [(i, (i + 1) % tiles) for i in range(1, tiles, 2)]
    pairs_p = [(i, i + 1) for i in range(0, tiles, 2)]
    pairs_s = [(i, (i + 2) % tiles) for i in range(tiles) if i % 4 >= 2]
    pairs_r = [(i, i + 2) for i in range(tiles) if i % 4 < 2]

    send_q, send_p = call(
        edges_kernel,
        (f32(3, GR, GA), f32(3, GR, GA)),
        scratch=[pltpu.VMEM((COMP + 1, GX, GR, GA), jnp.float32), pltpu.SemaphoreType.DMA((COMP + 1,))],
        specs=[HBM] * 2,
        moved=2 << 20,
        limit=53.75,
    )(gas, kappa)
    recv_q = swap(send_q, "blk", pairs_q)
    recv_p = swap(send_p, "blk", pairs_p)
    heating_column = heating.reshape(VALS, 1)
    packed, cells = call(
        pack_kernel,
        (f32(MOVES, VALS, CAP), i32(MOVES, SPOTS, 128)),
        scratch=[
            pltpu.VMEM((VALS, VALS, 128), jnp.float32),
            pltpu.VMEM((CHUNKS, 24, 128), jnp.float32),
            pltpu.VMEM((MOVES * CHUNKS, 128), jnp.int32),
            pltpu.VMEM((MOVES * CHUNKS, 128), jnp.int32),
            pltpu.VMEM((MOVES * CHUNKS, 128), jnp.int32),
        ],
        specs=[VMEM] * 5 + [ANY],
        moved=4 << 20,
    )(tile_hop.reshape(CHUNKS, 128), wall_cell.reshape(CHUNKS, 128), particles, mixing, heating_column, send_p)

    send_a, send_wall = call(
        sends_kernel,
        (f32(LAYERS, GR, GA), f32(LAYERS - 1 + TILES, 8, GA)),
        specs=[VMEM] * 6 + [ANY],
        moved=2 << 20,
    )(gas, kappa, send_q, send_p, recv_q, recv_p, cells)
    recv_wall = swap(send_wall, "sect", pairs_b)
    recv_a = swap(send_a, "sect", pairs_a)

    strips = call(strips_kernel, f32(len(STRIPS), GR, GA), specs=[VMEM] * 4 + [ANY], moved=1 << 20)(
        send_q, send_p, recv_q, recv_p, send_a
    )

    whole = f32(COMP, GX, GR, GA)
    first, second, middle = call(
        inner_kernel,
        (f32(COMP, len(SEAM), GR, GA), f32(COMP, len(SEAM), GR, GA), f32(COMP, GX - 6, GR, GA)),
        scratch=[
            pltpu.VMEM((COMP, GX, GR, GA), jnp.float32),
            pltpu.VMEM((COMP, GX, GR, GA), jnp.float32),
            pltpu.VMEM((ITERS, COMP, GR, GA), jnp.float32),
        ],
        specs=[VMEM] * 3 + [SMEM],
        moved=12 << 20,
    )(gas, kappa, strips, reaction)

    send_rest = call(rest_kernel, f32(LAYERS - 1, GR - 8, GA), specs=[VMEM] * 2 + [ANY], moved=1 << 18)(gas, kappa, middle)
    recv_rest = swap(send_rest, "sect", pairs_b)

    wall = call(
        wall_kernel,
        f32(GX, GA),
        scratch=[
            pltpu.VMEM((COMP, EXT, 8, GA), jnp.float32),
            pltpu.VMEM((COMP, EXT, 8, GA), jnp.float32),
            pltpu.VMEM((EXT, 8, GA), jnp.float32),
            pltpu.VMEM((ITERS, COMP, 8, GA), jnp.float32),
        ],
        specs=[VMEM] * 8 + [SMEM, ANY],
        moved=4 << 20,
    )(gas, kappa, strips, recv_wall, recv_a, first, second, middle, reaction, send_rest)
    earlier = lax.ppermute(wall, "sect", [(i, i + 1) for i in range(sections - 1)])

    own, *sends = call(
        heat_kernel,
        (f32(VALS, CAP),) * MOVES,
        scratch=[pltpu.VMEM((MOVES, SPOTS, 128), jnp.float32)],
        specs=[VMEM] * 5,
        moved=2 << 20,
        flops=1 << 34,
    )(wall, earlier, packed, cells, heating_column)
    pieces = [swap(x, "blk", pairs) for x, pairs in zip(sends, (pairs_q, pairs_s, pairs_r, pairs_p))]

    field, token = call(
        outer_kernel,
        (whole, f32(8, 128)),
        scratch=[
            pltpu.VMEM((COMP, EXT, GR, GA), jnp.float32),
            pltpu.VMEM((COMP, EXT, GR, GA), jnp.float32),
            pltpu.VMEM((EXT, GR, GA), jnp.float32),
            pltpu.VMEM((ITERS, COMP, GR, GA), jnp.float32),
        ],
        specs=[ANY] + [VMEM] * 9 + [SMEM],
        moved=8 << 20,
    )(pieces[0], gas, kappa, strips, first, second, middle, recv_wall, recv_a, recv_rest, reaction)
    arrived = call(
        join_kernel,
        f32(VALS, MOVES * CAP),
        scratch=[pltpu.SemaphoreType.DMA((MOVES,))],
        specs=[VMEM] * MOVES + [ANY],
        out_specs=HBM,
        moved=1 << 20,
    )(own, *pieces, token)
    return field, arrived


def solution(mesh):
    in_specs = (
        P(None, "sect", None, "blk"),
        P("sect", None, "blk"),
        P(),
        P(None, ("sect", "blk")),
        P(),
        P(),
        P(("sect", "blk")),
        P(("sect", "blk"), None),
    )
    out_specs = (P(None, "sect", None, "blk"), P(None, ("sect", "blk")))
    return jax.shard_map(local, mesh=mesh, in_specs=in_specs, out_specs=out_specs, check_vma=False)
```

```python
import jax
import jax.numpy as jnp
from jax import lax
from jax.experimental import pallas as pl
from jax.experimental.pallas import tpu as pltpu
from jax.sharding import PartitionSpec as P

REACH = 2
MOVES = 2 * REACH + 1
ITERS = 3
DIFFUSE = (1.0, 0.8, 0.6, 0.9, 0.7)
COMP = 5
GX = 16
GR = 32
GA = 128
TILES = GR // 8
EXT = GX + 2 * ITERS
CHUNKS = 16
VALS = 16
CAP = 1024
SPOTS = CAP // 128

FIELD_COLUMNS = (3, 2, 1, 0, -1)
KAPPA_COLUMNS = (2, 1, 0)
STRIPS = [(c, k) for c in range(COMP) for k in FIELD_COLUMNS] + [(COMP, k) for k in KAPPA_COLUMNS]
STRIP_AT = {key: i for i, key in enumerate(STRIPS)}
CORNERS = [(c, 1) for c in range(COMP)] + [(c, 2) for c in range(COMP)] + [(COMP, 1)] + [(c, 0) for c in range(COMP)]
LAYERS = 3 * COMP + 2 + 1
SEAM = (1, 2, GX - 3, GX - 2)

VMEM = pl.BlockSpec(memory_space=pltpu.VMEM)
SMEM = pl.BlockSpec(memory_space=pltpu.SMEM)
ANY = pl.BlockSpec(memory_space=pl.ANY)
HBM = pl.BlockSpec(memory_space=pltpu.HBM)


def f32(*shape):
    return jax.ShapeDtypeStruct(shape, jnp.float32)


def i32(*shape):
    return jax.ShapeDtypeStruct(shape, jnp.int32)


def lanes(shape=(8, 128)):
    return lax.broadcasted_iota(jnp.int32, shape, len(shape) - 1)


def pick(x, index):
    return jnp.take_along_axis(x, index, axis=1, mode="promise_in_bounds")


def rows(tile):
    return slice(8 * tile, 8 * tile + 8)


def call(kernel, outs, scratch=(), specs=None, out_specs=None, flops=0, moved=0, limit=16):
    return pl.pallas_call(
        kernel,
        out_shape=outs,
        in_specs=specs,
        out_specs=jax.tree.map(lambda _: VMEM, outs) if out_specs is None else out_specs,
        scratch_shapes=list(scratch),
        cost_estimate=pl.CostEstimate(flops=flops, bytes_accessed=moved, transcendentals=0),
        compiler_params=pltpu.CompilerParams(vmem_limit_bytes=int(limit * 2**20)),
    )


def edges_kernel(gas, kappa, send_q, send_p, held, arrived):
    copies = [pltpu.make_async_copy(gas.at[q], held.at[q], arrived.at[q]) for q in range(COMP)]
    copies.append(pltpu.make_async_copy(kappa, held.at[COMP], arrived.at[COMP]))
    for copy in copies:
        copy.start()
    lane = lanes()
    within = lane & 63
    depth, cell = within >> 4, within & 15
    high = jnp.maximum(6 * cell + 2 - depth, 0)
    low = 6 * cell + 3 + depth
    odd = lax.rem(lax.axis_index("blk"), 2) == 1
    index_q, index_p = jnp.where(odd, high, low), jnp.where(odd, low, high)
    for pair in range((COMP + 1) // 2):
        packed = {}
        for q in (2 * pair, 2 * pair + 1):
            copies[q].wait()
            for tile in range(TILES):
                total = jnp.zeros((8, 128), jnp.float32)
                for x in range(GX):
                    here = (lane >= 6 * x) & (lane < 6 * x + 6)
                    total = jnp.where(here, pltpu.roll(held[q, x, rows(tile), :], 6 * x + 3, 1), total)
                packed[q, tile] = total
        for tile in range(TILES):
            first, second = packed[2 * pair, tile], packed[2 * pair + 1, tile]
            for out, index in ((send_q, index_q), (send_p, index_p)):
                out[pair, rows(tile), :] = jnp.where(lane < 64, pick(first, index), pick(second, index))


def strips_kernel(gas, kappa, send_q, send_p, recv_q, recv_p, _, strips, send_a, send_wall):
    lane = lanes()
    low_side = (lane & 1) == 1
    cell = jnp.clip((lane >> 1) - 3, 0, GX - 1)
    even = lax.rem(lax.axis_index("sect"), 2) == 0
    odd_tile = lax.rem(lax.axis_index("blk"), 2) == 1
    for tile in range(TILES):
        held = {}
        slabs = [[ref[s, rows(tile), :] for s in range(3)] for ref in (send_q, send_p, recv_q, recv_p)]
        own_q, own_p, got_q, got_p = slabs
        to_left = [jnp.where(odd_tile, p, q) for q, p in zip(own_q, own_p)]
        to_right = [jnp.where(odd_tile, q, p) for q, p in zip(own_q, own_p)]
        from_left = [jnp.where(odd_tile, p, q) for q, p in zip(got_q, got_p)]
        from_right = [jnp.where(odd_tile, q, p) for q, p in zip(got_q, got_p)]
        for q, k in STRIPS:
            depth = k - 1 if k > 0 else -k
            index = cell + ((q % 2) * 64 + depth * 16)
            low, high = (from_left, from_right) if k > 0 else (to_left, to_right)
            value = jnp.where(low_side, pick(low[q // 2], index), pick(high[q // 2], index))
            strips[STRIP_AT[q, k], rows(tile), :] = value
            held[q, k] = value
        top = jnp.zeros((8, 128), jnp.float32)
        bottom = top
        for i, key in enumerate(CORNERS):
            here = (lane >> 2) == i
            top = jnp.where(here, pltpu.roll(held[key], (4 * i - 34) % 128, 1), top)
            bottom = jnp.where(here, pltpu.roll(held[key], (4 * i - 6) % 128, 1), bottom)
        for_a = jnp.where(even, top, bottom)
        for_b = jnp.where(even, bottom, top)
        send_a[LAYERS - 1, rows(tile), :] = for_a
        send_wall[LAYERS - 1 + tile] = for_b
    at_a, at_b = jnp.where(even, GX - 3, 0), jnp.where(even, 0, GX - 3)
    kappa_a, kappa_b = jnp.where(even, GX - 2, 0), jnp.where(even, 0, GX - 2)
    for c in range(COMP):
        for layer in range(3):
            send_a[3 * c + layer] = gas[c, at_a + layer]
            send_wall[3 * c + layer] = gas[c, at_b + layer, GR - 8 :, :]
    for layer in range(2):
        send_a[3 * COMP + layer] = kappa[kappa_a + layer]
        send_wall[3 * COMP + layer] = kappa[kappa_b + layer, GR - 8 :, :]


def rest_kernel(gas, kappa, _, send_rest):
    even = lax.rem(lax.axis_index("sect"), 2) == 0
    split = GR - 8
    from_b, from_kappa = jnp.where(even, 0, GX - 3), jnp.where(even, 0, GX - 2)
    for c in range(COMP):
        for layer in range(3):
            send_rest[3 * c + layer] = gas[c, from_b + layer, :split, :]
    for layer in range(2):
        send_rest[3 * COMP + layer] = kappa[from_kappa + layer, :split, :]


def coupling(reaction):
    return [[0.3 * reaction[c, d] + (1.0 if c == d else 0.0) for d in range(COMP)] for c in range(COMP)]


def updated(c, values, neighbours, kappa, mix):
    total = mix[c][0] * values[0]
    for d in range(1, COMP):
        total = total + mix[c][d] * values[d]
    rate = kappa if DIFFUSE[c] == 1.0 else DIFFUSE[c] * kappa
    return total + rate * (neighbours - 6.0 * values[c])


def radial_sum(tiles, wall_only):
    sub = lax.broadcasted_iota(jnp.int32, (8, 128), 0)
    down = [pltpu.roll(t, 1, 0) for t in tiles]
    up = [pltpu.roll(t, 7, 0) for t in tiles]
    last = len(tiles) - 1
    sums = []
    for i, t in enumerate(tiles):
        if wall_only:
            below = down[i]
        else:
            below = jnp.where(sub == 0, down[i - 1] if i > 0 else t, down[i])
        above = jnp.where(sub == 7, up[i + 1] if i < last else t, up[i])
        sums.append(below + above)
    return sums


def radial_sum_of(src, c, at, values):
    sub = lax.broadcasted_iota(jnp.int32, (8, 128), 0)
    sums = []
    for t in range(TILES):
        first, last = t == 0, t == TILES - 1
        below = jnp.where(sub == 0, values[t], pltpu.roll(values[t], 1, 0)) if first else src[c, at, 8 * t - 1 : 8 * t + 7, :]
        above = jnp.where(sub == 7, values[t], pltpu.roll(values[t], 7, 0)) if last else src[c, at, 8 * t + 1 : 8 * t + 9, :]
        sums.append(below + above)
    return sums


def strip_levels(strips, low_corner, high_corner, mix, edge, tiles):
    lane = lanes()
    wall_only = len(tiles) == 1
    from_low = (lane >= 2) & (lane < 6)
    from_high = (lane >= 38) & (lane < 42)
    held = {}
    for key in STRIPS:
        held[key] = [strips[STRIP_AT[key], rows(t), :] for t in tiles]
    for i, key in enumerate(CORNERS if low_corner else ()):
        for n in range(len(tiles)):
            value = jnp.where(from_low, pltpu.roll(low_corner[n], (2 - 4 * i) % 128, 1), held[key][n])
            held[key][n] = jnp.where(from_high, pltpu.roll(high_corner[n], (38 - 4 * i) % 128, 1), value)
    for step in range(ITERS):
        for c in range(COMP):
            for n in range(len(tiles)):
                edge[step, c, rows(n), :] = held[c, 1][n]
        if step == ITERS - 1:
            break
        later = {}
        for k in (2, 1, 0) if step == 0 else (1,):
            for c in range(COMP):
                radial = radial_sum(held[c, k], wall_only)
                later[c, k] = []
                for n in range(len(tiles)):
                    value = held[c, k][n]
                    around = held[c, k + 1][n] + held[c, k - 1][n]
                    around = around + pltpu.roll(value, 2, 1) + pltpu.roll(value, 126, 1) + radial[n]
                    later[c, k].append(updated(c, [held[d, k][n] for d in range(COMP)], around, held[COMP, k][n], mix))
        for key in [key for key in held if key[0] == COMP]:
            later[key] = held[key]
        held = later


def plane(src, kappa, edge, step, at, x, mix, count, comps):
    lane = lanes()
    first, last = lane == 0, lane == 127
    shift = 121 - 2 * x
    values = [[src[c, at, rows(t), :] for t in range(count)] for c in range(COMP)]
    kap = [kappa[at, rows(t), :] for t in range(count)]
    out = {}
    for c in comps:
        radial = radial_sum(values[c], True) if count == 1 else radial_sum_of(src, c, at, values[c])
        for t in range(count):
            value = values[c][t]
            beyond = pltpu.roll(edge[step, c, rows(t), :], shift, 1)
            around = src[c, at - 1, rows(t), :] + src[c, at + 1, rows(t), :] + radial[t]
            around = around + jnp.where(first, beyond, pltpu.roll(value, 1, 1))
            around = around + jnp.where(last, beyond, pltpu.roll(value, 127, 1))
            out[c, t] = updated(c, [values[d][t] for d in range(COMP)], around, kap[t], mix)
    return out


def wall_kernel(
    gas, kappa, strips, recv_wall, recv_a, first, second, middle, reaction, _, wall, now, later, kap, edge
):
    even = lax.rem(lax.axis_index("sect"), 2) == 0
    mix = coupling(reaction)
    top = slice(GR - 8, GR)
    at_a, at_b = jnp.where(even, GX + 3, 0), jnp.where(even, 0, GX + 3)
    kappa_a, kappa_b = jnp.where(even, GX + 3, 1), jnp.where(even, 1, GX + 3)
    for c in range(COMP):
        for x in (0, 1, GX - 2, GX - 1):
            now[c, x + 3] = gas[c, x, top, :]
        for layer in range(3):
            now[c, at_a + layer] = recv_a[3 * c + layer, top, :]
            now[c, at_b + layer] = recv_wall[3 * c + layer]
        for i, x in enumerate(SEAM):
            later[c, x + 3] = first[c, i, top, :]
    for x in (0, 1, 2, GX - 3, GX - 2, GX - 1):
        kap[x + 3] = kappa[x, top, :]
    for layer in range(2):
        kap[kappa_a + layer] = recv_a[3 * COMP + layer, top, :]
        kap[kappa_b + layer] = recv_wall[3 * COMP + layer]
    corner_a, corner_b = recv_a[LAYERS - 1, top, :], recv_wall[LAYERS - 1 + TILES - 1]
    low, high = jnp.where(even, corner_b, corner_a), jnp.where(even, corner_a, corner_b)
    strip_levels(strips, [low], [high], mix, edge, [TILES - 1])
    wall[3 : GX - 3, :] = middle[0, :, GR - 1, :]
    for step, (src, dst) in enumerate(((now, later), (later, now), (now, None))):
        last = step == ITERS - 1
        if last:
            for c in range(COMP):
                for i, x in enumerate(SEAM):
                    now[c, (x + 1 if i < 2 else x - 1) + 3] = second[c, i, top, :]
        for i in range(3):
            for at in (step + 1 + i, GX + 2 - step + i):
                out = plane(src, kap, edge, step, at, at - 3, mix, 1, (0,) if last else range(COMP))
                if last:
                    wall[at - 3 : at - 2, :] = out[0, 0][7:8, :]
                    continue
                for c in range(COMP):
                    dst[c, at] = out[c, 0]


def inner_kernel(gas, kappa, strips, reaction, first, second, middle, one, two, edge):
    mix = coupling(reaction)
    strip_levels(strips, None, None, mix, edge, list(range(TILES)))
    for step, (src, dst) in enumerate(((gas, one), (one, two), (two, middle))):

        def body(x, carry, step=step, src=src, dst=dst):
            out = plane(src, kappa, edge, step, x, x, mix, TILES, range(COMP))
            into = x - 3 if step == ITERS - 1 else x
            for (c, t), value in out.items():
                dst[c, into, rows(t), :] = value
            return carry

        lax.fori_loop(step + 1, GX - 1 - step, body, 0, unroll=2)
    for c in range(COMP):
        for i, x in enumerate(SEAM):
            first[c, i] = one[c, x]
            second[c, i] = two[c, x + 1 if i < 2 else x - 1]


def outer_kernel(
    _, gas, kappa, strips, first, second, middle, recv_wall, recv_a, recv_rest, reaction, result, token, now, later, kap, edge
):
    token[...] = jnp.zeros((8, 128), jnp.float32)
    even = lax.rem(lax.axis_index("sect"), 2) == 0
    mix = coupling(reaction)
    split = GR - 8
    at_a, at_b = jnp.where(even, GX + 3, 0), jnp.where(even, 0, GX + 3)
    kappa_a, kappa_b = jnp.where(even, GX + 3, 1), jnp.where(even, 1, GX + 3)
    for c in range(COMP):
        for x in (0, 1, GX - 2, GX - 1):
            now[c, x + 3] = gas[c, x]
        for layer in range(3):
            now[c, at_a + layer] = recv_a[3 * c + layer]
            now[c, at_b + layer, split:, :] = recv_wall[3 * c + layer]
            now[c, at_b + layer, :split, :] = recv_rest[3 * c + layer]
        for i, x in enumerate(SEAM):
            later[c, x + 3] = first[c, i]
    for x in (0, 1, 2, GX - 3, GX - 2, GX - 1):
        kap[x + 3] = kappa[x]
    for layer in range(2):
        kap[kappa_a + layer] = recv_a[3 * COMP + layer]
        kap[kappa_b + layer, split:, :] = recv_wall[3 * COMP + layer]
        kap[kappa_b + layer, :split, :] = recv_rest[3 * COMP + layer]
    low, high = [], []
    for t in range(TILES):
        corner_a = recv_a[LAYERS - 1, rows(t), :]
        corner_b = recv_wall[LAYERS - 1 + t]
        low.append(jnp.where(even, corner_b, corner_a))
        high.append(jnp.where(even, corner_a, corner_b))
    strip_levels(strips, low, high, mix, edge, list(range(TILES)))
    for c in range(COMP):
        result[c, 3 : GX - 3] = middle[c]
    for step, (src, dst) in enumerate(((now, later), (later, now), (now, None))):
        if step == ITERS - 1:
            for c in range(COMP):
                for i, x in enumerate(SEAM):
                    now[c, (x + 1 if i < 2 else x - 1) + 3] = second[c, i]
        for i in range(3):
            for at in (step + 1 + i, GX + 2 - step + i):
                out = plane(src, kap, edge, step, at, at - 3, mix, TILES, range(COMP))
                for (c, t), value in out.items():
                    if step == ITERS - 1:
                        result[c, at - 3, rows(t), :] = value
                    else:
                        dst[c, at, rows(t), :] = value


def pack_kernel(hop, cell, particles, mixing, heating, _, packed, cells, spread, ordered, source, begin, end):
    lane = lanes()
    square = (128, 128)
    down, across = lax.broadcasted_iota(jnp.int32, square, 0), lanes(square)
    moves = hop[...]
    named = [moves == j for j in range(MOVES)]
    table = jnp.concatenate(
        [jnp.where(m, 1.0, 0.0) for m in named] + [jnp.zeros((128 - MOVES * CHUNKS, 128), jnp.float32)], axis=0
    )
    running = jnp.dot(table, jnp.where(down <= across, 1.0, 0.0), preferred_element_type=jnp.float32)
    count = jnp.dot(table, jnp.ones(square, jnp.float32), preferred_element_type=jnp.float32)
    before = jnp.where(((down >> 4) == (across >> 4)) & (across < down), 1.0, 0.0)
    base = jnp.dot(before, count, preferred_element_type=jnp.float32)
    offset = jnp.zeros((CHUNKS, 128), jnp.float32)
    place = jnp.zeros((CHUNKS, 128), jnp.float32)
    across16 = lanes((CHUNKS, 128))
    for j in range(MOVES):
        part = slice(CHUNKS * j, CHUNKS * (j + 1))
        place = jnp.where(named[j], offset + running[part] - 1.0, place)
        first = base[part].astype(jnp.int32)
        source[part, :] = (across16 + offset.astype(jnp.int32) - first) & 127
        begin[part, :] = across16 - first
        end[part, :] = across16 - first - count[part].astype(jnp.int32)
        offset = offset + count[part]
    own = lax.broadcasted_iota(jnp.int32, (VALS, VALS), 0) == lax.broadcasted_iota(jnp.int32, (VALS, VALS), 1)
    weights = 0.5 * mixing[...] + jnp.where(own, 1.0, 0.0)
    first_value = lax.broadcasted_iota(jnp.int32, (VALS, VALS), 1) == 0
    weights = weights - jnp.where(first_value, heating[...], 0.0)
    for v in range(VALS):
        spread[v] = jnp.broadcast_to(weights[:, v : v + 1], (VALS, 128))
    place = place.astype(jnp.int32)
    position = lane.astype(jnp.float32)
    for chunk in range(CHUNKS):
        part = slice(128 * chunk, 128 * (chunk + 1))
        total = spread[0] * particles[0:1, part]
        for v in range(1, VALS):
            total = total + spread[v] * particles[v : v + 1, part]
        hot = jnp.where(down == place[chunk : chunk + 1, :], 1.0, 0.0)
        order = lax.dot_general(position, hot, (((1,), (1,)), ((), ())), preferred_element_type=jnp.float32)
        order = order.astype(jnp.int32)
        ordered[chunk, 0:8, :] = pick(total[0:8], order)
        ordered[chunk, 8:16, :] = pick(total[8:16], order)
        ordered[chunk, 16:24, :] = pick(
            jnp.broadcast_to(cell[chunk : chunk + 1, :], (8, 128)).astype(jnp.float32), order
        )

    def block(j, carry):
        held = [[jnp.zeros((8, 128), jnp.float32)] * 2 + [jnp.full((8, 128), -1.0)] for _ in range(SPOTS)]
        for chunk in range(CHUNKS):
            row = pl.ds(CHUNKS * j + chunk, 1)
            index = jnp.broadcast_to(source[row, :], (8, 128))
            parts = [pick(ordered[chunk, rows(n), :], index) for n in range(3)]
            start = jnp.broadcast_to(begin[row, :], (8, 128))
            stop = jnp.broadcast_to(end[row, :], (8, 128))
            for spot in range(SPOTS):
                here = (start >= -128 * spot) & (stop < -128 * spot)
                held[spot] = [jnp.where(here, new, old) for new, old in zip(parts, held[spot])]
        for spot in range(SPOTS):
            part = slice(128 * spot, 128 * (spot + 1))
            packed[j, 0:8, part] = held[spot][0]
            packed[j, 8:16, part] = held[spot][1]
            cells[j, spot : spot + 1, :] = held[spot][2][0:1, :].astype(jnp.int32)
        return carry

    lax.fori_loop(0, MOVES, block, 0)


def moves_of_swaps():
    tile = lax.axis_index("blk")
    odd, late = lax.rem(tile, 2), lax.rem(tile, 4) >> 1
    return [REACH - 1 + 2 * odd, 2 * REACH * late, 2 * REACH * (1 - late), REACH + 1 - 2 * odd]


def heat_kernel(wall, earlier, packed, cells, heating, own, send_q, send_s, send_r, send_p, look):
    flux = 0.5 * (wall[...] + earlier[...])
    heat = jnp.broadcast_to(heating[...], (VALS, 128))
    for j in range(MOVES):
        where_to = cells[j]
        row, column = where_to >> 7, where_to & 127
        found = jnp.zeros((8, 128), jnp.float32)
        for x in range(GX):
            line = jnp.broadcast_to(flux[x : x + 1, :], (8, 128))
            found = jnp.where(row == x, pick(line, column), found)
        look[j] = found
    for out, j in zip((own, send_q, send_s, send_r, send_p), [REACH] + moves_of_swaps()):
        for spot in range(SPOTS):
            part = slice(128 * spot, 128 * (spot + 1))
            out[:, part] = packed[j, :, part] + heat * look[j, spot : spot + 1, :]


def join_kernel(own, recv_q, recv_s, recv_r, recv_p, _, out, done):
    copies = []
    for n, (piece, j) in enumerate(zip((own, recv_q, recv_s, recv_r, recv_p), [REACH] + moves_of_swaps())):
        place = pl.multiple_of((2 * REACH - j) * CAP, CAP)
        copies.append(pltpu.make_async_copy(piece, out.at[:, pl.ds(place, CAP)], done.at[n]))
    for copy in copies:
        copy.start()
    for copy in copies:
        copy.wait()


def swap(x, axis, pairs):
    return lax.ppermute(x, axis, pairs + [(j, i) for i, j in pairs])


def local(gas, kappa, reaction, particles, mixing, heating, wall_cell, tile_hop):
    sections, tiles = lax.axis_size("sect"), lax.axis_size("blk")
    pairs_a = [(i, i + 1) for i in range(0, sections, 2)]
    pairs_b = [(i, i + 1) for i in range(1, sections - 1, 2)]
    pairs_q = [(i, (i + 1) % tiles) for i in range(1, tiles, 2)]
    pairs_p = [(i, i + 1) for i in range(0, tiles, 2)]
    pairs_s = [(i, (i + 2) % tiles) for i in range(tiles) if i % 4 >= 2]
    pairs_r = [(i, i + 2) for i in range(tiles) if i % 4 < 2]

    send_q, send_p = call(
        edges_kernel,
        (f32(3, GR, GA), f32(3, GR, GA)),
        scratch=[pltpu.VMEM((COMP + 1, GX, GR, GA), jnp.float32), pltpu.SemaphoreType.DMA((COMP + 1,))],
        specs=[HBM] * 2,
        moved=2 << 20,
        limit=53.75,
    )(gas, kappa)
    recv_q = swap(send_q, "blk", pairs_q)
    recv_p = swap(send_p, "blk", pairs_p)
    heating_column = heating.reshape(VALS, 1)
    packed, cells = call(
        pack_kernel,
        (f32(MOVES, VALS, CAP), i32(MOVES, SPOTS, 128)),
        scratch=[
            pltpu.VMEM((VALS, VALS, 128), jnp.float32),
            pltpu.VMEM((CHUNKS, 24, 128), jnp.float32),
            pltpu.VMEM((MOVES * CHUNKS, 128), jnp.int32),
            pltpu.VMEM((MOVES * CHUNKS, 128), jnp.int32),
            pltpu.VMEM((MOVES * CHUNKS, 128), jnp.int32),
        ],
        specs=[VMEM] * 5 + [ANY],
        moved=4 << 20,
    )(tile_hop.reshape(CHUNKS, 128), wall_cell.reshape(CHUNKS, 128), particles, mixing, heating_column, send_p)

    strips, send_a, send_wall = call(
        strips_kernel,
        (f32(len(STRIPS), GR, GA), f32(LAYERS, GR, GA), f32(LAYERS - 1 + TILES, 8, GA)),
        specs=[VMEM] * 6 + [ANY],
        moved=2 << 20,
    )(gas, kappa, send_q, send_p, recv_q, recv_p, cells)
    recv_wall = swap(send_wall, "sect", pairs_b)
    recv_a = swap(send_a, "sect", pairs_a)

    whole = f32(COMP, GX, GR, GA)
    first, second, middle = call(
        inner_kernel,
        (f32(COMP, len(SEAM), GR, GA), f32(COMP, len(SEAM), GR, GA), f32(COMP, GX - 6, GR, GA)),
        scratch=[
            pltpu.VMEM((COMP, GX, GR, GA), jnp.float32),
            pltpu.VMEM((COMP, GX, GR, GA), jnp.float32),
            pltpu.VMEM((ITERS, COMP, GR, GA), jnp.float32),
        ],
        specs=[VMEM] * 3 + [SMEM],
        moved=12 << 20,
    )(gas, kappa, strips, reaction)

    send_rest = call(rest_kernel, f32(LAYERS - 1, GR - 8, GA), specs=[VMEM] * 2 + [ANY], moved=1 << 18)(gas, kappa, middle)
    recv_rest = swap(send_rest, "sect", pairs_b)

    wall = call(
        wall_kernel,
        f32(GX, GA),
        scratch=[
            pltpu.VMEM((COMP, EXT, 8, GA), jnp.float32),
            pltpu.VMEM((COMP, EXT, 8, GA), jnp.float32),
            pltpu.VMEM((EXT, 8, GA), jnp.float32),
            pltpu.VMEM((ITERS, COMP, 8, GA), jnp.float32),
        ],
        specs=[VMEM] * 8 + [SMEM, ANY],
        moved=4 << 20,
    )(gas, kappa, strips, recv_wall, recv_a, first, second, middle, reaction, send_rest)
    earlier = lax.ppermute(wall, "sect", [(i, i + 1) for i in range(sections - 1)])

    own, *sends = call(
        heat_kernel,
        (f32(VALS, CAP),) * MOVES,
        scratch=[pltpu.VMEM((MOVES, SPOTS, 128), jnp.float32)],
        specs=[VMEM] * 5,
        moved=2 << 20,
        flops=1 << 34,
    )(wall, earlier, packed, cells, heating_column)
    pieces = [swap(x, "blk", pairs) for x, pairs in zip(sends, (pairs_q, pairs_s, pairs_r, pairs_p))]

    field, token = call(
        outer_kernel,
        (whole, f32(8, 128)),
        scratch=[
            pltpu.VMEM((COMP, EXT, GR, GA), jnp.float32),
            pltpu.VMEM((COMP, EXT, GR, GA), jnp.float32),
            pltpu.VMEM((EXT, GR, GA), jnp.float32),
            pltpu.VMEM((ITERS, COMP, GR, GA), jnp.float32),
        ],
        specs=[ANY] + [VMEM] * 9 + [SMEM],
        moved=8 << 20,
    )(pieces[0], gas, kappa, strips, first, second, middle, recv_wall, recv_a, recv_rest, reaction)
    arrived = call(
        join_kernel,
        f32(VALS, MOVES * CAP),
        scratch=[pltpu.SemaphoreType.DMA((MOVES,))],
        specs=[VMEM] * MOVES + [ANY],
        out_specs=HBM,
        moved=1 << 20,
    )(own, *pieces, token)
    return field, arrived


def solution(mesh):
    in_specs = (
        P(None, "sect", None, "blk"),
        P("sect", None, "blk"),
        P(),
        P(None, ("sect", "blk")),
        P(),
        P(),
        P(("sect", "blk")),
        P(("sect", "blk"), None),
    )
    out_specs = (P(None, "sect", None, "blk"), P(None, ("sect", "blk")))
    return jax.shard_map(local, mesh=mesh, in_specs=in_specs, out_specs=out_specs, check_vma=False)
```

```python
import jax
import jax.numpy as jnp
from jax import lax
from jax.experimental import pallas as pl
from jax.experimental.pallas import tpu as pltpu
from jax.sharding import PartitionSpec as P

REACH = 2
MOVES = 2 * REACH + 1
ITERS = 3
DIFFUSE = (1.0, 0.8, 0.6, 0.9, 0.7)
COMP = 5
GX = 16
GR = 32
GA = 128
TILES = GR // 8
EXT = GX + 2 * ITERS
CHUNKS = 16
VALS = 16
CAP = 1024
SPOTS = CAP // 128

FIELD_COLUMNS = (3, 2, 1, 0, -1)
KAPPA_COLUMNS = (2, 1, 0)
STRIPS = [(c, k) for c in range(COMP) for k in FIELD_COLUMNS] + [(COMP, k) for k in KAPPA_COLUMNS]
STRIP_AT = {key: i for i, key in enumerate(STRIPS)}
CORNERS = [(c, 1) for c in range(COMP)] + [(c, 2) for c in range(COMP)] + [(COMP, 1)] + [(c, 0) for c in range(COMP)]
LAYERS = 3 * COMP + 2 + 1
SEAM = (1, 2, GX - 3, GX - 2)

VMEM = pl.BlockSpec(memory_space=pltpu.VMEM)
SMEM = pl.BlockSpec(memory_space=pltpu.SMEM)
ANY = pl.BlockSpec(memory_space=pl.ANY)
HBM = pl.BlockSpec(memory_space=pltpu.HBM)


def f32(*shape):
    return jax.ShapeDtypeStruct(shape, jnp.float32)


def i32(*shape):
    return jax.ShapeDtypeStruct(shape, jnp.int32)


def lanes(shape=(8, 128)):
    return lax.broadcasted_iota(jnp.int32, shape, len(shape) - 1)


def pick(x, index):
    return jnp.take_along_axis(x, index, axis=1, mode="promise_in_bounds")


def rows(tile):
    return slice(8 * tile, 8 * tile + 8)


def call(kernel, outs, scratch=(), specs=None, out_specs=None, flops=0, moved=0, limit=16):
    return pl.pallas_call(
        kernel,
        out_shape=outs,
        in_specs=specs,
        out_specs=jax.tree.map(lambda _: VMEM, outs) if out_specs is None else out_specs,
        scratch_shapes=list(scratch),
        cost_estimate=pl.CostEstimate(flops=flops, bytes_accessed=moved, transcendentals=0),
        compiler_params=pltpu.CompilerParams(vmem_limit_bytes=int(limit * 2**20)),
    )


def edges_kernel(gas, kappa, send_q, send_p, held, arrived):
    copies = [pltpu.make_async_copy(gas.at[q], held.at[q], arrived.at[q]) for q in range(COMP)]
    copies.append(pltpu.make_async_copy(kappa, held.at[COMP], arrived.at[COMP]))
    for copy in copies:
        copy.start()
    lane = lanes()
    within = lane & 63
    depth, cell = within >> 4, within & 15
    high = jnp.maximum(6 * cell + 2 - depth, 0)
    low = 6 * cell + 3 + depth
    odd = lax.rem(lax.axis_index("blk"), 2) == 1
    index_q, index_p = jnp.where(odd, high, low), jnp.where(odd, low, high)
    for pair in range((COMP + 1) // 2):
        packed = {}
        for q in (2 * pair, 2 * pair + 1):
            copies[q].wait()
            for tile in range(TILES):
                total = jnp.zeros((8, 128), jnp.float32)
                for x in range(GX):
                    here = (lane >= 6 * x) & (lane < 6 * x + 6)
                    total = jnp.where(here, pltpu.roll(held[q, x, rows(tile), :], 6 * x + 3, 1), total)
                packed[q, tile] = total
        for tile in range(TILES):
            first, second = packed[2 * pair, tile], packed[2 * pair + 1, tile]
            for out, index in ((send_q, index_q), (send_p, index_p)):
                out[pair, rows(tile), :] = jnp.where(lane < 64, pick(first, index), pick(second, index))


def strips_kernel(gas, kappa, send_q, send_p, recv_q, recv_p, _, strips, send_a, send_wall):
    lane = lanes()
    low_side = (lane & 1) == 1
    cell = jnp.clip((lane >> 1) - 3, 0, GX - 1)
    even = lax.rem(lax.axis_index("sect"), 2) == 0
    odd_tile = lax.rem(lax.axis_index("blk"), 2) == 1
    for tile in range(TILES):
        held = {}
        slabs = [[ref[s, rows(tile), :] for s in range(3)] for ref in (send_q, send_p, recv_q, recv_p)]
        own_q, own_p, got_q, got_p = slabs
        to_left = [jnp.where(odd_tile, p, q) for q, p in zip(own_q, own_p)]
        to_right = [jnp.where(odd_tile, q, p) for q, p in zip(own_q, own_p)]
        from_left = [jnp.where(odd_tile, p, q) for q, p in zip(got_q, got_p)]
        from_right = [jnp.where(odd_tile, q, p) for q, p in zip(got_q, got_p)]
        for q, k in STRIPS:
            depth = k - 1 if k > 0 else -k
            index = cell + ((q % 2) * 64 + depth * 16)
            low, high = (from_left, from_right) if k > 0 else (to_left, to_right)
            value = jnp.where(low_side, pick(low[q // 2], index), pick(high[q // 2], index))
            strips[STRIP_AT[q, k], rows(tile), :] = value
            held[q, k] = value
        top = jnp.zeros((8, 128), jnp.float32)
        bottom = top
        for i, key in enumerate(CORNERS):
            here = (lane >> 2) == i
            top = jnp.where(here, pltpu.roll(held[key], (4 * i - 34) % 128, 1), top)
            bottom = jnp.where(here, pltpu.roll(held[key], (4 * i - 6) % 128, 1), bottom)
        for_a = jnp.where(even, top, bottom)
        for_b = jnp.where(even, bottom, top)
        send_a[LAYERS - 1, rows(tile), :] = for_a
        send_wall[LAYERS - 1 + tile] = for_b
    at_a, at_b = jnp.where(even, GX - 3, 0), jnp.where(even, 0, GX - 3)
    kappa_a, kappa_b = jnp.where(even, GX - 2, 0), jnp.where(even, 0, GX - 2)
    for c in range(COMP):
        for layer in range(3):
            send_a[3 * c + layer] = gas[c, at_a + layer]
            send_wall[3 * c + layer] = gas[c, at_b + layer, GR - 8 :, :]
    for layer in range(2):
        send_a[3 * COMP + layer] = kappa[kappa_a + layer]
        send_wall[3 * COMP + layer] = kappa[kappa_b + layer, GR - 8 :, :]


def rest_kernel(gas, kappa, _, send_rest):
    even = lax.rem(lax.axis_index("sect"), 2) == 0
    split = GR - 8
    from_b, from_kappa = jnp.where(even, 0, GX - 3), jnp.where(even, 0, GX - 2)
    for c in range(COMP):
        for layer in range(3):
            send_rest[3 * c + layer] = gas[c, from_b + layer, :split, :]
    for layer in range(2):
        send_rest[3 * COMP + layer] = kappa[from_kappa + layer, :split, :]


def coupling(reaction):
    return [[0.3 * reaction[c, d] + (1.0 if c == d else 0.0) for d in range(COMP)] for c in range(COMP)]


def updated(c, values, neighbours, kappa, mix):
    total = mix[c][0] * values[0]
    for d in range(1, COMP):
        total = total + mix[c][d] * values[d]
    rate = kappa if DIFFUSE[c] == 1.0 else DIFFUSE[c] * kappa
    return total + rate * (neighbours - 6.0 * values[c])


def radial_sum(tiles, wall_only):
    sub = lax.broadcasted_iota(jnp.int32, (8, 128), 0)
    down = [pltpu.roll(t, 1, 0) for t in tiles]
    up = [pltpu.roll(t, 7, 0) for t in tiles]
    last = len(tiles) - 1
    sums = []
    for i, t in enumerate(tiles):
        if wall_only:
            below = down[i]
        else:
            below = jnp.where(sub == 0, down[i - 1] if i > 0 else t, down[i])
        above = jnp.where(sub == 7, up[i + 1] if i < last else t, up[i])
        sums.append(below + above)
    return sums


def radial_sum_of(src, c, at, values):
    sub = lax.broadcasted_iota(jnp.int32, (8, 128), 0)
    sums = []
    for t in range(TILES):
        first, last = t == 0, t == TILES - 1
        below = jnp.where(sub == 0, values[t], pltpu.roll(values[t], 1, 0)) if first else src[c, at, 8 * t - 1 : 8 * t + 7, :]
        above = jnp.where(sub == 7, values[t], pltpu.roll(values[t], 7, 0)) if last else src[c, at, 8 * t + 1 : 8 * t + 9, :]
        sums.append(below + above)
    return sums


def strip_levels(strips, low_corner, high_corner, mix, edge, tiles):
    lane = lanes()
    wall_only = len(tiles) == 1
    from_low = (lane >= 2) & (lane < 6)
    from_high = (lane >= 38) & (lane < 42)
    held = {}
    for key in STRIPS:
        held[key] = [strips[STRIP_AT[key], rows(t), :] for t in tiles]
    for i, key in enumerate(CORNERS if low_corner else ()):
        for n in range(len(tiles)):
            value = jnp.where(from_low, pltpu.roll(low_corner[n], (2 - 4 * i) % 128, 1), held[key][n])
            held[key][n] = jnp.where(from_high, pltpu.roll(high_corner[n], (38 - 4 * i) % 128, 1), value)
    for step in range(ITERS):
        for c in range(COMP):
            for n in range(len(tiles)):
                edge[step, c, rows(n), :] = held[c, 1][n]
        if step == ITERS - 1:
            break
        later = {}
        for k in (2, 1, 0) if step == 0 else (1,):
            for c in range(COMP):
                radial = radial_sum(held[c, k], wall_only)
                later[c, k] = []
                for n in range(len(tiles)):
                    value = held[c, k][n]
                    around = held[c, k + 1][n] + held[c, k - 1][n]
                    around = around + pltpu.roll(value, 2, 1) + pltpu.roll(value, 126, 1) + radial[n]
                    later[c, k].append(updated(c, [held[d, k][n] for d in range(COMP)], around, held[COMP, k][n], mix))
        for key in [key for key in held if key[0] == COMP]:
            later[key] = held[key]
        held = later


def plane(src, kappa, edge, step, at, x, mix, count, comps):
    lane = lanes()
    first, last = lane == 0, lane == 127
    shift = 121 - 2 * x
    values = [[src[c, at, rows(t), :] for t in range(count)] for c in range(COMP)]
    kap = [kappa[at, rows(t), :] for t in range(count)]
    out = {}
    for c in comps:
        radial = radial_sum(values[c], True) if count == 1 else radial_sum_of(src, c, at, values[c])
        for t in range(count):
            value = values[c][t]
            beyond = pltpu.roll(edge[step, c, rows(t), :], shift, 1)
            around = src[c, at - 1, rows(t), :] + src[c, at + 1, rows(t), :] + radial[t]
            around = around + jnp.where(first, beyond, pltpu.roll(value, 1, 1))
            around = around + jnp.where(last, beyond, pltpu.roll(value, 127, 1))
            out[c, t] = updated(c, [values[d][t] for d in range(COMP)], around, kap[t], mix)
    return out


def wall_kernel(
    gas, kappa, strips, recv_wall, recv_a, first, second, middle, reaction, _, wall, now, later, kap, edge
):
    even = lax.rem(lax.axis_index("sect"), 2) == 0
    mix = coupling(reaction)
    top = slice(GR - 8, GR)
    at_a, at_b = jnp.where(even, GX + 3, 0), jnp.where(even, 0, GX + 3)
    kappa_a, kappa_b = jnp.where(even, GX + 3, 1), jnp.where(even, 1, GX + 3)
    for c in range(COMP):
        for x in (0, 1, GX - 2, GX - 1):
            now[c, x + 3] = gas[c, x, top, :]
        for layer in range(3):
            now[c, at_a + layer] = recv_a[3 * c + layer, top, :]
            now[c, at_b + layer] = recv_wall[3 * c + layer]
        for i, x in enumerate(SEAM):
            later[c, x + 3] = first[c, i, top, :]
    for x in (0, 1, 2, GX - 3, GX - 2, GX - 1):
        kap[x + 3] = kappa[x, top, :]
    for layer in range(2):
        kap[kappa_a + layer] = recv_a[3 * COMP + layer, top, :]
        kap[kappa_b + layer] = recv_wall[3 * COMP + layer]
    corner_a, corner_b = recv_a[LAYERS - 1, top, :], recv_wall[LAYERS - 1 + TILES - 1]
    low, high = jnp.where(even, corner_b, corner_a), jnp.where(even, corner_a, corner_b)
    strip_levels(strips, [low], [high], mix, edge, [TILES - 1])
    wall[3 : GX - 3, :] = middle[0, :, GR - 1, :]
    for step, (src, dst) in enumerate(((now, later), (later, now), (now, None))):
        last = step == ITERS - 1
        if last:
            for c in range(COMP):
                for i, x in enumerate(SEAM):
                    now[c, (x + 1 if i < 2 else x - 1) + 3] = second[c, i, top, :]
        for i in range(3):
            for at in (step + 1 + i, GX + 2 - step + i):
                out = plane(src, kap, edge, step, at, at - 3, mix, 1, (0,) if last else range(COMP))
                if last:
                    wall[at - 3 : at - 2, :] = out[0, 0][7:8, :]
                    continue
                for c in range(COMP):
                    dst[c, at] = out[c, 0]


def inner_kernel(gas, kappa, strips, reaction, first, second, middle, one, two, edge):
    mix = coupling(reaction)
    strip_levels(strips, None, None, mix, edge, list(range(TILES)))
    for step, (src, dst) in enumerate(((gas, one), (one, two), (two, middle))):

        def body(x, carry, step=step, src=src, dst=dst):
            out = plane(src, kappa, edge, step, x, x, mix, TILES, range(COMP))
            into = x - 3 if step == ITERS - 1 else x
            for (c, t), value in out.items():
                dst[c, into, rows(t), :] = value
            return carry

        lax.fori_loop(step + 1, GX - 1 - step, body, 0, unroll=2)
    for c in range(COMP):
        for i, x in enumerate(SEAM):
            first[c, i] = one[c, x]
            second[c, i] = two[c, x + 1 if i < 2 else x - 1]


def outer_kernel(
    _, gas, kappa, strips, first, second, middle, recv_wall, recv_a, recv_rest, reaction, result, token, now, later, kap, edge
):
    token[...] = jnp.zeros((8, 128), jnp.float32)
    even = lax.rem(lax.axis_index("sect"), 2) == 0
    mix = coupling(reaction)
    split = GR - 8
    at_a, at_b = jnp.where(even, GX + 3, 0), jnp.where(even, 0, GX + 3)
    kappa_a, kappa_b = jnp.where(even, GX + 3, 1), jnp.where(even, 1, GX + 3)
    for c in range(COMP):
        for x in (0, 1, GX - 2, GX - 1):
            now[c, x + 3] = gas[c, x]
        for layer in range(3):
            now[c, at_a + layer] = recv_a[3 * c + layer]
            now[c, at_b + layer, split:, :] = recv_wall[3 * c + layer]
            now[c, at_b + layer, :split, :] = recv_rest[3 * c + layer]
        for i, x in enumerate(SEAM):
            later[c, x + 3] = first[c, i]
    for x in (0, 1, 2, GX - 3, GX - 2, GX - 1):
        kap[x + 3] = kappa[x]
    for layer in range(2):
        kap[kappa_a + layer] = recv_a[3 * COMP + layer]
        kap[kappa_b + layer, split:, :] = recv_wall[3 * COMP + layer]
        kap[kappa_b + layer, :split, :] = recv_rest[3 * COMP + layer]
    low, high = [], []
    for t in range(TILES):
        corner_a = recv_a[LAYERS - 1, rows(t), :]
        corner_b = recv_wall[LAYERS - 1 + t]
        low.append(jnp.where(even, corner_b, corner_a))
        high.append(jnp.where(even, corner_a, corner_b))
    strip_levels(strips, low, high, mix, edge, list(range(TILES)))
    for c in range(COMP):
        result[c, 3 : GX - 3] = middle[c]
    for step, (src, dst) in enumerate(((now, later), (later, now), (now, None))):
        if step == ITERS - 1:
            for c in range(COMP):
                for i, x in enumerate(SEAM):
                    now[c, (x + 1 if i < 2 else x - 1) + 3] = second[c, i]
        for i in range(3):
            for at in (step + 1 + i, GX + 2 - step + i):
                out = plane(src, kap, edge, step, at, at - 3, mix, TILES, range(COMP))
                for (c, t), value in out.items():
                    if step == ITERS - 1:
                        result[c, at - 3, rows(t), :] = value
                    else:
                        dst[c, at, rows(t), :] = value


def pack_kernel(hop, cell, particles, mixing, heating, _, packed, cells, spread, ordered, source, begin, end):
    lane = lanes()
    square = (128, 128)
    down, across = lax.broadcasted_iota(jnp.int32, square, 0), lanes(square)
    moves = hop[...]
    named = [moves == j for j in range(MOVES)]
    table = jnp.concatenate(
        [jnp.where(m, 1.0, 0.0) for m in named] + [jnp.zeros((128 - MOVES * CHUNKS, 128), jnp.float32)], axis=0
    )
    running = jnp.dot(table, jnp.where(down <= across, 1.0, 0.0), preferred_element_type=jnp.float32)
    count = jnp.dot(table, jnp.ones(square, jnp.float32), preferred_element_type=jnp.float32)
    before = jnp.where(((down >> 4) == (across >> 4)) & (across < down), 1.0, 0.0)
    base = jnp.dot(before, count, preferred_element_type=jnp.float32)
    offset = jnp.zeros((CHUNKS, 128), jnp.float32)
    place = jnp.zeros((CHUNKS, 128), jnp.float32)
    across16 = lanes((CHUNKS, 128))
    for j in range(MOVES):
        part = slice(CHUNKS * j, CHUNKS * (j + 1))
        place = jnp.where(named[j], offset + running[part] - 1.0, place)
        first = base[part].astype(jnp.int32)
        source[part, :] = (across16 + offset.astype(jnp.int32) - first) & 127
        begin[part, :] = across16 - first
        end[part, :] = across16 - first - count[part].astype(jnp.int32)
        offset = offset + count[part]
    own = lax.broadcasted_iota(jnp.int32, (VALS, VALS), 0) == lax.broadcasted_iota(jnp.int32, (VALS, VALS), 1)
    weights = 0.5 * mixing[...] + jnp.where(own, 1.0, 0.0)
    first_value = lax.broadcasted_iota(jnp.int32, (VALS, VALS), 1) == 0
    weights = weights - jnp.where(first_value, heating[...], 0.0)
    for v in range(VALS):
        spread[v] = jnp.broadcast_to(weights[:, v : v + 1], (VALS, 128))
    place = place.astype(jnp.int32)
    position = lane.astype(jnp.float32)
    for chunk in range(CHUNKS):
        part = slice(128 * chunk, 128 * (chunk + 1))
        total = spread[0] * particles[0:1, part]
        for v in range(1, VALS):
            total = total + spread[v] * particles[v : v + 1, part]
        hot = jnp.where(down == place[chunk : chunk + 1, :], 1.0, 0.0)
        order = lax.dot_general(position, hot, (((1,), (1,)), ((), ())), preferred_element_type=jnp.float32)
        order = order.astype(jnp.int32)
        ordered[chunk, 0:8, :] = pick(total[0:8], order)
        ordered[chunk, 8:16, :] = pick(total[8:16], order)
        ordered[chunk, 16:24, :] = pick(
            jnp.broadcast_to(cell[chunk : chunk + 1, :], (8, 128)).astype(jnp.float32), order
        )

    def block(j, carry):
        held = [[jnp.zeros((8, 128), jnp.float32)] * 2 + [jnp.full((8, 128), -1.0)] for _ in range(SPOTS)]
        for chunk in range(CHUNKS):
            row = pl.ds(CHUNKS * j + chunk, 1)
            index = jnp.broadcast_to(source[row, :], (8, 128))
            parts = [pick(ordered[chunk, rows(n), :], index) for n in range(3)]
            start = jnp.broadcast_to(begin[row, :], (8, 128))
            stop = jnp.broadcast_to(end[row, :], (8, 128))
            for spot in range(SPOTS):
                here = (start >= -128 * spot) & (stop < -128 * spot)
                held[spot] = [jnp.where(here, new, old) for new, old in zip(parts, held[spot])]
        for spot in range(SPOTS):
            part = slice(128 * spot, 128 * (spot + 1))
            packed[j, 0:8, part] = held[spot][0]
            packed[j, 8:16, part] = held[spot][1]
            cells[j, spot : spot + 1, :] = held[spot][2][0:1, :].astype(jnp.int32)
        return carry

    lax.fori_loop(0, MOVES, block, 0)


def moves_of_swaps():
    tile = lax.axis_index("blk")
    odd, late = lax.rem(tile, 2), lax.rem(tile, 4) >> 1
    return [REACH - 1 + 2 * odd, 2 * REACH * (1 - late), 2 * REACH * late, REACH + 1 - 2 * odd]


def heat_kernel(wall, earlier, packed, cells, heating, own, send_q, send_r, send_s, send_p, look):
    flux = 0.5 * (wall[...] + earlier[...])
    heat = jnp.broadcast_to(heating[...], (VALS, 128))
    for j in range(MOVES):
        where_to = cells[j]
        row, column = where_to >> 7, where_to & 127
        found = jnp.zeros((8, 128), jnp.float32)
        for x in range(GX):
            line = jnp.broadcast_to(flux[x : x + 1, :], (8, 128))
            found = jnp.where(row == x, pick(line, column), found)
        look[j] = found
    for out, j in zip((own, send_q, send_r, send_s, send_p), [REACH] + moves_of_swaps()):
        for spot in range(SPOTS):
            part = slice(128 * spot, 128 * (spot + 1))
            out[:, part] = packed[j, :, part] + heat * look[j, spot : spot + 1, :]


def join_kernel(own, recv_q, recv_r, recv_s, recv_p, _, out, done):
    copies = []
    for n, (piece, j) in enumerate(zip((own, recv_q, recv_r, recv_s, recv_p), [REACH] + moves_of_swaps())):
        place = pl.multiple_of((2 * REACH - j) * CAP, CAP)
        copies.append(pltpu.make_async_copy(piece, out.at[:, pl.ds(place, CAP)], done.at[n]))
    for copy in copies:
        copy.start()
    for copy in copies:
        copy.wait()


def swap(x, axis, pairs):
    return lax.ppermute(x, axis, pairs + [(j, i) for i, j in pairs])


def local(gas, kappa, reaction, particles, mixing, heating, wall_cell, tile_hop):
    sections, tiles = lax.axis_size("sect"), lax.axis_size("blk")
    pairs_a = [(i, i + 1) for i in range(0, sections, 2)]
    pairs_b = [(i, i + 1) for i in range(1, sections - 1, 2)]
    pairs_q = [(i, (i + 1) % tiles) for i in range(1, tiles, 2)]
    pairs_p = [(i, i + 1) for i in range(0, tiles, 2)]
    pairs_s = [(i, (i + 2) % tiles) for i in range(tiles) if i % 4 >= 2]
    pairs_r = [(i, i + 2) for i in range(tiles) if i % 4 < 2]

    send_q, send_p = call(
        edges_kernel,
        (f32(3, GR, GA), f32(3, GR, GA)),
        scratch=[pltpu.VMEM((COMP + 1, GX, GR, GA), jnp.float32), pltpu.SemaphoreType.DMA((COMP + 1,))],
        specs=[HBM] * 2,
        moved=2 << 20,
        limit=53.75,
    )(gas, kappa)
    recv_q = swap(send_q, "blk", pairs_q)
    recv_p = swap(send_p, "blk", pairs_p)
    heating_column = heating.reshape(VALS, 1)
    packed, cells = call(
        pack_kernel,
        (f32(MOVES, VALS, CAP), i32(MOVES, SPOTS, 128)),
        scratch=[
            pltpu.VMEM((VALS, VALS, 128), jnp.float32),
            pltpu.VMEM((CHUNKS, 24, 128), jnp.float32),
            pltpu.VMEM((MOVES * CHUNKS, 128), jnp.int32),
            pltpu.VMEM((MOVES * CHUNKS, 128), jnp.int32),
            pltpu.VMEM((MOVES * CHUNKS, 128), jnp.int32),
        ],
        specs=[VMEM] * 5 + [ANY],
        moved=4 << 20,
    )(tile_hop.reshape(CHUNKS, 128), wall_cell.reshape(CHUNKS, 128), particles, mixing, heating_column, send_p)

    strips, send_a, send_wall = call(
        strips_kernel,
        (f32(len(STRIPS), GR, GA), f32(LAYERS, GR, GA), f32(LAYERS - 1 + TILES, 8, GA)),
        specs=[VMEM] * 6 + [ANY],
        moved=2 << 20,
    )(gas, kappa, send_q, send_p, recv_q, recv_p, cells)
    recv_wall = swap(send_wall, "sect", pairs_b)
    recv_a = swap(send_a, "sect", pairs_a)

    whole = f32(COMP, GX, GR, GA)
    first, second, middle = call(
        inner_kernel,
        (f32(COMP, len(SEAM), GR, GA), f32(COMP, len(SEAM), GR, GA), f32(COMP, GX - 6, GR, GA)),
        scratch=[
            pltpu.VMEM((COMP, GX, GR, GA), jnp.float32),
            pltpu.VMEM((COMP, GX, GR, GA), jnp.float32),
            pltpu.VMEM((ITERS, COMP, GR, GA), jnp.float32),
        ],
        specs=[VMEM] * 3 + [SMEM],
        moved=12 << 20,
    )(gas, kappa, strips, reaction)

    send_rest = call(rest_kernel, f32(LAYERS - 1, GR - 8, GA), specs=[VMEM] * 2 + [ANY], moved=1 << 18)(gas, kappa, middle)
    recv_rest = swap(send_rest, "sect", pairs_b)

    wall = call(
        wall_kernel,
        f32(GX, GA),
        scratch=[
            pltpu.VMEM((COMP, EXT, 8, GA), jnp.float32),
            pltpu.VMEM((COMP, EXT, 8, GA), jnp.float32),
            pltpu.VMEM((EXT, 8, GA), jnp.float32),
            pltpu.VMEM((ITERS, COMP, 8, GA), jnp.float32),
        ],
        specs=[VMEM] * 8 + [SMEM, ANY],
        moved=4 << 20,
    )(gas, kappa, strips, recv_wall, recv_a, first, second, middle, reaction, send_rest)
    earlier = lax.ppermute(wall, "sect", [(i, i + 1) for i in range(sections - 1)])

    own, *sends = call(
        heat_kernel,
        (f32(VALS, CAP),) * MOVES,
        scratch=[pltpu.VMEM((MOVES, SPOTS, 128), jnp.float32)],
        specs=[VMEM] * 5,
        moved=2 << 20,
        flops=1 << 34,
    )(wall, earlier, packed, cells, heating_column)
    pieces = [swap(x, "blk", pairs) for x, pairs in zip(sends, (pairs_q, pairs_r, pairs_s, pairs_p))]

    field, token = call(
        outer_kernel,
        (whole, f32(8, 128)),
        scratch=[
            pltpu.VMEM((COMP, EXT, GR, GA), jnp.float32),
            pltpu.VMEM((COMP, EXT, GR, GA), jnp.float32),
            pltpu.VMEM((EXT, GR, GA), jnp.float32),
            pltpu.VMEM((ITERS, COMP, GR, GA), jnp.float32),
        ],
        specs=[ANY] + [VMEM] * 9 + [SMEM],
        moved=8 << 20,
    )(pieces[0], gas, kappa, strips, first, second, middle, recv_wall, recv_a, recv_rest, reaction)
    arrived = call(
        join_kernel,
        f32(VALS, MOVES * CAP),
        scratch=[pltpu.SemaphoreType.DMA((MOVES,))],
        specs=[VMEM] * MOVES + [ANY],
        out_specs=HBM,
        moved=1 << 20,
    )(own, *pieces, token)
    return field, arrived


def solution(mesh):
    in_specs = (
        P(None, "sect", None, "blk"),
        P("sect", None, "blk"),
        P(),
        P(None, ("sect", "blk")),
        P(),
        P(),
        P(("sect", "blk")),
        P(("sect", "blk"), None),
    )
    out_specs = (P(None, "sect", None, "blk"), P(None, ("sect", "blk")))
    return jax.shard_map(local, mesh=mesh, in_specs=in_specs, out_specs=out_specs, check_vma=False)
```

```python
import jax
import jax.numpy as jnp
from jax import lax
from jax.experimental import pallas as pl
from jax.experimental.pallas import tpu as pltpu
from jax.sharding import PartitionSpec as P

REACH = 2
MOVES = 2 * REACH + 1
ITERS = 3
DIFFUSE = (1.0, 0.8, 0.6, 0.9, 0.7)
COMP = 5
GX = 16
GR = 32
GA = 128
TILES = GR // 8
EXT = GX + 2 * ITERS
CHUNKS = 16
VALS = 16
CAP = 1024
SPOTS = CAP // 128

FIELD_COLUMNS = (3, 2, 1, 0, -1)
KAPPA_COLUMNS = (2, 1, 0)
STRIPS = [(c, k) for c in range(COMP) for k in FIELD_COLUMNS] + [(COMP, k) for k in KAPPA_COLUMNS]
STRIP_AT = {key: i for i, key in enumerate(STRIPS)}
CORNERS = [(c, 1) for c in range(COMP)] + [(c, 2) for c in range(COMP)] + [(COMP, 1)] + [(c, 0) for c in range(COMP)]
LAYERS = 3 * COMP + 2 + 1
SEAM = (1, 2, GX - 3, GX - 2)

VMEM = pl.BlockSpec(memory_space=pltpu.VMEM)
SMEM = pl.BlockSpec(memory_space=pltpu.SMEM)
ANY = pl.BlockSpec(memory_space=pl.ANY)
HBM = pl.BlockSpec(memory_space=pltpu.HBM)


def f32(*shape):
    return jax.ShapeDtypeStruct(shape, jnp.float32)


def i32(*shape):
    return jax.ShapeDtypeStruct(shape, jnp.int32)


def lanes(shape=(8, 128)):
    return lax.broadcasted_iota(jnp.int32, shape, len(shape) - 1)


def pick(x, index):
    return jnp.take_along_axis(x, index, axis=1, mode="promise_in_bounds")


def rows(tile):
    return slice(8 * tile, 8 * tile + 8)


def call(kernel, outs, scratch=(), specs=None, out_specs=None, flops=0, moved=0, limit=16):
    return pl.pallas_call(
        kernel,
        out_shape=outs,
        in_specs=specs,
        out_specs=jax.tree.map(lambda _: VMEM, outs) if out_specs is None else out_specs,
        scratch_shapes=list(scratch),
        cost_estimate=pl.CostEstimate(flops=flops, bytes_accessed=moved, transcendentals=0),
        compiler_params=pltpu.CompilerParams(vmem_limit_bytes=int(limit * 2**20)),
    )


def edges_kernel(gas, kappa, send_q, send_p, held, arrived):
    copies = [pltpu.make_async_copy(gas.at[q], held.at[q], arrived.at[q]) for q in range(COMP)]
    copies.append(pltpu.make_async_copy(kappa, held.at[COMP], arrived.at[COMP]))
    for copy in copies:
        copy.start()
    lane = lanes()
    within = lane & 63
    depth, cell = within >> 4, within & 15
    high = jnp.maximum(6 * cell + 2 - depth, 0)
    low = 6 * cell + 3 + depth
    odd = lax.rem(lax.axis_index("blk"), 2) == 1
    index_q, index_p = jnp.where(odd, high, low), jnp.where(odd, low, high)
    for pair in range((COMP + 1) // 2):
        packed = {}
        for q in (2 * pair, 2 * pair + 1):
            copies[q].wait()
            for tile in range(TILES):
                total = jnp.zeros((8, 128), jnp.float32)
                for x in range(GX):
                    here = (lane >= 6 * x) & (lane < 6 * x + 6)
                    total = jnp.where(here, pltpu.roll(held[q, x, rows(tile), :], 6 * x + 3, 1), total)
                packed[q, tile] = total
        for tile in range(TILES):
            first, second = packed[2 * pair, tile], packed[2 * pair + 1, tile]
            for out, index in ((send_q, index_q), (send_p, index_p)):
                out[pair, rows(tile), :] = jnp.where(lane < 64, pick(first, index), pick(second, index))


def strips_kernel(gas, kappa, send_q, send_p, recv_q, recv_p, _, strips, send_a, send_wall, corner):
    lane = lanes()
    low_side = (lane & 1) == 1
    cell = jnp.clip((lane >> 1) - 3, 0, GX - 1)
    even = lax.rem(lax.axis_index("sect"), 2) == 0
    odd_tile = lax.rem(lax.axis_index("blk"), 2) == 1
    for tile in range(TILES):
        held = {}
        slabs = [[ref[s, rows(tile), :] for s in range(3)] for ref in (send_q, send_p, recv_q, recv_p)]
        own_q, own_p, got_q, got_p = slabs
        to_left = [jnp.where(odd_tile, p, q) for q, p in zip(own_q, own_p)]
        to_right = [jnp.where(odd_tile, q, p) for q, p in zip(own_q, own_p)]
        from_left = [jnp.where(odd_tile, p, q) for q, p in zip(got_q, got_p)]
        from_right = [jnp.where(odd_tile, q, p) for q, p in zip(got_q, got_p)]
        for q, k in STRIPS:
            depth = k - 1 if k > 0 else -k
            index = cell + ((q % 2) * 64 + depth * 16)
            low, high = (from_left, from_right) if k > 0 else (to_left, to_right)
            value = jnp.where(low_side, pick(low[q // 2], index), pick(high[q // 2], index))
            strips[STRIP_AT[q, k], rows(tile), :] = value
            held[q, k] = value
        top = jnp.zeros((8, 128), jnp.float32)
        bottom = top
        for i, key in enumerate(CORNERS):
            here = (lane >> 2) == i
            top = jnp.where(here, pltpu.roll(held[key], (4 * i - 34) % 128, 1), top)
            bottom = jnp.where(here, pltpu.roll(held[key], (4 * i - 6) % 128, 1), bottom)
        for_a = jnp.where(even, top, bottom)
        for_b = jnp.where(even, bottom, top)
        send_a[LAYERS - 1, rows(tile), :] = for_a
        if tile == TILES - 1:
            send_wall[LAYERS - 1] = for_b
        else:
            corner[rows(tile), :] = for_b
    at_a, at_b = jnp.where(even, GX - 3, 0), jnp.where(even, 0, GX - 3)
    kappa_a, kappa_b = jnp.where(even, GX - 2, 0), jnp.where(even, 0, GX - 2)
    for c in range(COMP):
        for layer in range(3):
            send_a[3 * c + layer] = gas[c, at_a + layer]
            send_wall[3 * c + layer] = gas[c, at_b + layer, GR - 8 :, :]
    for layer in range(2):
        send_a[3 * COMP + layer] = kappa[kappa_a + layer]
        send_wall[3 * COMP + layer] = kappa[kappa_b + layer, GR - 8 :, :]


def rest_kernel(gas, kappa, corner, _, send_rest):
    send_rest[LAYERS - 1] = corner[...]
    even = lax.rem(lax.axis_index("sect"), 2) == 0
    split = GR - 8
    from_b, from_kappa = jnp.where(even, 0, GX - 3), jnp.where(even, 0, GX - 2)
    for c in range(COMP):
        for layer in range(3):
            send_rest[3 * c + layer] = gas[c, from_b + layer, :split, :]
    for layer in range(2):
        send_rest[3 * COMP + layer] = kappa[from_kappa + layer, :split, :]


def coupling(reaction):
    return [[0.3 * reaction[c, d] + (1.0 if c == d else 0.0) for d in range(COMP)] for c in range(COMP)]


def updated(c, values, neighbours, kappa, mix):
    total = mix[c][0] * values[0]
    for d in range(1, COMP):
        total = total + mix[c][d] * values[d]
    rate = kappa if DIFFUSE[c] == 1.0 else DIFFUSE[c] * kappa
    return total + rate * (neighbours - 6.0 * values[c])


def radial_sum(tiles, wall_only):
    sub = lax.broadcasted_iota(jnp.int32, (8, 128), 0)
    down = [pltpu.roll(t, 1, 0) for t in tiles]
    up = [pltpu.roll(t, 7, 0) for t in tiles]
    last = len(tiles) - 1
    sums = []
    for i, t in enumerate(tiles):
        if wall_only:
            below = down[i]
        else:
            below = jnp.where(sub == 0, down[i - 1] if i > 0 else t, down[i])
        above = jnp.where(sub == 7, up[i + 1] if i < last else t, up[i])
        sums.append(below + above)
    return sums


def radial_sum_of(src, c, at, values):
    sub = lax.broadcasted_iota(jnp.int32, (8, 128), 0)
    sums = []
    for t in range(TILES):
        first, last = t == 0, t == TILES - 1
        below = jnp.where(sub == 0, values[t], pltpu.roll(values[t], 1, 0)) if first else src[c, at, 8 * t - 1 : 8 * t + 7, :]
        above = jnp.where(sub == 7, values[t], pltpu.roll(values[t], 7, 0)) if last else src[c, at, 8 * t + 1 : 8 * t + 9, :]
        sums.append(below + above)
    return sums


def strip_levels(strips, low_corner, high_corner, mix, edge, tiles):
    lane = lanes()
    wall_only = len(tiles) == 1
    from_low = (lane >= 2) & (lane < 6)
    from_high = (lane >= 38) & (lane < 42)
    held = {}
    for key in STRIPS:
        held[key] = [strips[STRIP_AT[key], rows(t), :] for t in tiles]
    for i, key in enumerate(CORNERS if low_corner else ()):
        for n in range(len(tiles)):
            value = jnp.where(from_low, pltpu.roll(low_corner[n], (2 - 4 * i) % 128, 1), held[key][n])
            held[key][n] = jnp.where(from_high, pltpu.roll(high_corner[n], (38 - 4 * i) % 128, 1), value)
    for step in range(ITERS):
        for c in range(COMP):
            for n in range(len(tiles)):
                edge[step, c, rows(n), :] = held[c, 1][n]
        if step == ITERS - 1:
            break
        later = {}
        for k in (2, 1, 0) if step == 0 else (1,):
            for c in range(COMP):
                radial = radial_sum(held[c, k], wall_only)
                later[c, k] = []
                for n in range(len(tiles)):
                    value = held[c, k][n]
                    around = held[c, k + 1][n] + held[c, k - 1][n]
                    around = around + pltpu.roll(value, 2, 1) + pltpu.roll(value, 126, 1) + radial[n]
                    later[c, k].append(updated(c, [held[d, k][n] for d in range(COMP)], around, held[COMP, k][n], mix))
        for key in [key for key in held if key[0] == COMP]:
            later[key] = held[key]
        held = later


def plane(src, kappa, edge, step, at, x, mix, count, comps):
    lane = lanes()
    first, last = lane == 0, lane == 127
    shift = 121 - 2 * x
    values = [[src[c, at, rows(t), :] for t in range(count)] for c in range(COMP)]
    kap = [kappa[at, rows(t), :] for t in range(count)]
    out = {}
    for c in comps:
        radial = radial_sum(values[c], True) if count == 1 else radial_sum_of(src, c, at, values[c])
        for t in range(count):
            value = values[c][t]
            beyond = pltpu.roll(edge[step, c, rows(t), :], shift, 1)
            around = src[c, at - 1, rows(t), :] + src[c, at + 1, rows(t), :] + radial[t]
            around = around + jnp.where(first, beyond, pltpu.roll(value, 1, 1))
            around = around + jnp.where(last, beyond, pltpu.roll(value, 127, 1))
            out[c, t] = updated(c, [values[d][t] for d in range(COMP)], around, kap[t], mix)
    return out


def wall_kernel(
    gas, kappa, strips, recv_wall, recv_a, first, second, middle, reaction, _, wall, now, later, kap, edge
):
    even = lax.rem(lax.axis_index("sect"), 2) == 0
    mix = coupling(reaction)
    top = slice(GR - 8, GR)
    at_a, at_b = jnp.where(even, GX + 3, 0), jnp.where(even, 0, GX + 3)
    kappa_a, kappa_b = jnp.where(even, GX + 3, 1), jnp.where(even, 1, GX + 3)
    for c in range(COMP):
        for x in (0, 1, GX - 2, GX - 1):
            now[c, x + 3] = gas[c, x, top, :]
        for layer in range(3):
            now[c, at_a + layer] = recv_a[3 * c + layer, top, :]
            now[c, at_b + layer] = recv_wall[3 * c + layer]
        for i, x in enumerate(SEAM):
            later[c, x + 3] = first[c, i, top, :]
    for x in (0, 1, 2, GX - 3, GX - 2, GX - 1):
        kap[x + 3] = kappa[x, top, :]
    for layer in range(2):
        kap[kappa_a + layer] = recv_a[3 * COMP + layer, top, :]
        kap[kappa_b + layer] = recv_wall[3 * COMP + layer]
    corner_a, corner_b = recv_a[LAYERS - 1, top, :], recv_wall[LAYERS - 1]
    low, high = jnp.where(even, corner_b, corner_a), jnp.where(even, corner_a, corner_b)
    strip_levels(strips, [low], [high], mix, edge, [TILES - 1])
    wall[3 : GX - 3, :] = middle[0, :, GR - 1, :]
    for step, (src, dst) in enumerate(((now, later), (later, now), (now, None))):
        last = step == ITERS - 1
        if last:
            for c in range(COMP):
                for i, x in enumerate(SEAM):
                    now[c, (x + 1 if i < 2 else x - 1) + 3] = second[c, i, top, :]
        for i in range(3):
            for at in (step + 1 + i, GX + 2 - step + i):
                out = plane(src, kap, edge, step, at, at - 3, mix, 1, (0,) if last else range(COMP))
                if last:
                    wall[at - 3 : at - 2, :] = out[0, 0][7:8, :]
                    continue
                for c in range(COMP):
                    dst[c, at] = out[c, 0]


def inner_kernel(gas, kappa, strips, reaction, first, second, middle, one, two, edge):
    mix = coupling(reaction)
    strip_levels(strips, None, None, mix, edge, list(range(TILES)))
    for step, (src, dst) in enumerate(((gas, one), (one, two), (two, middle))):

        def body(x, carry, step=step, src=src, dst=dst):
            out = plane(src, kappa, edge, step, x, x, mix, TILES, range(COMP))
            into = x - 3 if step == ITERS - 1 else x
            for (c, t), value in out.items():
                dst[c, into, rows(t), :] = value
            return carry

        lax.fori_loop(step + 1, GX - 1 - step, body, 0, unroll=2)
    for c in range(COMP):
        for i, x in enumerate(SEAM):
            first[c, i] = one[c, x]
            second[c, i] = two[c, x + 1 if i < 2 else x - 1]


def outer_kernel(
    _, gas, kappa, strips, first, second, middle, recv_wall, recv_a, recv_rest, reaction, result, token, now, later, kap, edge
):
    token[...] = jnp.zeros((8, 128), jnp.float32)
    even = lax.rem(lax.axis_index("sect"), 2) == 0
    mix = coupling(reaction)
    split = GR - 8
    at_a, at_b = jnp.where(even, GX + 3, 0), jnp.where(even, 0, GX + 3)
    kappa_a, kappa_b = jnp.where(even, GX + 3, 1), jnp.where(even, 1, GX + 3)
    for c in range(COMP):
        for x in (0, 1, GX - 2, GX - 1):
            now[c, x + 3] = gas[c, x]
        for layer in range(3):
            now[c, at_a + layer] = recv_a[3 * c + layer]
            now[c, at_b + layer, split:, :] = recv_wall[3 * c + layer]
            now[c, at_b + layer, :split, :] = recv_rest[3 * c + layer]
        for i, x in enumerate(SEAM):
            later[c, x + 3] = first[c, i]
    for x in (0, 1, 2, GX - 3, GX - 2, GX - 1):
        kap[x + 3] = kappa[x]
    for layer in range(2):
        kap[kappa_a + layer] = recv_a[3 * COMP + layer]
        kap[kappa_b + layer, split:, :] = recv_wall[3 * COMP + layer]
        kap[kappa_b + layer, :split, :] = recv_rest[3 * COMP + layer]
    low, high = [], []
    for t in range(TILES):
        corner_a = recv_a[LAYERS - 1, rows(t), :]
        corner_b = recv_wall[LAYERS - 1] if t == TILES - 1 else recv_rest[LAYERS - 1, rows(t), :]
        low.append(jnp.where(even, corner_b, corner_a))
        high.append(jnp.where(even, corner_a, corner_b))
    strip_levels(strips, low, high, mix, edge, list(range(TILES)))
    for c in range(COMP):
        result[c, 3 : GX - 3] = middle[c]
    for step, (src, dst) in enumerate(((now, later), (later, now), (now, None))):
        if step == ITERS - 1:
            for c in range(COMP):
                for i, x in enumerate(SEAM):
                    now[c, (x + 1 if i < 2 else x - 1) + 3] = second[c, i]
        for i in range(3):
            for at in (step + 1 + i, GX + 2 - step + i):
                out = plane(src, kap, edge, step, at, at - 3, mix, TILES, range(COMP))
                for (c, t), value in out.items():
                    if step == ITERS - 1:
                        result[c, at - 3, rows(t), :] = value
                    else:
                        dst[c, at, rows(t), :] = value


def pack_kernel(hop, cell, particles, mixing, heating, _, packed, cells, spread, ordered, source, begin, end):
    lane = lanes()
    square = (128, 128)
    down, across = lax.broadcasted_iota(jnp.int32, square, 0), lanes(square)
    moves = hop[...]
    named = [moves == j for j in range(MOVES)]
    table = jnp.concatenate(
        [jnp.where(m, 1.0, 0.0) for m in named] + [jnp.zeros((128 - MOVES * CHUNKS, 128), jnp.float32)], axis=0
    )
    running = jnp.dot(table, jnp.where(down <= across, 1.0, 0.0), preferred_element_type=jnp.float32)
    count = jnp.dot(table, jnp.ones(square, jnp.float32), preferred_element_type=jnp.float32)
    before = jnp.where(((down >> 4) == (across >> 4)) & (across < down), 1.0, 0.0)
    base = jnp.dot(before, count, preferred_element_type=jnp.float32)
    offset = jnp.zeros((CHUNKS, 128), jnp.float32)
    place = jnp.zeros((CHUNKS, 128), jnp.float32)
    across16 = lanes((CHUNKS, 128))
    for j in range(MOVES):
        part = slice(CHUNKS * j, CHUNKS * (j + 1))
        place = jnp.where(named[j], offset + running[part] - 1.0, place)
        first = base[part].astype(jnp.int32)
        source[part, :] = (across16 + offset.astype(jnp.int32) - first) & 127
        begin[part, :] = across16 - first
        end[part, :] = across16 - first - count[part].astype(jnp.int32)
        offset = offset + count[part]
    own = lax.broadcasted_iota(jnp.int32, (VALS, VALS), 0) == lax.broadcasted_iota(jnp.int32, (VALS, VALS), 1)
    weights = 0.5 * mixing[...] + jnp.where(own, 1.0, 0.0)
    first_value = lax.broadcasted_iota(jnp.int32, (VALS, VALS), 1) == 0
    weights = weights - jnp.where(first_value, heating[...], 0.0)
    for v in range(VALS):
        spread[v] = jnp.broadcast_to(weights[:, v : v + 1], (VALS, 128))
    place = place.astype(jnp.int32)
    position = lane.astype(jnp.float32)
    for chunk in range(CHUNKS):
        part = slice(128 * chunk, 128 * (chunk + 1))
        total = spread[0] * particles[0:1, part]
        for v in range(1, VALS):
            total = total + spread[v] * particles[v : v + 1, part]
        hot = jnp.where(down == place[chunk : chunk + 1, :], 1.0, 0.0)
        order = lax.dot_general(position, hot, (((1,), (1,)), ((), ())), preferred_element_type=jnp.float32)
        order = order.astype(jnp.int32)
        ordered[chunk, 0:8, :] = pick(total[0:8], order)
        ordered[chunk, 8:16, :] = pick(total[8:16], order)
        ordered[chunk, 16:24, :] = pick(
            jnp.broadcast_to(cell[chunk : chunk + 1, :], (8, 128)).astype(jnp.float32), order
        )

    def block(j, carry):
        held = [[jnp.zeros((8, 128), jnp.float32)] * 2 + [jnp.full((8, 128), -1.0)] for _ in range(SPOTS)]
        for chunk in range(CHUNKS):
            row = pl.ds(CHUNKS * j + chunk, 1)
            index = jnp.broadcast_to(source[row, :], (8, 128))
            parts = [pick(ordered[chunk, rows(n), :], index) for n in range(3)]
            start = jnp.broadcast_to(begin[row, :], (8, 128))
            stop = jnp.broadcast_to(end[row, :], (8, 128))
            for spot in range(SPOTS):
                here = (start >= -128 * spot) & (stop < -128 * spot)
                held[spot] = [jnp.where(here, new, old) for new, old in zip(parts, held[spot])]
        for spot in range(SPOTS):
            part = slice(128 * spot, 128 * (spot + 1))
            packed[j, 0:8, part] = held[spot][0]
            packed[j, 8:16, part] = held[spot][1]
            cells[j, spot : spot + 1, :] = held[spot][2][0:1, :].astype(jnp.int32)
        return carry

    lax.fori_loop(0, MOVES, block, 0)


def moves_of_swaps():
    tile = lax.axis_index("blk")
    odd, late = lax.rem(tile, 2), lax.rem(tile, 4) >> 1
    return [REACH - 1 + 2 * odd, 2 * REACH * (1 - late), 2 * REACH * late, REACH + 1 - 2 * odd]


def heat_kernel(wall, earlier, packed, cells, heating, own, send_q, send_r, send_s, send_p, look):
    flux = 0.5 * (wall[...] + earlier[...])
    heat = jnp.broadcast_to(heating[...], (VALS, 128))
    for j in range(MOVES):
        where_to = cells[j]
        row, column = where_to >> 7, where_to & 127
        found = jnp.zeros((8, 128), jnp.float32)
        for x in range(GX):
            line = jnp.broadcast_to(flux[x : x + 1, :], (8, 128))
            found = jnp.where(row == x, pick(line, column), found)
        look[j] = found
    for out, j in zip((own, send_q, send_r, send_s, send_p), [REACH] + moves_of_swaps()):
        for spot in range(SPOTS):
            part = slice(128 * spot, 128 * (spot + 1))
            out[:, part] = packed[j, :, part] + heat * look[j, spot : spot + 1, :]


def join_kernel(own, recv_q, recv_r, recv_s, recv_p, _, out, done):
    copies = []
    for n, (piece, j) in enumerate(zip((own, recv_q, recv_r, recv_s, recv_p), [REACH] + moves_of_swaps())):
        place = pl.multiple_of((2 * REACH - j) * CAP, CAP)
        copies.append(pltpu.make_async_copy(piece, out.at[:, pl.ds(place, CAP)], done.at[n]))
    for copy in copies:
        copy.start()
    for copy in copies:
        copy.wait()


def swap(x, axis, pairs):
    return lax.ppermute(x, axis, pairs + [(j, i) for i, j in pairs])


def local(gas, kappa, reaction, particles, mixing, heating, wall_cell, tile_hop):
    sections, tiles = lax.axis_size("sect"), lax.axis_size("blk")
    pairs_a = [(i, i + 1) for i in range(0, sections, 2)]
    pairs_b = [(i, i + 1) for i in range(1, sections - 1, 2)]
    pairs_q = [(i, (i + 1) % tiles) for i in range(1, tiles, 2)]
    pairs_p = [(i, i + 1) for i in range(0, tiles, 2)]
    pairs_s = [(i, (i + 2) % tiles) for i in range(tiles) if i % 4 >= 2]
    pairs_r = [(i, i + 2) for i in range(tiles) if i % 4 < 2]

    send_q, send_p = call(
        edges_kernel,
        (f32(3, GR, GA), f32(3, GR, GA)),
        scratch=[pltpu.VMEM((COMP + 1, GX, GR, GA), jnp.float32), pltpu.SemaphoreType.DMA((COMP + 1,))],
        specs=[HBM] * 2,
        moved=2 << 20,
        limit=53.75,
    )(gas, kappa)
    recv_q = swap(send_q, "blk", pairs_q)
    recv_p = swap(send_p, "blk", pairs_p)
    heating_column = heating.reshape(VALS, 1)
    packed, cells = call(
        pack_kernel,
        (f32(MOVES, VALS, CAP), i32(MOVES, SPOTS, 128)),
        scratch=[
            pltpu.VMEM((VALS, VALS, 128), jnp.float32),
            pltpu.VMEM((CHUNKS, 24, 128), jnp.float32),
            pltpu.VMEM((MOVES * CHUNKS, 128), jnp.int32),
            pltpu.VMEM((MOVES * CHUNKS, 128), jnp.int32),
            pltpu.VMEM((MOVES * CHUNKS, 128), jnp.int32),
        ],
        specs=[VMEM] * 5 + [ANY],
        moved=4 << 20,
    )(tile_hop.reshape(CHUNKS, 128), wall_cell.reshape(CHUNKS, 128), particles, mixing, heating_column, send_p)

    strips, send_a, send_wall, corner = call(
        strips_kernel,
        (f32(len(STRIPS), GR, GA), f32(LAYERS, GR, GA), f32(LAYERS, 8, GA), f32(GR - 8, GA)),
        specs=[VMEM] * 6 + [ANY],
        moved=2 << 20,
    )(gas, kappa, send_q, send_p, recv_q, recv_p, cells)
    recv_wall = swap(send_wall, "sect", pairs_b)
    recv_a = swap(send_a, "sect", pairs_a)

    whole = f32(COMP, GX, GR, GA)
    first, second, middle = call(
        inner_kernel,
        (f32(COMP, len(SEAM), GR, GA), f32(COMP, len(SEAM), GR, GA), f32(COMP, GX - 6, GR, GA)),
        scratch=[
            pltpu.VMEM((COMP, GX, GR, GA), jnp.float32),
            pltpu.VMEM((COMP, GX, GR, GA), jnp.float32),
            pltpu.VMEM((ITERS, COMP, GR, GA), jnp.float32),
        ],
        specs=[VMEM] * 3 + [SMEM],
        moved=12 << 20,
    )(gas, kappa, strips, reaction)

    send_rest = call(rest_kernel, f32(LAYERS, GR - 8, GA), specs=[VMEM] * 3 + [ANY], moved=1 << 18)(
        gas, kappa, corner, middle
    )
    recv_rest = swap(send_rest, "sect", pairs_b)

    wall = call(
        wall_kernel,
        f32(GX, GA),
        scratch=[
            pltpu.VMEM((COMP, EXT, 8, GA), jnp.float32),
            pltpu.VMEM((COMP, EXT, 8, GA), jnp.float32),
            pltpu.VMEM((EXT, 8, GA), jnp.float32),
            pltpu.VMEM((ITERS, COMP, 8, GA), jnp.float32),
        ],
        specs=[VMEM] * 8 + [SMEM, ANY],
        moved=4 << 20,
    )(gas, kappa, strips, recv_wall, recv_a, first, second, middle, reaction, send_rest)
    earlier = lax.ppermute(wall, "sect", [(i, i + 1) for i in range(sections - 1)])

    own, *sends = call(
        heat_kernel,
        (f32(VALS, CAP),) * MOVES,
        scratch=[pltpu.VMEM((MOVES, SPOTS, 128), jnp.float32)],
        specs=[VMEM] * 5,
        moved=2 << 20,
        flops=1 << 34,
    )(wall, earlier, packed, cells, heating_column)
    pieces = [swap(x, "blk", pairs) for x, pairs in zip(sends, (pairs_q, pairs_r, pairs_s, pairs_p))]

    field, token = call(
        outer_kernel,
        (whole, f32(8, 128)),
        scratch=[
            pltpu.VMEM((COMP, EXT, GR, GA), jnp.float32),
            pltpu.VMEM((COMP, EXT, GR, GA), jnp.float32),
            pltpu.VMEM((EXT, GR, GA), jnp.float32),
            pltpu.VMEM((ITERS, COMP, GR, GA), jnp.float32),
        ],
        specs=[ANY] + [VMEM] * 9 + [SMEM],
        moved=8 << 20,
    )(pieces[0], gas, kappa, strips, first, second, middle, recv_wall, recv_a, recv_rest, reaction)
    arrived = call(
        join_kernel,
        f32(VALS, MOVES * CAP),
        scratch=[pltpu.SemaphoreType.DMA((MOVES,))],
        specs=[VMEM] * MOVES + [ANY],
        out_specs=HBM,
        moved=1 << 20,
    )(own, *pieces, token)
    return field, arrived


def solution(mesh):
    in_specs = (
        P(None, "sect", None, "blk"),
        P("sect", None, "blk"),
        P(),
        P(None, ("sect", "blk")),
        P(),
        P(),
        P(("sect", "blk")),
        P(("sect", "blk"), None),
    )
    out_specs = (P(None, "sect", None, "blk"), P(None, ("sect", "blk")))
    return jax.shard_map(local, mesh=mesh, in_specs=in_specs, out_specs=out_specs, check_vma=False)
```

```python
import jax
import jax.numpy as jnp
from jax import lax
from jax.experimental import pallas as pl
from jax.experimental.pallas import tpu as pltpu
from jax.sharding import PartitionSpec as P

REACH = 2
MOVES = 2 * REACH + 1
ITERS = 3
DIFFUSE = (1.0, 0.8, 0.6, 0.9, 0.7)
COMP = 5
GX = 16
GR = 32
GA = 128
TILES = GR // 8
EXT = GX + 2 * ITERS
CHUNKS = 16
VALS = 16
CAP = 1024
SPOTS = CAP // 128

FIELD_COLUMNS = (3, 2, 1, 0, -1)
KAPPA_COLUMNS = (2, 1, 0)
STRIPS = [(c, k) for c in range(COMP) for k in FIELD_COLUMNS] + [(COMP, k) for k in KAPPA_COLUMNS]
STRIP_AT = {key: i for i, key in enumerate(STRIPS)}
CORNERS = [(c, 1) for c in range(COMP)] + [(c, 2) for c in range(COMP)] + [(COMP, 1)] + [(c, 0) for c in range(COMP)]
LAYERS = 3 * COMP + 2 + 1
SEAM = (1, 2, GX - 3, GX - 2)

VMEM = pl.BlockSpec(memory_space=pltpu.VMEM)
SMEM = pl.BlockSpec(memory_space=pltpu.SMEM)
ANY = pl.BlockSpec(memory_space=pl.ANY)
HBM = pl.BlockSpec(memory_space=pltpu.HBM)


def f32(*shape):
    return jax.ShapeDtypeStruct(shape, jnp.float32)


def i32(*shape):
    return jax.ShapeDtypeStruct(shape, jnp.int32)


def lanes(shape=(8, 128)):
    return lax.broadcasted_iota(jnp.int32, shape, len(shape) - 1)


def pick(x, index):
    return jnp.take_along_axis(x, index, axis=1, mode="promise_in_bounds")


def rows(tile):
    return slice(8 * tile, 8 * tile + 8)


def call(kernel, outs, scratch=(), specs=None, out_specs=None, flops=0, moved=0, limit=16):
    return pl.pallas_call(
        kernel,
        out_shape=outs,
        in_specs=specs,
        out_specs=jax.tree.map(lambda _: VMEM, outs) if out_specs is None else out_specs,
        scratch_shapes=list(scratch),
        cost_estimate=pl.CostEstimate(flops=flops, bytes_accessed=moved, transcendentals=0),
        compiler_params=pltpu.CompilerParams(vmem_limit_bytes=int(limit * 2**20)),
    )


def edges_kernel(gas, kappa, send_q, send_p, held, arrived):
    copies = [pltpu.make_async_copy(gas.at[q], held.at[q], arrived.at[q]) for q in range(COMP)]
    copies.append(pltpu.make_async_copy(kappa, held.at[COMP], arrived.at[COMP]))
    for copy in copies:
        copy.start()
    lane = lanes()
    within = lane & 63
    depth, cell = within >> 4, within & 15
    high = jnp.maximum(6 * cell + 2 - depth, 0)
    low = 6 * cell + 3 + depth
    odd = lax.rem(lax.axis_index("blk"), 2) == 1
    index_q, index_p = jnp.where(odd, high, low), jnp.where(odd, low, high)
    for pair in range((COMP + 1) // 2):
        packed = {}
        for q in (2 * pair, 2 * pair + 1):
            copies[q].wait()
            for tile in range(TILES):
                total = jnp.zeros((8, 128), jnp.float32)
                for x in range(GX):
                    here = (lane >= 6 * x) & (lane < 6 * x + 6)
                    total = jnp.where(here, pltpu.roll(held[q, x, rows(tile), :], 6 * x + 3, 1), total)
                packed[q, tile] = total
        for tile in range(TILES):
            first, second = packed[2 * pair, tile], packed[2 * pair + 1, tile]
            for out, index in ((send_q, index_q), (send_p, index_p)):
                out[pair, rows(tile), :] = jnp.where(lane < 64, pick(first, index), pick(second, index))


def section_slabs(gas, kappa, corner, at, kappa_at):
    top = slice(GR - 8, GR)
    slabs = [gas[c, at + layer, top, :] for c in range(COMP) for layer in range(3)]
    return slabs + [kappa[kappa_at + layer, top, :] for layer in range(2)] + [corner]


def halves(slabs, upper):
    high = lax.broadcasted_iota(jnp.int32, (8, 128), 0) >= 4
    return [
        jnp.where(high == upper, a, pltpu.roll(b, 4, 0)) for a, b in zip(slabs[::2], slabs[1::2])
    ]


def strips_kernel(gas, kappa, send_q, send_p, recv_q, recv_p, _, strips, send_a, send_wall, corner):
    lane = lanes()
    low_side = (lane & 1) == 1
    cell = jnp.clip((lane >> 1) - 3, 0, GX - 1)
    even = lax.rem(lax.axis_index("sect"), 2) == 0
    odd_tile = lax.rem(lax.axis_index("blk"), 2) == 1
    for tile in range(TILES):
        held = {}
        slabs = [[ref[s, rows(tile), :] for s in range(3)] for ref in (send_q, send_p, recv_q, recv_p)]
        own_q, own_p, got_q, got_p = slabs
        to_left = [jnp.where(odd_tile, p, q) for q, p in zip(own_q, own_p)]
        to_right = [jnp.where(odd_tile, q, p) for q, p in zip(own_q, own_p)]
        from_left = [jnp.where(odd_tile, p, q) for q, p in zip(got_q, got_p)]
        from_right = [jnp.where(odd_tile, q, p) for q, p in zip(got_q, got_p)]
        for q, k in STRIPS:
            depth = k - 1 if k > 0 else -k
            index = cell + ((q % 2) * 64 + depth * 16)
            low, high = (from_left, from_right) if k > 0 else (to_left, to_right)
            value = jnp.where(low_side, pick(low[q // 2], index), pick(high[q // 2], index))
            strips[STRIP_AT[q, k], rows(tile), :] = value
            held[q, k] = value
        top = jnp.zeros((8, 128), jnp.float32)
        bottom = top
        for i, key in enumerate(CORNERS):
            here = (lane >> 2) == i
            top = jnp.where(here, pltpu.roll(held[key], (4 * i - 34) % 128, 1), top)
            bottom = jnp.where(here, pltpu.roll(held[key], (4 * i - 6) % 128, 1), bottom)
        for_a = jnp.where(even, top, bottom)
        for_b = jnp.where(even, bottom, top)
        send_a[LAYERS - 1, rows(tile), :] = for_a
        corner[rows(tile), :] = for_b
    at_a, at_b = jnp.where(even, GX - 3, 0), jnp.where(even, 0, GX - 3)
    kappa_a, kappa_b = jnp.where(even, GX - 2, 0), jnp.where(even, 0, GX - 2)
    for c in range(COMP):
        for layer in range(3):
            send_a[3 * c + layer] = gas[c, at_a + layer]
    for layer in range(2):
        send_a[3 * COMP + layer] = kappa[kappa_a + layer]


    for n, tile in enumerate(halves(section_slabs(gas, kappa, for_b, at_b, kappa_b), True)):
        send_wall[n] = tile


def rest_kernel(gas, kappa, corner, _, send_rest):
    even = lax.rem(lax.axis_index("sect"), 2) == 0
    from_b, from_kappa = jnp.where(even, 0, GX - 3), jnp.where(even, 0, GX - 2)
    for t in range(TILES - 1):
        for c in range(COMP):
            for layer in range(3):
                send_rest[3 * (3 * c + layer) + t] = gas[c, from_b + layer, rows(t), :]
        for layer in range(2):
            send_rest[3 * (3 * COMP + layer) + t] = kappa[from_kappa + layer, rows(t), :]
        send_rest[3 * (LAYERS - 1) + t] = corner[rows(t), :]
    slabs = section_slabs(gas, kappa, corner[rows(TILES - 1), :], from_b, from_kappa)
    for n, tile in enumerate(halves(slabs, False)):
        send_rest[3 * LAYERS + n] = tile


def coupling(reaction):
    return [[0.3 * reaction[c, d] + (1.0 if c == d else 0.0) for d in range(COMP)] for c in range(COMP)]


def updated(c, values, neighbours, kappa, mix):
    total = mix[c][0] * values[0]
    for d in range(1, COMP):
        total = total + mix[c][d] * values[d]
    rate = kappa if DIFFUSE[c] == 1.0 else DIFFUSE[c] * kappa
    return total + rate * (neighbours - 6.0 * values[c])


def radial_sum(tiles, wall_only):
    sub = lax.broadcasted_iota(jnp.int32, (8, 128), 0)
    down = [pltpu.roll(t, 1, 0) for t in tiles]
    up = [pltpu.roll(t, 7, 0) for t in tiles]
    last = len(tiles) - 1
    sums = []
    for i, t in enumerate(tiles):
        if wall_only:
            below = down[i]
        else:
            below = jnp.where(sub == 0, down[i - 1] if i > 0 else t, down[i])
        above = jnp.where(sub == 7, up[i + 1] if i < last else t, up[i])
        sums.append(below + above)
    return sums


def radial_sum_of(src, c, at, values):
    sub = lax.broadcasted_iota(jnp.int32, (8, 128), 0)
    sums = []
    for t in range(TILES):
        first, last = t == 0, t == TILES - 1
        below = jnp.where(sub == 0, values[t], pltpu.roll(values[t], 1, 0)) if first else src[c, at, 8 * t - 1 : 8 * t + 7, :]
        above = jnp.where(sub == 7, values[t], pltpu.roll(values[t], 7, 0)) if last else src[c, at, 8 * t + 1 : 8 * t + 9, :]
        sums.append(below + above)
    return sums


def strip_levels(strips, low_corner, high_corner, mix, edge, tiles):
    lane = lanes()
    wall_only = len(tiles) == 1
    from_low = (lane >= 2) & (lane < 6)
    from_high = (lane >= 38) & (lane < 42)
    held = {}
    for key in STRIPS:
        held[key] = [strips[STRIP_AT[key], rows(t), :] for t in tiles]
    for i, key in enumerate(CORNERS if low_corner else ()):
        for n in range(len(tiles)):
            value = jnp.where(from_low, pltpu.roll(low_corner[n], (2 - 4 * i) % 128, 1), held[key][n])
            held[key][n] = jnp.where(from_high, pltpu.roll(high_corner[n], (38 - 4 * i) % 128, 1), value)
    for step in range(ITERS):
        for c in range(COMP):
            for n in range(len(tiles)):
                edge[step, c, rows(n), :] = held[c, 1][n]
        if step == ITERS - 1:
            break
        later = {}
        for k in (2, 1, 0) if step == 0 else (1,):
            for c in range(COMP):
                radial = radial_sum(held[c, k], wall_only)
                later[c, k] = []
                for n in range(len(tiles)):
                    value = held[c, k][n]
                    around = held[c, k + 1][n] + held[c, k - 1][n]
                    around = around + pltpu.roll(value, 2, 1) + pltpu.roll(value, 126, 1) + radial[n]
                    later[c, k].append(updated(c, [held[d, k][n] for d in range(COMP)], around, held[COMP, k][n], mix))
        for key in [key for key in held if key[0] == COMP]:
            later[key] = held[key]
        held = later


def plane(src, kappa, edge, step, at, x, mix, count, comps):
    lane = lanes()
    first, last = lane == 0, lane == 127
    shift = 121 - 2 * x
    values = [[src[c, at, rows(t), :] for t in range(count)] for c in range(COMP)]
    kap = [kappa[at, rows(t), :] for t in range(count)]
    out = {}
    for c in comps:
        radial = radial_sum(values[c], True) if count == 1 else radial_sum_of(src, c, at, values[c])
        for t in range(count):
            value = values[c][t]
            beyond = pltpu.roll(edge[step, c, rows(t), :], shift, 1)
            around = src[c, at - 1, rows(t), :] + src[c, at + 1, rows(t), :] + radial[t]
            around = around + jnp.where(first, beyond, pltpu.roll(value, 1, 1))
            around = around + jnp.where(last, beyond, pltpu.roll(value, 127, 1))
            out[c, t] = updated(c, [values[d][t] for d in range(COMP)], around, kap[t], mix)
    return out


def wall_kernel(
    gas, kappa, strips, recv_wall, recv_a, first, second, middle, reaction, _, wall, now, later, kap, edge
):
    even = lax.rem(lax.axis_index("sect"), 2) == 0
    mix = coupling(reaction)
    top = slice(GR - 8, GR)

    def upper(i):
        return recv_wall[i // 2] if i % 2 == 0 else pltpu.roll(recv_wall[i // 2], 4, 0)

    at_a, at_b = jnp.where(even, GX + 3, 0), jnp.where(even, 0, GX + 3)
    kappa_a, kappa_b = jnp.where(even, GX + 3, 1), jnp.where(even, 1, GX + 3)
    for c in range(COMP):
        for x in (0, 1, GX - 2, GX - 1):
            now[c, x + 3] = gas[c, x, top, :]
        for layer in range(3):
            now[c, at_a + layer] = recv_a[3 * c + layer, top, :]
            now[c, at_b + layer] = upper(3 * c + layer)
        for i, x in enumerate(SEAM):
            later[c, x + 3] = first[c, i, top, :]
    for x in (0, 1, 2, GX - 3, GX - 2, GX - 1):
        kap[x + 3] = kappa[x, top, :]
    for layer in range(2):
        kap[kappa_a + layer] = recv_a[3 * COMP + layer, top, :]
        kap[kappa_b + layer] = upper(3 * COMP + layer)
    corner_a, corner_b = recv_a[LAYERS - 1, top, :], upper(LAYERS - 1)
    low, high = jnp.where(even, corner_b, corner_a), jnp.where(even, corner_a, corner_b)
    strip_levels(strips, [low], [high], mix, edge, [TILES - 1])
    wall[3 : GX - 3, :] = middle[0, :, GR - 1, :]
    for step, (src, dst) in enumerate(((now, later), (later, now), (now, None))):
        last = step == ITERS - 1
        if last:
            for c in range(COMP):
                for i, x in enumerate(SEAM):
                    now[c, (x + 1 if i < 2 else x - 1) + 3] = second[c, i, top, :]
        for i in range(3):
            for at in (step + 1 + i, GX + 2 - step + i):
                out = plane(src, kap, edge, step, at, at - 3, mix, 1, (0,) if last else range(COMP))
                if last:
                    wall[at - 3 : at - 2, :] = out[0, 0][7:8, :]
                    continue
                for c in range(COMP):
                    dst[c, at] = out[c, 0]


def inner_kernel(gas, kappa, strips, reaction, first, second, middle, one, two, edge):
    mix = coupling(reaction)
    strip_levels(strips, None, None, mix, edge, list(range(TILES)))
    for step, (src, dst) in enumerate(((gas, one), (one, two), (two, middle))):

        def body(x, carry, step=step, src=src, dst=dst):
            out = plane(src, kappa, edge, step, x, x, mix, TILES, range(COMP))
            into = x - 3 if step == ITERS - 1 else x
            for (c, t), value in out.items():
                dst[c, into, rows(t), :] = value
            return carry

        lax.fori_loop(step + 1, GX - 1 - step, body, 0, unroll=2)
    for c in range(COMP):
        for i, x in enumerate(SEAM):
            first[c, i] = one[c, x]
            second[c, i] = two[c, x + 1 if i < 2 else x - 1]


def outer_kernel(
    _, gas, kappa, strips, first, second, middle, recv_wall, recv_a, recv_rest, reaction, result, token, now, later, kap, edge
):
    token[...] = jnp.zeros((8, 128), jnp.float32)
    even = lax.rem(lax.axis_index("sect"), 2) == 0
    mix = coupling(reaction)
    late = lax.broadcasted_iota(jnp.int32, (8, 128), 0) >= 4

    def part(i, t):
        if t < TILES - 1:
            return recv_rest[3 * i + t]
        wall, other = recv_wall[i // 2], recv_rest[3 * LAYERS + i // 2]
        return jnp.where(late, wall, other) if i % 2 == 0 else pltpu.roll(jnp.where(late, other, wall), 4, 0)

    at_a, at_b = jnp.where(even, GX + 3, 0), jnp.where(even, 0, GX + 3)
    kappa_a, kappa_b = jnp.where(even, GX + 3, 1), jnp.where(even, 1, GX + 3)
    for c in range(COMP):
        for x in (0, 1, GX - 2, GX - 1):
            now[c, x + 3] = gas[c, x]
        for layer in range(3):
            now[c, at_a + layer] = recv_a[3 * c + layer]
            for t in range(TILES):
                now[c, at_b + layer, rows(t), :] = part(3 * c + layer, t)
        for i, x in enumerate(SEAM):
            later[c, x + 3] = first[c, i]
    for x in (0, 1, 2, GX - 3, GX - 2, GX - 1):
        kap[x + 3] = kappa[x]
    for layer in range(2):
        kap[kappa_a + layer] = recv_a[3 * COMP + layer]
        for t in range(TILES):
            kap[kappa_b + layer, rows(t), :] = part(3 * COMP + layer, t)
    low, high = [], []
    for t in range(TILES):
        corner_a = recv_a[LAYERS - 1, rows(t), :]
        corner_b = part(LAYERS - 1, t)
        low.append(jnp.where(even, corner_b, corner_a))
        high.append(jnp.where(even, corner_a, corner_b))
    strip_levels(strips, low, high, mix, edge, list(range(TILES)))
    for c in range(COMP):
        result[c, 3 : GX - 3] = middle[c]
    for step, (src, dst) in enumerate(((now, later), (later, now), (now, None))):
        if step == ITERS - 1:
            for c in range(COMP):
                for i, x in enumerate(SEAM):
                    now[c, (x + 1 if i < 2 else x - 1) + 3] = second[c, i]
        for i in range(3):
            for at in (step + 1 + i, GX + 2 - step + i):
                out = plane(src, kap, edge, step, at, at - 3, mix, TILES, range(COMP))
                for (c, t), value in out.items():
                    if step == ITERS - 1:
                        result[c, at - 3, rows(t), :] = value
                    else:
                        dst[c, at, rows(t), :] = value


def pack_kernel(hop, cell, particles, mixing, heating, _, packed, cells, spread, ordered, source, begin, end):
    lane = lanes()
    square = (128, 128)
    down, across = lax.broadcasted_iota(jnp.int32, square, 0), lanes(square)
    moves = hop[...]
    named = [moves == j for j in range(MOVES)]
    table = jnp.concatenate(
        [jnp.where(m, 1.0, 0.0) for m in named] + [jnp.zeros((128 - MOVES * CHUNKS, 128), jnp.float32)], axis=0
    )
    running = jnp.dot(table, jnp.where(down <= across, 1.0, 0.0), preferred_element_type=jnp.float32)
    count = jnp.dot(table, jnp.ones(square, jnp.float32), preferred_element_type=jnp.float32)
    before = jnp.where(((down >> 4) == (across >> 4)) & (across < down), 1.0, 0.0)
    base = jnp.dot(before, count, preferred_element_type=jnp.float32)
    offset = jnp.zeros((CHUNKS, 128), jnp.float32)
    place = jnp.zeros((CHUNKS, 128), jnp.float32)
    across16 = lanes((CHUNKS, 128))
    for j in range(MOVES):
        part = slice(CHUNKS * j, CHUNKS * (j + 1))
        place = jnp.where(named[j], offset + running[part] - 1.0, place)
        first = base[part].astype(jnp.int32)
        source[part, :] = (across16 + offset.astype(jnp.int32) - first) & 127
        begin[part, :] = across16 - first
        end[part, :] = across16 - first - count[part].astype(jnp.int32)
        offset = offset + count[part]
    own = lax.broadcasted_iota(jnp.int32, (VALS, VALS), 0) == lax.broadcasted_iota(jnp.int32, (VALS, VALS), 1)
    weights = 0.5 * mixing[...] + jnp.where(own, 1.0, 0.0)
    first_value = lax.broadcasted_iota(jnp.int32, (VALS, VALS), 1) == 0
    weights = weights - jnp.where(first_value, heating[...], 0.0)
    for v in range(VALS):
        spread[v] = jnp.broadcast_to(weights[:, v : v + 1], (VALS, 128))
    place = place.astype(jnp.int32)
    position = lane.astype(jnp.float32)
    for chunk in range(CHUNKS):
        part = slice(128 * chunk, 128 * (chunk + 1))
        total = spread[0] * particles[0:1, part]
        for v in range(1, VALS):
            total = total + spread[v] * particles[v : v + 1, part]
        hot = jnp.where(down == place[chunk : chunk + 1, :], 1.0, 0.0)
        order = lax.dot_general(position, hot, (((1,), (1,)), ((), ())), preferred_element_type=jnp.float32)
        order = order.astype(jnp.int32)
        ordered[chunk, 0:8, :] = pick(total[0:8], order)
        ordered[chunk, 8:16, :] = pick(total[8:16], order)
        ordered[chunk, 16:24, :] = pick(
            jnp.broadcast_to(cell[chunk : chunk + 1, :], (8, 128)).astype(jnp.float32), order
        )

    def block(j, carry):
        held = [[jnp.zeros((8, 128), jnp.float32)] * 2 + [jnp.full((8, 128), -1.0)] for _ in range(SPOTS)]
        for chunk in range(CHUNKS):
            row = pl.ds(CHUNKS * j + chunk, 1)
            index = jnp.broadcast_to(source[row, :], (8, 128))
            parts = [pick(ordered[chunk, rows(n), :], index) for n in range(3)]
            start = jnp.broadcast_to(begin[row, :], (8, 128))
            stop = jnp.broadcast_to(end[row, :], (8, 128))
            for spot in range(SPOTS):
                here = (start >= -128 * spot) & (stop < -128 * spot)
                held[spot] = [jnp.where(here, new, old) for new, old in zip(parts, held[spot])]
        for spot in range(SPOTS):
            part = slice(128 * spot, 128 * (spot + 1))
            packed[j, 0:8, part] = held[spot][0]
            packed[j, 8:16, part] = held[spot][1]
            cells[j, spot : spot + 1, :] = held[spot][2][0:1, :].astype(jnp.int32)
        return carry

    lax.fori_loop(0, MOVES, block, 0)


def moves_of_swaps():
    tile = lax.axis_index("blk")
    odd, late = lax.rem(tile, 2), lax.rem(tile, 4) >> 1
    return [REACH - 1 + 2 * odd, 2 * REACH * (1 - late), 2 * REACH * late, REACH + 1 - 2 * odd]


def heat_kernel(wall, earlier, packed, cells, heating, own, send_q, send_r, send_s, send_p, look):
    flux = 0.5 * (wall[...] + earlier[...])
    heat = jnp.broadcast_to(heating[...], (VALS, 128))
    for j in range(MOVES):
        where_to = cells[j]
        row, column = where_to >> 7, where_to & 127
        found = jnp.zeros((8, 128), jnp.float32)
        for x in range(GX):
            line = jnp.broadcast_to(flux[x : x + 1, :], (8, 128))
            found = jnp.where(row == x, pick(line, column), found)
        look[j] = found
    for out, j in zip((own, send_q, send_r, send_s, send_p), [REACH] + moves_of_swaps()):
        for spot in range(SPOTS):
            part = slice(128 * spot, 128 * (spot + 1))
            out[:, part] = packed[j, :, part] + heat * look[j, spot : spot + 1, :]


def join_kernel(own, recv_q, recv_r, recv_s, recv_p, _, out, done):
    copies = []
    for n, (piece, j) in enumerate(zip((own, recv_q, recv_r, recv_s, recv_p), [REACH] + moves_of_swaps())):
        place = pl.multiple_of((2 * REACH - j) * CAP, CAP)
        copies.append(pltpu.make_async_copy(piece, out.at[:, pl.ds(place, CAP)], done.at[n]))
    for copy in copies:
        copy.start()
    for copy in copies:
        copy.wait()


def swap(x, axis, pairs):
    return lax.ppermute(x, axis, pairs + [(j, i) for i, j in pairs])


def local(gas, kappa, reaction, particles, mixing, heating, wall_cell, tile_hop):
    sections, tiles = lax.axis_size("sect"), lax.axis_size("blk")
    pairs_a = [(i, i + 1) for i in range(0, sections, 2)]
    pairs_b = [(i, i + 1) for i in range(1, sections - 1, 2)]
    pairs_q = [(i, (i + 1) % tiles) for i in range(1, tiles, 2)]
    pairs_p = [(i, i + 1) for i in range(0, tiles, 2)]
    pairs_s = [(i, (i + 2) % tiles) for i in range(tiles) if i % 4 >= 2]
    pairs_r = [(i, i + 2) for i in range(tiles) if i % 4 < 2]

    send_q, send_p = call(
        edges_kernel,
        (f32(3, GR, GA), f32(3, GR, GA)),
        scratch=[pltpu.VMEM((COMP + 1, GX, GR, GA), jnp.float32), pltpu.SemaphoreType.DMA((COMP + 1,))],
        specs=[HBM] * 2,
        moved=2 << 20,
        limit=53.75,
    )(gas, kappa)
    recv_q = swap(send_q, "blk", pairs_q)
    recv_p = swap(send_p, "blk", pairs_p)
    heating_column = heating.reshape(VALS, 1)
    packed, cells = call(
        pack_kernel,
        (f32(MOVES, VALS, CAP), i32(MOVES, SPOTS, 128)),
        scratch=[
            pltpu.VMEM((VALS, VALS, 128), jnp.float32),
            pltpu.VMEM((CHUNKS, 24, 128), jnp.float32),
            pltpu.VMEM((MOVES * CHUNKS, 128), jnp.int32),
            pltpu.VMEM((MOVES * CHUNKS, 128), jnp.int32),
            pltpu.VMEM((MOVES * CHUNKS, 128), jnp.int32),
        ],
        specs=[VMEM] * 5 + [ANY],
        moved=4 << 20,
    )(tile_hop.reshape(CHUNKS, 128), wall_cell.reshape(CHUNKS, 128), particles, mixing, heating_column, send_p)

    strips, send_a, send_wall, corner = call(
        strips_kernel,
        (f32(len(STRIPS), GR, GA), f32(LAYERS, GR, GA), f32(LAYERS // 2, 8, GA), f32(GR, GA)),
        specs=[VMEM] * 6 + [ANY],
        moved=2 << 20,
    )(gas, kappa, send_q, send_p, recv_q, recv_p, cells)
    recv_wall = swap(send_wall, "sect", pairs_b)
    recv_a = swap(send_a, "sect", pairs_a)

    whole = f32(COMP, GX, GR, GA)
    first, second, middle = call(
        inner_kernel,
        (f32(COMP, len(SEAM), GR, GA), f32(COMP, len(SEAM), GR, GA), f32(COMP, GX - 6, GR, GA)),
        scratch=[
            pltpu.VMEM((COMP, GX, GR, GA), jnp.float32),
            pltpu.VMEM((COMP, GX, GR, GA), jnp.float32),
            pltpu.VMEM((ITERS, COMP, GR, GA), jnp.float32),
        ],
        specs=[VMEM] * 3 + [SMEM],
        moved=12 << 20,
    )(gas, kappa, strips, reaction)

    send_rest = call(rest_kernel, f32(3 * LAYERS + LAYERS // 2, 8, GA), specs=[VMEM] * 3 + [ANY], moved=1 << 18)(
        gas, kappa, corner, middle
    )
    recv_rest = swap(send_rest, "sect", pairs_b)

    wall = call(
        wall_kernel,
        f32(GX, GA),
        scratch=[
            pltpu.VMEM((COMP, EXT, 8, GA), jnp.float32),
            pltpu.VMEM((COMP, EXT, 8, GA), jnp.float32),
            pltpu.VMEM((EXT, 8, GA), jnp.float32),
            pltpu.VMEM((ITERS, COMP, 8, GA), jnp.float32),
        ],
        specs=[VMEM] * 8 + [SMEM, ANY],
        moved=4 << 20,
    )(gas, kappa, strips, recv_wall, recv_a, first, second, middle, reaction, send_rest)
    earlier = lax.ppermute(wall, "sect", [(i, i + 1) for i in range(sections - 1)])

    own, *sends = call(
        heat_kernel,
        (f32(VALS, CAP),) * MOVES,
        scratch=[pltpu.VMEM((MOVES, SPOTS, 128), jnp.float32)],
        specs=[VMEM] * 5,
        moved=2 << 20,
        flops=1 << 34,
    )(wall, earlier, packed, cells, heating_column)
    pieces = [swap(x, "blk", pairs) for x, pairs in zip(sends, (pairs_q, pairs_r, pairs_s, pairs_p))]

    field, token = call(
        outer_kernel,
        (whole, f32(8, 128)),
        scratch=[
            pltpu.VMEM((COMP, EXT, GR, GA), jnp.float32),
            pltpu.VMEM((COMP, EXT, GR, GA), jnp.float32),
            pltpu.VMEM((EXT, GR, GA), jnp.float32),
            pltpu.VMEM((ITERS, COMP, GR, GA), jnp.float32),
        ],
        specs=[ANY] + [VMEM] * 9 + [SMEM],
        moved=8 << 20,
    )(pieces[0], gas, kappa, strips, first, second, middle, recv_wall, recv_a, recv_rest, reaction)
    arrived = call(
        join_kernel,
        f32(VALS, MOVES * CAP),
        scratch=[pltpu.SemaphoreType.DMA((MOVES,))],
        specs=[VMEM] * MOVES + [ANY],
        out_specs=HBM,
        moved=1 << 20,
    )(own, *pieces, token)
    return field, arrived


def solution(mesh):
    in_specs = (
        P(None, "sect", None, "blk"),
        P("sect", None, "blk"),
        P(),
        P(None, ("sect", "blk")),
        P(),
        P(),
        P(("sect", "blk")),
        P(("sect", "blk"), None),
    )
    out_specs = (P(None, "sect", None, "blk"), P(None, ("sect", "blk")))
    return jax.shard_map(local, mesh=mesh, in_specs=in_specs, out_specs=out_specs, check_vma=False)
```
